32 devices in a mesh: groups: 2 (over y), section: 4 (over z), head: 4 (over x, core).
Axes of the slice: x: 2, y: 2, z: 4, core: 2. Of those that a mesh axis runs over, the one named last changes fastest.
Arguments:
- rising: bfloat16 [8, 128, 1024], P(('groups', 'section')), parts along dimension 0, may hold values from -24 to 24
- falling: bfloat16 [8, 128, 1024], P(('groups', 'section')), parts along dimension 0, may hold values from -6 to 6
- stash: bfloat16 [8, 3, 128, 1024], P(('groups', 'section')), parts along dimension 0, may hold values from -24 to 24
- queue: bfloat16 [12, 128, 1024], P('groups'), parts along dimension 0, may hold values from -24 to 24
- order: int32 [12], P('groups'), parts along dimension 0, may hold values from 0 to 5, each once
- buckets: int32 [128, 128], replicated, may hold values from 0 to 31, as said below
- bias_table: float32 [4, 32, 64], P('section', None, 'head'), may hold values from -3 to 260
- gain: float32 [4, 1024], P('section'), may hold values from 0.1 to 1.9
- w_qkv: bfloat16 [4, 1024, 64, 3, 128], P('section', None, 'head'), may hold values from -0.1875 to 0.1875
- w_out: bfloat16 [4, 64, 128, 1024], P('section', 'head'), may hold values from -0.0625 to 0.0625
Outputs:
- rising_out: bfloat16 [8, 128, 1024], P(('groups', 'section')), parts along dimension 0
- falling_out: bfloat16 [8, 128, 1024], P(('groups', 'section')), parts along dimension 0
- table_grad: float32 [8, 32, 64], P(('groups', 'section'), None, 'head'), parts along dimension 0
The draws below stay inside these ranges and needn't reach their ends.
There are 2 independent parts, one for each index of `groups`. The reference program is written for one: setup_inputs(seed, part) draws one part's arguments, and reference() takes and returns one part's arrays. A program takes and returns all parts, laid end to end along the dimension named above; an argument that names none is the same for every part. Nothing has to cross between parts.
Inputs may be any that keep to these rules, and one draw needn't show every extreme that they name: `order`: a permutation of 0 to 5. T5's bidirectional bucket of the key's position minus the query's, 32 buckets, distances of 128 or more in the outermost; positions rise by 1 to 4 from token to token, with one jump of 128 or more.
All inputs are finite; a program needn't handle non-finite values.
Results may differ from the reference program's by a relative error of at most 0.019.
Values may be sent and summed in bfloat16 or wider, within the bound.
No kernel may reach another device: no remote copies, remote signals or barrier semaphores. Data moves between devices by JAX's collectives and lax.ppermute only.
A program may use at most 128 MiB of HBM per device.

```python
import math
import jax
import jax.numpy as jnp
from jax import lax

D = 1024
HEADS = 64
HD = 128
NB = 32
MAX_DIST = 128
TOK = 128
TICKS = 3
QUEUE = 6
SECTIONS = 4


bucket_edges = (12, 16, 23, 32, 46, 64, 91)


def scaled_rows(key, shape):
    keys = jax.random.split(key, 3)
    base = jax.random.normal(keys[0], shape, jnp.float32)
    row_scale = jnp.exp(jax.random.uniform(keys[1], shape[:-1] + (1,), jnp.float32, math.log(0.3), math.log(3.0)))
    col_scale = jnp.exp(jax.random.uniform(keys[2], (shape[-1],), jnp.float32, math.log(0.3), math.log(3.0)))
    return jnp.clip(base * row_scale * col_scale, -24.0, 24.0).astype(jnp.bfloat16)


def draw_rising(key, part):
    return scaled_rows(jax.random.fold_in(key, 101), (SECTIONS, TOK, D))


def draw_stash(key, part):
    return scaled_rows(jax.random.fold_in(key, 202), (SECTIONS, TICKS, TOK, D))


def draw_queue(key, part):
    return scaled_rows(jax.random.fold_in(key, 303), (QUEUE, TOK, D))


def draw_buckets(key, part):
    keys = jax.random.split(jax.random.fold_in(key, 404), 2)
    steps_between = jax.random.randint(keys[0], (TOK,), 1, 5, dtype=jnp.int32)
    jump_at = jax.random.randint(keys[1], (), 1, TOK, dtype=jnp.int32)
    token_ids = jnp.arange(TOK, dtype=jnp.int32)
    steps_between = jnp.where(token_ids == jump_at, steps_between + MAX_DIST, steps_between)
    positions = jnp.cumsum(steps_between).astype(jnp.int32)
    offset = positions[:, None] - positions[None, :]
    distance = jnp.abs(offset)
    half = NB // 2
    exact = half // 2
    far = jnp.full(distance.shape, exact, jnp.int32)
    for edge in bucket_edges:
        far = far + (distance >= edge).astype(jnp.int32)
    within = jnp.where(distance < exact, distance, jnp.minimum(far, half - 1))
    return (jnp.where(offset < 0, half, 0) + within).astype(jnp.int32)


def draw_bias_table(key, part):
    keys = jax.random.split(jax.random.fold_in(key, 505), 1)
    table = jnp.clip(jax.random.normal(keys[0], (SECTIONS, NB, HEADS), jnp.float32), -3.0, 3.0)
    return table.astype(jnp.float32)


def block_scale(rng, shape, cuts, low, high):
    level, own = 1.0, jax.random.fold_in(rng, 6)
    for position, parts in cuts:
        draws = jnp.exp(jax.random.uniform(jax.random.fold_in(own, position), (parts,), jnp.float32, low / len(cuts), high / len(cuts)))
        level = level * jnp.repeat(draws, shape[position] // parts).reshape([-1 if axis == position else 1 for axis in range(len(shape))])
    return level


def centred(stream_key, dims, width, bound, cuts=(), kind=jnp.bfloat16):
    factor_of = block_scale(stream_key, dims, cuts, -0.22, 0.18) if cuts else 1.0
    entries = jax.random.normal(stream_key, dims, jnp.float32) * width * factor_of
    return jnp.minimum(jnp.maximum(entries, -bound), bound).astype(kind)


def setup_inputs(seed: int = 0, part: int = 0) -> dict:
    key_list = jax.random.split(jax.random.key(seed), 11)
    part_keys = jax.random.split(jax.random.fold_in(key_list[10], part), 11)
    rising = draw_rising(jax.random.fold_in(jax.random.fold_in(key_list[10], part), 71), part)
    falling = centred(part_keys[1], (SECTIONS, TOK, D), 1.0, 6.0, ((0, 4),))
    stash = draw_stash(jax.random.fold_in(jax.random.fold_in(key_list[10], part), 71), part)
    queue = draw_queue(jax.random.fold_in(jax.random.fold_in(key_list[10], part), 71), part)
    order = jax.random.permutation(part_keys[4], QUEUE).astype(jnp.int32)
    buckets = draw_buckets(jax.random.fold_in(key_list[10], 71), part)
    bias_table = draw_bias_table(jax.random.fold_in(key_list[10], 71), part)
    gain = jnp.clip(1.0 + 0.18 * jax.random.normal(key_list[7], (SECTIONS, D), jnp.float32), 0.1, 1.9)
    w_qkv = centred(key_list[8], (SECTIONS, D, HEADS, 3, HD), D ** -0.5, 0.1875, ((0, 4), (2, 4)))
    w_out = centred(key_list[9], (SECTIONS, HEADS, HD, D), (HEADS * HD) ** -0.5, 0.0625, ((0, 4), (1, 4)))
    return dict(rising=rising, falling=falling, stash=stash, queue=queue, order=order, buckets=buckets, bias_table=bias_table, gain=gain, w_qkv=w_qkv, w_out=w_out)


EPSILON = 1e-06
CONTRACT_LAST = (((1,), (1,)), ((), ()))

def normalize(inputs, gain_row):
    as_float = inputs.astype(jnp.float32)
    inverse = lax.rsqrt(lax.optimization_barrier(jnp.mean(as_float * as_float, axis=-1, keepdims=True)) + EPSILON)
    return ((as_float * inverse * gain_row).astype(jnp.bfloat16), inverse)

def forward_parts(inputs, gain_row, w_in, biases):
    normed, inverse = normalize(inputs, gain_row)
    qkv = jnp.dot(normed, w_in, preferred_element_type=jnp.float32).astype(jnp.bfloat16)
    qkv = qkv.reshape(inputs.shape[0], HEADS, 3, HD)
    queries = qkv[:, :, 0]
    keys_part = qkv[:, :, 1]
    values_part = qkv[:, :, 2]
    scores = jnp.einsum('ihd,jhd->hij', queries.astype(jnp.float32), keys_part.astype(jnp.float32)) * HD ** (-0.5) + biases
    attention_probs = jax.nn.softmax(scores, axis=-1)
    return (inverse, queries, keys_part, values_part, attention_probs, attention_probs.astype(jnp.bfloat16))

def section_forward(inputs, gain_row, w_in, w_back, biases):
    inverse, queries, keys_part, values_part, attention_probs, probs_half = forward_parts(inputs, gain_row, w_in, biases)
    attended = jnp.einsum('hij,jhd->ihd', probs_half.astype(jnp.float32), values_part.astype(jnp.float32))
    attended = attended.astype(jnp.bfloat16).reshape(inputs.shape[0], HEADS * HD)
    projected = jnp.dot(attended, w_back, preferred_element_type=jnp.float32)
    return (inputs.astype(jnp.float32) + projected).astype(jnp.bfloat16)

def section_backward(inputs, cotangent, gain_row, w_in, w_back, biases):
    inverse, queries, keys_part, values_part, attention_probs, probs_half = forward_parts(inputs, gain_row, w_in, biases)
    tokens = inputs.shape[0]
    grad_attn = lax.dot_general(cotangent, w_back, CONTRACT_LAST, preferred_element_type=jnp.float32)
    grad_attn = grad_attn.astype(jnp.bfloat16).reshape(tokens, HEADS, HD).astype(jnp.float32)
    grad_probs = jnp.einsum('ihd,jhd->hij', grad_attn, values_part.astype(jnp.float32))
    grad_value = jnp.einsum('hij,ihd->jhd', probs_half.astype(jnp.float32), grad_attn).astype(jnp.bfloat16)
    grad_scores = attention_probs * (grad_probs - lax.optimization_barrier(jnp.sum(attention_probs * grad_probs, axis=-1, keepdims=True)))
    scores_half = grad_scores.astype(jnp.bfloat16).astype(jnp.float32)
    grad_query = (jnp.einsum('hij,jhd->ihd', scores_half, keys_part.astype(jnp.float32)) * HD ** (-0.5)).astype(jnp.bfloat16)
    grad_key = (jnp.einsum('hij,ihd->jhd', scores_half, queries.astype(jnp.float32)) * HD ** (-0.5)).astype(jnp.bfloat16)
    stacked = jnp.stack([grad_query, grad_key, grad_value], axis=2).reshape(tokens, HEADS * 3 * HD)
    grad_normed = lax.dot_general(stacked, w_in, CONTRACT_LAST, preferred_element_type=jnp.float32)
    as_float = inputs.astype(jnp.float32)
    weighted = gain_row * grad_normed
    cubed = inverse * inverse * inverse
    result = cotangent.astype(jnp.float32) + inverse * weighted - as_float * cubed * lax.optimization_barrier(jnp.mean(as_float * weighted, axis=-1, keepdims=True))
    return (result.astype(jnp.bfloat16), grad_scores)

def reference(rising, falling, stash, queue, order, buckets, bias_table, gain, w_qkv, w_out):
    hbias = jnp.transpose(bias_table[:, buckets, :], (0, 3, 1, 2))
    w_in_all = w_qkv.reshape(SECTIONS, D, HEADS * 3 * HD)
    w_back_all = w_out.reshape(SECTIONS, HEADS * HD, D)
    upward = rising
    downward = falling
    accum = jnp.zeros((SECTIONS, HEADS, TOK, TOK), jnp.float32)

    def one_section(packed):
        arriving, kept_rows, cotangent, gain_row, w_in, w_back, biases = packed
        lifted = section_forward(arriving, gain_row, w_in, w_back, biases)
        lowered, grad_scores = section_backward(kept_rows, cotangent, gain_row, w_in, w_back, biases)
        return (lifted, lowered, grad_scores)
    out_up = upward
    out_down = downward
    for tick_index in range(TICKS):
        kept = stash[:, tick_index]
        out_up, out_down, grad_scores = lax.map(one_section, (upward, kept, downward, gain, w_in_all, w_back_all, hbias))
        accum = accum + grad_scores
        if tick_index + 1 < TICKS:
            arrival = queue[order[tick_index]]
            upward = jnp.concatenate([arrival[None], out_up[:-1]], axis=0)
            downward = jnp.concatenate([out_down[1:], out_up[-1:]], axis=0)

    def fold_table(section_accum):
        flat = section_accum.reshape(HEADS, TOK * TOK).T
        return jax.ops.segment_sum(flat, buckets.reshape(-1), num_segments=NB)
    table_grad = lax.map(fold_table, accum)
    return (out_up, out_down, table_grad)
```

```python
import functools

import jax
import jax.numpy as jnp
from jax import lax
from jax.experimental import pallas as pl
from jax.experimental.pallas import tpu as pltpu
from jax.sharding import PartitionSpec as P

TICKS = 3
EPSILON = 1e-06
LANES = 128
ROWS16 = 16
LAST = (((1,), (1,)), ((), ()))
FIRST = (((0,), (0,)), ((), ()))
F32 = jnp.float32
BF16 = jnp.bfloat16
WHOLE = pl.BlockSpec(memory_space=pltpu.VMEM)
SCALARS = pl.BlockSpec(memory_space=pltpu.SMEM)
MIB = 1 << 20


def dot(a, b, dims=None):
    if dims is None:
        return jnp.dot(a, b, preferred_element_type=F32)
    return lax.dot_general(a, b, dims, preferred_element_type=F32)


def rms_normed(rows, gain_row):
    x = rows.astype(F32)
    inverse = lax.rsqrt(jnp.mean(x * x, axis=-1, keepdims=True) + EPSILON)
    return (x * inverse * gain_row).astype(BF16)


def relayout_kernel(heads, x_ref, gain_ref, w_ref, w_out_ref, qkv_ref, normed):
    @pl.when(pl.program_id(0) == 0)
    def _():
        normed[...] = rms_normed(x_ref[0], gain_ref[...])

    depth = w_ref.shape[0]
    size = ROWS16 * ROWS16
    row = lax.broadcasted_iota(jnp.int32, (size, size), 0)
    col = lax.broadcasted_iota(jnp.int32, (size, size), 1)
    wanted = (row & (ROWS16 - 1)) * ROWS16 + (row >> 4)
    permute = (col == wanted).astype(F32).astype(BF16)

    def step(i, carry):
        d0 = pl.multiple_of(i * 2 * ROWS16, 2 * ROWS16)
        first = w_ref[pl.ds(d0, ROWS16)].reshape(size, LANES)
        second = w_ref[pl.ds(d0 + ROWS16, ROWS16)].reshape(size, LANES)
        moved = dot(permute, jnp.concatenate([first, second], axis=1)).astype(BF16)
        for h in range(ROWS16):
            piece = moved[h * ROWS16 : (h + 1) * ROWS16]
            lanes = slice(h * LANES, (h + 1) * LANES)
            w_out_ref[0, pl.ds(d0, ROWS16), lanes] = piece[:, :LANES]
            w_out_ref[0, pl.ds(d0 + ROWS16, ROWS16), lanes] = piece[:, LANES:]
        return carry

    lax.fori_loop(0, depth // (2 * ROWS16), step, 0, unroll=2)
    qkv_ref[0] = dot(normed[...], w_out_ref[0]).astype(BF16)


def probs_of(query, key, table_row, bucket_ids, scale):
    bias = jnp.take_along_axis(
        jnp.broadcast_to(table_row, bucket_ids.shape), bucket_ids, axis=1
    )
    scores = dot(query, key, LAST) * scale + bias
    raised = jnp.exp(scores - jnp.max(scores, axis=-1, keepdims=True))
    return raised * (1.0 / jnp.sum(raised, axis=-1, keepdims=True))


def head_group(heads):
    return 4 if heads % 4 == 0 else 1


def forward_kernel(
    heads, projected, place_ref, *refs
):
    if projected:
        qkv_ref, table_ref, bucket_ref, wo_ref, send_ref, keep_ref, attended = refs
    else:
        (mine_ref, other_ref, arrival_ref, gain_ref, w_ref, table_ref, bucket_ref, wo_ref,
         send_ref, keep_ref, x_ref, attended) = refs
    head_dim = LANES
    scale = head_dim ** (-0.5)
    core = place_ref[0]
    half = send_ref.shape[0]
    group = head_group(heads)
    width = group * head_dim
    normed = None
    if not projected:
        x_ref[pl.ds(pl.multiple_of(core * half, half), half)] = mine_ref[...]
        x_ref[pl.ds(pl.multiple_of((1 - core) * half, half), half)] = other_ref[...]

        @pl.when(place_ref[1] == 0)
        def _():
            x_ref[...] = arrival_ref[...]

        normed = rms_normed(x_ref[...], gain_ref[...])

    def step(g, carry):
        at = pl.ds(pl.multiple_of(g * width, width), width)
        if projected:
            query, key, value = (qkv_ref[c, :, at] for c in range(3))
        else:
            query, key, value = (dot(normed, w_ref[c, :, at]).astype(BF16) for c in range(3))
        outs = []
        for h in range(group):
            sl = slice(h * head_dim, (h + 1) * head_dim)
            probs = probs_of(
                query[:, sl], key[:, sl], table_ref[pl.ds(g * group + h, 1)], bucket_ref[...], scale
            )
            outs.append(dot(probs.astype(BF16), value[:, sl]).astype(BF16))
        attended[:, at] = jnp.concatenate(outs, axis=1)
        return carry

    lax.fori_loop(0, heads // group, step, 0)
    send_at = pl.ds(pl.multiple_of((1 - core) * half, half), half)
    keep_at = pl.ds(pl.multiple_of(core * half, half), half)
    send_ref[...] = dot(attended[send_at], wo_ref[...]).astype(BF16)
    keep_ref[...] = dot(attended[keep_at], wo_ref[...])


def stash_kernel(x_ref, gain_ref, w_ref, qkv_ref, normed):
    ticks, tokens, _ = x_ref.shape
    for t in range(ticks):
        normed[t * tokens : (t + 1) * tokens] = rms_normed(x_ref[t], gain_ref[...])
    width = min(512, w_ref.shape[2])

    def step(i, carry):
        at = pl.ds(pl.multiple_of(i * width, width), width)
        for c in range(3):
            out = dot(normed[...], w_ref[c, :, at]).astype(BF16)
            for t in range(ticks):
                qkv_ref[t, c, :, at] = out[t * tokens : (t + 1) * tokens]
        return carry

    lax.fori_loop(0, w_ref.shape[2] // width, step, 0)


def backward_kernel(heads, first, place_ref, *refs):
    if first:
        (g_in_ref, qkv_ref, table_ref, bucket_ref, w_ref, wo_ref,
         send_ref, keep_ref, acc_ref, stacked) = refs
        g_ref = g_in_ref
    else:
        (mine_ref, other_ref, qkv_ref, table_ref, bucket_ref, w_ref, wo_ref, acc_in_ref,
         send_ref, keep_ref, acc_ref, stacked, g_ref) = refs
    head_dim = LANES
    scale = head_dim ** (-0.5)
    core = place_ref[0]
    half = send_ref.shape[0]
    group = head_group(heads)
    width = group * head_dim
    if not first:
        g_ref[pl.ds(pl.multiple_of(core * half, half), half)] = mine_ref[...]
        g_ref[pl.ds(pl.multiple_of((1 - core) * half, half), half)] = other_ref[...]

    def step(g, carry):
        at = pl.ds(pl.multiple_of(g * width, width), width)
        query, key, value = (qkv_ref[c, :, at] for c in range(3))
        grad_attn = dot(g_ref[...], wo_ref[at], LAST).astype(BF16)
        grads = ([], [], [])
        for h in range(group):
            sl = slice(h * head_dim, (h + 1) * head_dim)
            q, k, v, ga = query[:, sl], key[:, sl], value[:, sl], grad_attn[:, sl]
            probs = probs_of(q, k, table_ref[pl.ds(g * group + h, 1)], bucket_ref[...], scale)
            probs16 = probs.astype(BF16)
            grad_probs = dot(ga, v, LAST)
            row = jnp.sum(probs * grad_probs, axis=-1, keepdims=True)
            grad_scores = probs * (grad_probs - row)
            grad16 = grad_scores.astype(BF16)
            if first:
                acc_ref[g * group + h] = grad_scores
            else:
                acc_ref[g * group + h] = acc_in_ref[g * group + h] + grad_scores
            grads[0].append((dot(grad16, k) * scale).astype(BF16))
            grads[1].append((dot(grad16, q, FIRST) * scale).astype(BF16))
            grads[2].append(dot(probs16, ga, FIRST).astype(BF16))
        for c in range(3):
            stacked[c, :, at] = jnp.concatenate(grads[c], axis=1)
        return carry

    lax.fori_loop(0, heads // group, step, 0)
    total = dot(stacked[0], w_ref[0], LAST)
    total += dot(stacked[1], w_ref[1], LAST)
    total += dot(stacked[2], w_ref[2], LAST)

    @pl.when(core == 0)
    def _():
        send_ref[...] = total[half:].astype(BF16)
        keep_ref[...] = total[:half]

    @pl.when(core != 0)
    def _():
        send_ref[...] = total[:half].astype(BF16)
        keep_ref[...] = total[half:]


def finish_back_kernel(x_ref, g_ref, gain_ref, first_ref, second_ref, out_ref):
    x = x_ref[...].astype(F32)
    inverse = lax.rsqrt(jnp.mean(x * x, axis=-1, keepdims=True) + EPSILON)
    weighted = gain_ref[...] * (first_ref[...].astype(F32) + second_ref[...].astype(F32))
    mean = jnp.mean(x * weighted, axis=-1, keepdims=True)
    cubed = inverse * inverse * inverse
    out_ref[...] = (g_ref[...].astype(F32) + inverse * weighted - x * cubed * mean).astype(BF16)


def table_kernel(buckets_here, acc_ref, bucket_ref, out_ref):
    heads, tokens, _ = acc_ref.shape
    rows = 8
    cells = heads * rows
    columns = buckets_here * rows
    total = jnp.zeros((cells, columns), F32)
    for i in range(tokens // rows):
        at = slice(i * rows, (i + 1) * rows)
        ids = bucket_ref[at]
        hits = jnp.concatenate(
            [(ids == b).astype(F32) for b in range(buckets_here)], axis=0
        ).astype(BF16)
        part = acc_ref[:, at, :].reshape(cells, tokens)
        high = part.astype(BF16)
        low = (part - high.astype(F32)).astype(BF16)
        total += dot(high, hits, LAST) + dot(low, hits, LAST)
    row = lax.broadcasted_iota(jnp.int32, (cells, columns), 0)
    col = lax.broadcasted_iota(jnp.int32, (cells, columns), 1)
    total = jnp.where((row & (rows - 1)) == (col & (rows - 1)), total, 0.0)
    out_ref[...] = jnp.sum(total.reshape(heads, rows, columns), axis=1)


def call(kernel, out_shape, args, scratch=(), specs=None, flops=0, limit=40, **more):
    return pl.pallas_call(
        kernel,
        out_shape=out_shape,
        in_specs=specs or [WHOLE] * len(args),
        out_specs=jax.tree.map(lambda _: WHOLE, out_shape),
        scratch_shapes=list(scratch),
        compiler_params=pltpu.CompilerParams(vmem_limit_bytes=limit * MIB),
        cost_estimate=pl.CostEstimate(flops=flops, bytes_accessed=1 << 20, transcendentals=0),
        **more,
    )(*args)


def shape(dims, dtype=BF16):
    return jax.ShapeDtypeStruct(dims, dtype)


def vmem(x):
    return pltpu.with_memory_space_constraint(x, pltpu.VMEM)


def shifted(block, axis, distance):
    devices = range(lax.axis_size(axis))
    route = [(i - distance, i) for i in devices if i - distance in devices]
    return lax.ppermute(block, axis, route)


def swapped(block, bit):
    return lax.ppermute(block, "head", [(i, i ^ bit) for i in range(lax.axis_size("head"))])


def per_device(rising, falling, stash, queue, order, buckets, bias_table, gain, w_qkv, w_out):
    section_index = lax.axis_index("section")
    section_count = lax.axis_size("section")
    head_index = lax.axis_index("head")
    head_count = lax.axis_size("head")
    _, model_width, heads, _, head_dim = w_qkv.shape
    tokens = buckets.shape[0]
    bucket_count = bias_table.shape[1]
    half = tokens // 2
    inner = heads * head_dim
    core = head_index % 2
    place = jnp.stack([core, section_index]).astype(jnp.int32)
    table = jnp.pad(bias_table[0].T, ((0, 0), (0, LANES - bucket_count)))
    wo = w_out[0].reshape(inner, model_width)
    is_last = section_index == section_count - 1
    per_mac = 2 * tokens * model_width * inner

    def own_half(full):
        return lax.dynamic_slice_in_dim(full, core * half, half, 0)

    if heads % ROWS16 == 0:
        rows_first = jnp.transpose(w_qkv[0], (0, 2, 1, 3)).reshape(model_width, 3 * heads, head_dim)
        weights, qkv = pl.pallas_call(
            functools.partial(relayout_kernel, heads),
            grid=(3,),
            out_shape=(shape((3, model_width, inner)), shape((3, tokens, inner))),
            in_specs=[
                pl.BlockSpec((1, tokens, model_width), lambda c: (0, 0, 0)),
                pl.BlockSpec((1, model_width), lambda c: (0, 0)),
                pl.BlockSpec((model_width, heads, head_dim), lambda c: (0, c, 0)),
            ],
            out_specs=(
                pl.BlockSpec((1, model_width, inner), lambda c: (c, 0, 0)),
                pl.BlockSpec((1, tokens, inner), lambda c: (c, 0, 0)),
            ),
            scratch_shapes=[pltpu.VMEM((tokens, model_width), BF16)],
            compiler_params=pltpu.CompilerParams(vmem_limit_bytes=40 * MIB),
            cost_estimate=pl.CostEstimate(
                flops=9 * per_mac, bytes_accessed=8 * w_qkv.size, transcendentals=0
            ),
        )(rising, gain, rows_first)
    else:
        weights = jnp.transpose(w_qkv[0], (2, 0, 1, 3)).reshape(3, model_width, inner)
        qkv = call(
            stash_kernel,
            shape((1, 3, tokens, inner)),
            (rising, gain, weights),
            scratch=[pltpu.VMEM((tokens, model_width), BF16)],
            flops=3 * per_mac,
        )[0]

    def forward(x_parts, projections):
        scratch = [pltpu.VMEM((tokens, inner), BF16)]
        common = (table, buckets, wo)
        if x_parts is None:
            args = (place, projections) + common
        else:
            args = (place,) + x_parts + (gain, weights) + common
            scratch = [pltpu.VMEM((tokens, model_width), BF16)] + scratch
        return call(
            functools.partial(forward_kernel, heads, x_parts is None),
            (shape((half, model_width)), shape((half, model_width), F32)),
            args,
            scratch=scratch,
            specs=[SCALARS] + [WHOLE] * (len(args) - 1),
            flops=per_mac * (2 if x_parts is None else 5),
        )

    def backward(g_parts, projections, acc):
        scratch = [pltpu.VMEM((3, tokens, inner), BF16)]
        first = acc is None
        args = (place,) + g_parts + (projections, table, buckets, weights, wo)
        if not first:
            args += (acc,)
            scratch += [pltpu.VMEM((tokens, model_width), BF16)]
        return call(
            functools.partial(backward_kernel, heads, first),
            (
                shape((half, model_width)),
                shape((half, model_width), F32),
                shape((heads, tokens, tokens), F32),
            ),
            args,
            scratch=scratch,
            specs=[SCALARS] + [WHOLE] * (len(args) - 1),
            flops=per_mac * 6,
        )

    def reduced(send, keep):
        pair = (keep + swapped(send, 1).astype(F32)).astype(BF16)
        bit = 2
        while 2 * bit < head_count:
            pair = (pair.astype(F32) + swapped(pair, bit).astype(F32)).astype(BF16)
            bit *= 2
        return pair, swapped(pair, bit)

    x_half = own_half(rising[0])
    g_half = own_half(falling[0])
    x_parts = None
    g_parts = (falling[0],)
    acc = None
    stashed = None
    for t in range(TICKS):
        send, keep = forward(x_parts, qkv)
        first, second = reduced(send, keep)
        lifted = (x_half.astype(F32) + (first.astype(F32) + second.astype(F32))).astype(BF16)
        if stashed is None:
            stashed = call(
                stash_kernel,
                shape((TICKS, 3, tokens, inner)),
                (stash[0], gain, weights),
                scratch=[pltpu.VMEM((TICKS * tokens, model_width), BF16)],
                flops=3 * TICKS * per_mac,
            )
        send, keep, acc = backward(g_parts, stashed[t], acc)
        first, second = reduced(send, keep)
        lowered = call(
            finish_back_kernel,
            shape((half, model_width)),
            (own_half(stash[0, t]), g_half, gain, first, second),
        )
        if t + 1 < TICKS:
            arrival = lax.dynamic_index_in_dim(queue, order[t], 0, keepdims=False)
            climbed = shifted(lifted, "section", 1)
            x_parts = (climbed, swapped(climbed, 1), arrival)
            x_half = jnp.where(section_index == 0, own_half(arrival), climbed)
            g_half = jnp.where(is_last, lifted, shifted(lowered, "section", -1))
            g_parts = (g_half, swapped(g_half, 1))

    def whole(mine):
        other = swapped(mine, 1)
        low = jnp.where(core == 0, mine, other)
        high = jnp.where(core == 0, other, mine)
        return jnp.concatenate([low, high], axis=0)[None]

    cells = call(
        functools.partial(table_kernel, bucket_count), shape((heads, bucket_count * 8), F32), (acc, buckets)
    )
    table_grad = cells.reshape(heads, bucket_count, 8).sum(-1).T[None]
    return (whole(lifted), whole(lowered), table_grad)


def solution(mesh):
    return jax.shard_map(
        per_device,
        mesh=mesh,
        in_specs=(
            P(("groups", "section"), None, None),
            P(("groups", "section"), None, None),
            P(("groups", "section"), None, None, None),
            P("groups", None, None),
            P("groups"),
            P(),
            P("section", None, "head"),
            P("section", None),
            P("section", None, "head", None, None),
            P("section", "head", None, None),
        ),
        out_specs=(
            P(("groups", "section"), None, None),
            P(("groups", "section"), None, None),
            P(("groups", "section"), None, "head"),
        ),
        check_vma=False,
    )
```

```python
import functools

import jax
import jax.numpy as jnp
from jax import lax
from jax.experimental import pallas as pl
from jax.experimental.pallas import tpu as pltpu
from jax.sharding import PartitionSpec as P

TICKS = 3
EPSILON = 1e-06
LANES = 128
ROWS16 = 16
LAST = (((1,), (1,)), ((), ()))
FIRST = (((0,), (0,)), ((), ()))
F32 = jnp.float32
BF16 = jnp.bfloat16
WHOLE = pl.BlockSpec(memory_space=pltpu.VMEM)
SCALARS = pl.BlockSpec(memory_space=pltpu.SMEM)
UNREAD = pl.BlockSpec(memory_space=pl.ANY)
MIB = 1 << 20


def dot(a, b, dims=None):
    if dims is None:
        return jnp.dot(a, b, preferred_element_type=F32)
    return lax.dot_general(a, b, dims, preferred_element_type=F32)


def rms_normed(rows, gain_row):
    x = rows.astype(F32)
    inverse = lax.rsqrt(jnp.mean(x * x, axis=-1, keepdims=True) + EPSILON)
    return (x * inverse * gain_row).astype(BF16)


def rows_at(index, size):
    return pl.ds(pl.multiple_of(index * size, size), size)


def fill_bias(table_ref, bucket_ref, bias_ref):
    ids = bucket_ref[...].T
    for h in range(bias_ref.shape[0]):
        row = jnp.broadcast_to(table_ref[h : h + 1], ids.shape)
        bias_ref[h] = jnp.take_along_axis(row, ids, axis=1)


def bias_kernel(table_ref, bucket_ref, bias_ref):
    fill_bias(table_ref, bucket_ref, bias_ref)


def relayout_kernel(x_ref, gain_ref, table_ref, bucket_ref, w_ref, w_out_ref, qkv_ref, bias_ref, normed):
    which = pl.program_id(0)
    block = pl.program_id(1)

    @pl.when((which == 0) & (block == 0))
    def _():
        normed[...] = rms_normed(x_ref[0], gain_ref[...])
        fill_bias(table_ref, bucket_ref, bias_ref)

    depth = w_ref.shape[0]
    size = ROWS16 * ROWS16
    row = lax.broadcasted_iota(jnp.int32, (size, size), 0)
    col = lax.broadcasted_iota(jnp.int32, (size, size), 1)
    wanted = (row & (ROWS16 - 1)) * ROWS16 + (row >> 4)
    permute = (col == wanted).astype(F32).astype(BF16)

    def step(i, carry):
        d0 = pl.multiple_of(i * 2 * ROWS16, 2 * ROWS16)
        first = w_ref[pl.ds(d0, ROWS16)].reshape(size, LANES)
        second = w_ref[pl.ds(d0 + ROWS16, ROWS16)].reshape(size, LANES)
        moved = dot(permute, jnp.concatenate([first, second], axis=1)).astype(BF16)
        to = pl.multiple_of(block * depth + d0, 2 * ROWS16)
        for h in range(ROWS16):
            piece = moved[h * ROWS16 : (h + 1) * ROWS16]
            lanes = slice(h * LANES, (h + 1) * LANES)
            w_out_ref[which, pl.ds(to, ROWS16), lanes] = piece[:, :LANES]
            w_out_ref[which, pl.ds(to + ROWS16, ROWS16), lanes] = piece[:, LANES:]
        return carry

    lax.fori_loop(0, depth // (2 * ROWS16), step, 0, unroll=4)

    @pl.when(block == pl.num_programs(1) - 1)
    def _():
        qkv_ref[which] = dot(normed[...], w_out_ref[which]).astype(BF16)


def probs_of(query, key, bias, scale):
    scores = dot(key, query, LAST) * scale + bias
    raised = jnp.exp(scores - jnp.max(scores, axis=0, keepdims=True))
    return raised * (1.0 / jnp.sum(raised, axis=0, keepdims=True))


def attend(query, key, value, bias_ref, heads, first_head):
    scale = LANES ** (-0.5)
    lanes = [slice(h * LANES, (h + 1) * LANES) for h in range(heads)]
    probs = [
        probs_of(query[:, sl], key[:, sl], bias_ref[first_head + h], scale).astype(BF16)
        for h, sl in enumerate(lanes)
    ]
    return [dot(p, value[:, sl], FIRST).astype(BF16) for p, sl in zip(probs, lanes)]


def first_attend_kernel(qkv_ref, bias_ref, out_ref):
    heads = bias_ref.shape[0]
    group = heads // 2

    def step(g, carry):
        at = rows_at(g, group * LANES)
        query, key, value = (qkv_ref[c, :, at] for c in range(3))
        outs = attend(query, key, value, bias_ref, group, g * group)
        out_ref[:, at] = jnp.concatenate(outs, axis=1)
        return carry

    lax.fori_loop(0, 2, step, 0)


def project_attend(normed, w_ref, bias_ref, out_ref, part):
    heads = bias_ref.shape[0] // 2
    at = slice(part * heads * LANES, (part + 1) * heads * LANES)
    query, key, value = (dot(normed, w_ref[c, :, at]).astype(BF16) for c in range(3))
    outs = attend(query, key, value, bias_ref, heads, part * heads)
    for h, out in enumerate(outs):
        out_ref[:, h * LANES : (h + 1) * LANES] = out


def forward_a_kernel(
    tick, place_ref, order_ref, mine_ref, other_ref, queue_ref, gain_ref, w_ref, bias_ref,
    out_ref, normed_ref, x_half_ref, x_ref,
):
    core = place_ref[0]
    half = mine_ref.shape[0]
    x_ref[rows_at(core, half)] = mine_ref[...]
    x_ref[rows_at(1 - core, half)] = other_ref[...]

    @pl.when(place_ref[1] == 0)
    def _():
        x_ref[...] = queue_ref[order_ref[tick - 1]]

    x_half_ref[...] = x_ref[rows_at(core, half)]
    normed = rms_normed(x_ref[...], gain_ref[...])
    normed_ref[...] = normed
    project_attend(normed, w_ref, bias_ref, out_ref, 0)


def forward_b_kernel(normed_ref, w_ref, bias_ref, out_ref):
    project_attend(normed_ref[...], w_ref, bias_ref, out_ref, 1)


def forward_c_kernel(place_ref, *refs):
    *attended, wo_ref, send_ref, keep_ref, joined = refs
    core = place_ref[0]
    half = send_ref.shape[0]
    width = 0
    for a in attended:
        joined[:, width : width + a.shape[1]] = a[...]
        width += a.shape[1]
    total = dot(joined[...], wo_ref[...])
    split_halves(core, total, send_ref, keep_ref)


def split_halves(core, total, send_ref, keep_ref):
    half = send_ref.shape[0]

    @pl.when(core == 0)
    def _():
        send_ref[...] = total[half:].astype(BF16)
        keep_ref[...] = total[:half]

    @pl.when(core != 0)
    def _():
        send_ref[...] = total[:half].astype(BF16)
        keep_ref[...] = total[half:]


def stash_kernel(x_ref, gain_ref, w_ref, *refs):
    *outs, normed = refs
    ticks, tokens, _ = x_ref.shape
    for t in range(ticks):
        normed[t * tokens : (t + 1) * tokens] = rms_normed(x_ref[t], gain_ref[...])
    width = min(512, w_ref.shape[2])

    def step(i, carry):
        at = rows_at(i, width)
        for c in range(3):
            out = dot(normed[...], w_ref[c, :, at]).astype(BF16)
            for t in range(ticks):
                outs[t][c, :, at] = out[t * tokens : (t + 1) * tokens]
        return carry

    lax.fori_loop(0, w_ref.shape[2] // width, step, 0)


def grad_attend(g, qkv_ref, bias_ref, wo_ref, acc_in_ref, stacked_ref, acc_ref, part):
    heads = bias_ref.shape[0] // 2
    scale = LANES ** (-0.5)
    at = slice(part * heads * LANES, (part + 1) * heads * LANES)
    grad_attn = dot(wo_ref[at], g, LAST).astype(BF16)
    for h in range(heads):
        here = slice((part * heads + h) * LANES, (part * heads + h + 1) * LANES)
        own = slice(h * LANES, (h + 1) * LANES)
        q, k, v = (qkv_ref[c, :, here] for c in range(3))
        ga = grad_attn[own]
        probs = probs_of(q, k, bias_ref[part * heads + h], scale)
        grad_probs = dot(v, ga)
        total = jnp.sum(probs * grad_probs, axis=0, keepdims=True)
        grad_scores = probs * (grad_probs - total)
        grad16 = grad_scores.astype(BF16)
        if acc_in_ref is None:
            acc_ref[h] = grad_scores
        else:
            acc_ref[h] = acc_in_ref[h] + grad_scores
        stacked_ref[0, :, own] = (dot(grad16, k, FIRST) * scale).astype(BF16)
        stacked_ref[1, :, own] = (dot(grad16, q) * scale).astype(BF16)
        stacked_ref[2, :, own] = dot(probs.astype(BF16), ga, LAST).astype(BF16)


def backward_a_kernel(first, place_ref, *refs):
    core = place_ref[0]
    if first:
        full_ref, qkv_ref, bias_ref, wo_ref, stacked_ref, acc_ref, g_ref, g_half_ref = refs
        acc_in_ref = None
        half = g_half_ref.shape[0]
        g_ref[...] = full_ref[...]
    else:
        (mine_ref, other_ref, qkv_ref, bias_ref, wo_ref, acc_in_ref,
         stacked_ref, acc_ref, g_ref, g_half_ref) = refs
        half = g_half_ref.shape[0]
        g_ref[rows_at(core, half)] = mine_ref[...]
        g_ref[rows_at(1 - core, half)] = other_ref[...]
    g_half_ref[...] = g_ref[rows_at(core, half)]
    grad_attend(g_ref[...], qkv_ref, bias_ref, wo_ref, acc_in_ref, stacked_ref, acc_ref, 0)


def backward_b_kernel(first, g_ref, qkv_ref, bias_ref, wo_ref, *refs):
    acc_in_ref = None if first else refs[0]
    stacked_ref, acc_ref = refs[-2:]
    grad_attend(g_ref[...], qkv_ref, bias_ref, wo_ref, acc_in_ref, stacked_ref, acc_ref, 1)


def backward_c_kernel(place_ref, low_ref, high_ref, w_ref, send_ref, keep_ref):
    width = low_ref.shape[2]
    total = None
    for c in range(3):
        for part, ref in enumerate((low_ref, high_ref)):
            term = dot(w_ref[c, :, part * width : (part + 1) * width], ref[c], LAST)
            total = term if total is None else total + term
    split_halves(place_ref[0], total.T, send_ref, keep_ref)


def pair_kernel(keep_ref, received_ref, out_ref):
    out_ref[...] = (keep_ref[...].astype(F32) + received_ref[...].astype(F32)).astype(BF16)


def finish_up_kernel(x_ref, first_ref, second_ref, out_ref):
    total = first_ref[...].astype(F32) + second_ref[...].astype(F32)
    out_ref[...] = (x_ref[...].astype(F32) + total).astype(BF16)


def finish_down_kernel(tick, place_ref, stash_ref, g_ref, gain_ref, first_ref, second_ref, out_ref):
    half = out_ref.shape[0]
    x = stash_ref[tick, rows_at(place_ref[0], half)].astype(F32)
    inverse = lax.rsqrt(jnp.mean(x * x, axis=-1, keepdims=True) + EPSILON)
    weighted = gain_ref[...] * (first_ref[...].astype(F32) + second_ref[...].astype(F32))
    mean = jnp.mean(x * weighted, axis=-1, keepdims=True)
    cubed = inverse * inverse * inverse
    out_ref[...] = (g_ref[...].astype(F32) + inverse * weighted - x * cubed * mean).astype(BF16)


def choose_kernel(place_ref, own_ref, arrived_ref, out_ref):
    @pl.when(place_ref[2] == 1)
    def _():
        out_ref[...] = own_ref[...]

    @pl.when(place_ref[2] == 0)
    def _():
        out_ref[...] = arrived_ref[...]


def join_kernel(place_ref, mine_ref, other_ref, out_ref):
    core = place_ref[0]
    half = mine_ref.shape[0]
    out_ref[0, rows_at(core, half)] = mine_ref[...]
    out_ref[0, rows_at(1 - core, half)] = other_ref[...]


def table_kernel(buckets_here, low_ref, high_ref, bucket_ref, out_ref):
    heads, tokens, _ = low_ref.shape
    rows = 8
    cells = 2 * heads * rows
    columns = buckets_here * rows
    total = jnp.zeros((cells, columns), F32)
    turned = bucket_ref[...].T
    for i in range(tokens // rows):
        at = slice(i * rows, (i + 1) * rows)
        ids = turned[at]
        hits = jnp.concatenate(
            [(ids == b).astype(F32) for b in range(buckets_here)], axis=0
        ).astype(BF16)
        part = jnp.concatenate(
            [r[:, at, :].reshape(heads * rows, tokens) for r in (low_ref, high_ref)], axis=0
        )
        high = part.astype(BF16)
        low = (part - high.astype(F32)).astype(BF16)
        total += dot(high, hits, LAST) + dot(low, hits, LAST)
    row = lax.broadcasted_iota(jnp.int32, (cells, columns), 0)
    col = lax.broadcasted_iota(jnp.int32, (cells, columns), 1)
    total = jnp.where((row & (rows - 1)) == (col & (rows - 1)), total, 0.0)
    summed = jnp.sum(total.reshape(2 * heads, rows, columns), axis=1)
    spread = lax.broadcasted_iota(jnp.int32, (columns, buckets_here), 0) >> 3
    bucket = lax.broadcasted_iota(jnp.int32, (columns, buckets_here), 1)
    fold = (spread == bucket).astype(F32)
    out_ref[...] = jnp.dot(
        summed, fold, preferred_element_type=F32, precision=lax.Precision.HIGHEST
    )


def shape(dims, dtype=BF16):
    return jax.ShapeDtypeStruct(dims, dtype)


class Chain:
    def __init__(self):
        self.before = None

    def __call__(self, kernel, out_shape, args, scratch=(), scalars=0, after=(), flops=0, limit=16):
        outs = out_shape if isinstance(out_shape, tuple) else (out_shape,)
        extra = tuple(after) + (() if self.before is None else (self.before,))
        count = len(args)

        def body(*refs):
            kernel(*refs[:count], *refs[count + len(extra) :])

        results = pl.pallas_call(
            body,
            out_shape=outs,
            in_specs=[SCALARS] * scalars + [WHOLE] * (count - scalars) + [UNREAD] * len(extra),
            out_specs=tuple(WHOLE for _ in outs),
            scratch_shapes=list(scratch),
            compiler_params=pltpu.CompilerParams(vmem_limit_bytes=limit * MIB),
            cost_estimate=pl.CostEstimate(flops=flops, bytes_accessed=MIB, transcendentals=0),
        )(*args, *extra)
        self.before = results[0]
        return results if isinstance(out_shape, tuple) else results[0]


def vmem(x):
    return pltpu.with_memory_space_constraint(x, pltpu.VMEM)


def shifted(block, axis, distance):
    devices = range(lax.axis_size(axis))
    route = [(i - distance, i) for i in devices if i - distance in devices]
    return lax.ppermute(block, axis, route)


def swapped(block, bit):
    return lax.ppermute(block, "head", [(i, i ^ bit) for i in range(lax.axis_size("head"))])


def per_device(rising, falling, stash, queue, order, buckets, bias_table, gain, w_qkv, w_out):
    section_index = lax.axis_index("section")
    section_count = lax.axis_size("section")
    head_index = lax.axis_index("head")
    head_count = lax.axis_size("head")
    _, model_width, heads, _, head_dim = w_qkv.shape
    tokens = buckets.shape[0]
    bucket_count = bias_table.shape[1]
    half = tokens // 2
    inner = heads * head_dim
    core = head_index % 2
    is_last = section_index == section_count - 1
    place = jnp.stack([core, section_index, is_last]).astype(jnp.int32)
    table = jnp.pad(bias_table[0].T, ((0, 0), (0, LANES - bucket_count)))
    wo = vmem(w_out[0].reshape(inner, model_width))
    per_mac = 2 * tokens * model_width * inner
    run = Chain()
    pairs = [1 << b for b in range(1, head_count.bit_length() - 1)]

    if heads % ROWS16 == 0:
        rows_first = jnp.transpose(w_qkv[0], (0, 2, 1, 3)).reshape(model_width, 3 * heads, head_dim)
        blocks = 4
        depth = model_width // blocks
        fixed = lambda rank: lambda c, b: (0,) * rank
        weights, qkv, bias = pl.pallas_call(
            relayout_kernel,
            grid=(3, blocks),
            out_shape=(
                pltpu.VMEM((3, model_width, inner), BF16),
                shape((3, tokens, inner)),
                shape((heads, tokens, tokens), F32),
            ),
            in_specs=[
                pl.BlockSpec((1, tokens, model_width), fixed(3)),
                pl.BlockSpec((1, model_width), fixed(2)),
                pl.BlockSpec((heads, LANES), fixed(2)),
                pl.BlockSpec((tokens, tokens), fixed(2)),
                pl.BlockSpec((depth, heads, head_dim), lambda c, b: (b, c, 0)),
            ],
            out_specs=(
                WHOLE,
                pl.BlockSpec((3, tokens, inner), fixed(3)),
                pl.BlockSpec((heads, tokens, tokens), fixed(3)),
            ),
            scratch_shapes=[pltpu.VMEM((tokens, model_width), BF16)],
            compiler_params=pltpu.CompilerParams(vmem_limit_bytes=24 * MIB),
            cost_estimate=pl.CostEstimate(
                flops=9 * per_mac, bytes_accessed=2 * w_qkv.size, transcendentals=0
            ),
        )(rising, gain, table, buckets, rows_first)
        run.before = qkv
    else:
        weights = jnp.transpose(w_qkv[0], (2, 0, 1, 3)).reshape(3, model_width, inner)
        bias = run(bias_kernel, shape((heads, tokens, tokens), F32), (table, buckets))
        qkv = run(
            stash_kernel,
            shape((3, tokens, inner)),
            (rising, gain, weights),
            scratch=[pltpu.VMEM((tokens, model_width), BF16)],
            flops=3 * per_mac,
        )
    weights = vmem(weights)
    halves = (shape((half, model_width)), shape((half, model_width), F32))
    half_rows = shape((half, model_width))
    acc_shape = shape((heads // 2, tokens, tokens), F32)
    part_shape = shape((tokens, inner // 2))
    stacked_shape = shape((3, tokens, inner // 2))
    row_scratch = pltpu.VMEM((tokens, model_width), BF16)

    def out_projection(attended):
        return run(
            forward_c_kernel,
            halves,
            (place,) + attended + (wo,),
            scratch=[pltpu.VMEM((tokens, inner), BF16)],
            scalars=1,
            flops=per_mac,
        )

    def across(pair):
        for bit in pairs[:-1]:
            pair = run(pair_kernel, half_rows, (pair, swapped(pair, bit)))
        return pair, swapped(pair, pairs[-1])

    x_half = lax.dynamic_slice_in_dim(rising[0], core * half, half, 0)
    stashed = None
    pending = None
    acc = (None, None)
    x_mine = x_other = g_mine = g_other = None

    def finish_down(state):
        tick, g_half, first, second = state
        return run(
            functools.partial(finish_down_kernel, tick),
            half_rows,
            (place, stash[0], g_half, gain, first, second),
            scalars=1,
        )

    for t in range(TICKS):
        final = t + 1 == TICKS
        if t == 0:
            attended = (run(first_attend_kernel, shape((tokens, inner)), (qkv, bias)),)
        else:
            low, normed, x_half = run(
                functools.partial(forward_a_kernel, t),
                (part_shape, shape((tokens, model_width)), half_rows),
                (place, order, x_mine, x_other, queue, gain, weights, bias),
                scratch=[row_scratch],
                scalars=2,
                flops=3 * per_mac,
            )
            send, keep, g_half = pending
            pair = run(pair_kernel, half_rows, (keep, swapped(send, 1)))
            first, second = across(pair)
            high = run(forward_b_kernel, part_shape, (normed, weights, bias), flops=3 * per_mac)
            lowered = finish_down((t - 1, g_half, first, second))
            descended = shifted(lowered, "section", -1)
            attended = (low, high)
        send, keep = out_projection(attended)
        swap_up = swapped(send, 1)
        if t == 0:
            stashed = run(
                stash_kernel,
                (shape((3, tokens, inner)),) * TICKS,
                (stash[0], gain, weights),
                scratch=[pltpu.VMEM((TICKS * tokens, model_width), BF16)],
                flops=3 * TICKS * per_mac,
            )
            g_parts = (falling[0],)
        else:
            g_mine = run(choose_kernel, half_rows, (place, lifted, descended), scalars=1)
            g_other = swapped(g_mine, 1)
            g_parts = (g_mine, g_other)

        def add_up():
            return across(run(pair_kernel, half_rows, (keep, swap_up)))

        if t == 0:
            first, second = add_up()
        acc_args = () if t == 0 else (acc[0],)
        stacked_low, acc_low, g_full, g_half = run(
            functools.partial(backward_a_kernel, t == 0),
            (stacked_shape, acc_shape, shape((tokens, model_width)), half_rows),
            (place,) + g_parts + (stashed[t], bias, wo) + acc_args,
            scalars=1,
            flops=3 * per_mac,
        )
        if t > 0:
            first, second = add_up()
            after = ()
        else:
            lifted = run(finish_up_kernel, half_rows, (x_half, first, second))
            climbed = shifted(lifted, "section", 1)
            after = ()
        acc_args = () if t == 0 else (acc[1],)
        stacked_high, acc_high = run(
            functools.partial(backward_b_kernel, t == 0),
            (stacked_shape, acc_shape),
            (g_full, stashed[t], bias, wo) + acc_args,
            flops=3 * per_mac,
        )
        acc = (acc_low, acc_high)
        if t > 0:
            lifted = run(finish_up_kernel, half_rows, (x_half, first, second))
            if not final:
                climbed = shifted(lifted, "section", 1)
        if not final:
            x_mine = climbed
            x_other = swapped(climbed, 1)
            after = (climbed,) if t == 0 else ()
        else:
            x_other = swapped(lifted, 1)
        send, keep = run(
            backward_c_kernel,
            halves,
            (place, stacked_low, stacked_high, weights),
            scalars=1,
            after=after,
            flops=3 * per_mac,
        )
        pending = (send, keep, g_half)

    send, keep, g_half = pending
    received = swapped(send, 1)
    rows = shape((1, tokens, model_width))
    rising_out = run(join_kernel, rows, (place, lifted, x_other), scalars=1)
    pair = run(pair_kernel, half_rows, (keep, received))
    first, second = across(pair)
    table_grad = run(
        functools.partial(table_kernel, bucket_count),
        shape((heads, bucket_count), F32),
        acc + (buckets,),
    )
    lowered = finish_down((TICKS - 1, g_half, first, second))
    falling_out = run(join_kernel, rows, (place, lowered, swapped(lowered, 1)), scalars=1)
    return (rising_out, falling_out, table_grad.T[None])


def solution(mesh):
    return jax.shard_map(
        per_device,
        mesh=mesh,
        in_specs=(
            P(("groups", "section"), None, None),
            P(("groups", "section"), None, None),
            P(("groups", "section"), None, None, None),
            P("groups", None, None),
            P("groups"),
            P(),
            P("section", None, "head"),
            P("section", None),
            P("section", None, "head", None, None),
            P("section", "head", None, None),
        ),
        out_specs=(
            P(("groups", "section"), None, None),
            P(("groups", "section"), None, None),
            P(("groups", "section"), None, "head"),
        ),
        check_vma=False,
    )
```

```python
import functools

import jax
import jax.numpy as jnp
from jax import lax
from jax.experimental import pallas as pl
from jax.experimental.pallas import tpu as pltpu
from jax.sharding import PartitionSpec as P

TICKS = 3
EPSILON = 1e-06
LANES = 128
ROWS16 = 16
LAST = (((1,), (1,)), ((), ()))
FIRST = (((0,), (0,)), ((), ()))
F32 = jnp.float32
BF16 = jnp.bfloat16
WHOLE = pl.BlockSpec(memory_space=pltpu.VMEM)
SCALARS = pl.BlockSpec(memory_space=pltpu.SMEM)
UNREAD = pl.BlockSpec(memory_space=pl.ANY)
MIB = 1 << 20


def dot(a, b, dims=None):
    if dims is None:
        return jnp.dot(a, b, preferred_element_type=F32)
    return lax.dot_general(a, b, dims, preferred_element_type=F32)


def rms_normed(rows, gain_row):
    x = rows.astype(F32)
    inverse = lax.rsqrt(jnp.mean(x * x, axis=-1, keepdims=True) + EPSILON)
    return (x * inverse * gain_row).astype(BF16)


def rows_at(index, size):
    return pl.ds(pl.multiple_of(index * size, size), size)


def fill_bias(table_ref, bucket_ref, bias_ref):
    ids = bucket_ref[...].T
    rows, count = table_ref.shape
    table = jnp.concatenate([table_ref[...], jnp.zeros((rows, LANES - count), F32)], axis=1)
    for h in range(rows):
        row = jnp.broadcast_to(table[h : h + 1], ids.shape)
        bias_ref[h] = jnp.take_along_axis(row, ids, axis=1)


def bias_kernel(table_ref, bucket_ref, bias_ref):
    fill_bias(table_ref, bucket_ref, bias_ref)


def relayout_kernel(
    place_ref, x_ref, gain_ref, table_ref, bucket_ref, w_ref, back_ref,
    w_out_ref, qkv_ref, bias_ref, back_out_ref, normed, arrived,
):
    which = pl.program_id(0)
    block = pl.program_id(1)
    back_copy = pltpu.make_async_copy(back_ref, back_out_ref, arrived)

    @pl.when((which == 0) & (block == 0))
    def _():
        back_copy.start()
        normed[...] = rms_normed(x_ref[0], gain_ref[...])
        fill_bias(table_ref, bucket_ref, bias_ref)

    depth = w_ref.shape[0]
    size = ROWS16 * ROWS16
    row = lax.broadcasted_iota(jnp.int32, (size, size), 0)
    col = lax.broadcasted_iota(jnp.int32, (size, size), 1)
    wanted = (row & (ROWS16 - 1)) * ROWS16 + (row >> 4)
    permute = (col == wanted).astype(F32).astype(BF16)

    def step(i, carry):
        d0 = pl.multiple_of(i * 2 * ROWS16, 2 * ROWS16)
        first = w_ref[pl.ds(d0, ROWS16)].reshape(size, LANES)
        second = w_ref[pl.ds(d0 + ROWS16, ROWS16)].reshape(size, LANES)
        moved = dot(permute, jnp.concatenate([first, second], axis=1)).astype(BF16)
        to = pl.multiple_of(block * depth + d0, 2 * ROWS16)
        for h in range(ROWS16):
            piece = moved[h * ROWS16 : (h + 1) * ROWS16]
            lanes = slice(h * LANES, (h + 1) * LANES)
            w_out_ref[which, pl.ds(to, ROWS16), lanes] = piece[:, :LANES]
            w_out_ref[which, pl.ds(to + ROWS16, ROWS16), lanes] = piece[:, LANES:]
        return carry

    lax.fori_loop(0, depth // (2 * ROWS16), step, 0, unroll=4)

    @pl.when(block == pl.num_programs(1) - 1)
    def _():
        qkv_ref[which] = dot(normed[...], w_out_ref[which]).astype(BF16)

    @pl.when((which == pl.num_programs(0) - 1) & (block == pl.num_programs(1) - 1))
    def _():
        back_copy.wait()


def probs_of(query, key, bias, scale):
    scores = dot(key, query, LAST) * scale + bias
    raised = jnp.exp(scores - jnp.max(scores, axis=0, keepdims=True))
    return raised * (1.0 / jnp.sum(raised, axis=0, keepdims=True))


def attend(query, key, value, bias_ref, heads, first_head):
    scale = LANES ** (-0.5)
    lanes = [slice(h * LANES, (h + 1) * LANES) for h in range(heads)]
    probs = [
        probs_of(query[:, sl], key[:, sl], bias_ref[first_head + h], scale).astype(BF16)
        for h, sl in enumerate(lanes)
    ]
    return [dot(p, value[:, sl], FIRST).astype(BF16) for p, sl in zip(probs, lanes)]


def first_attend_kernel(place_ref, x_ref, qkv_ref, bias_ref, out_ref, x_half_ref):
    heads = bias_ref.shape[0]
    group = heads // 2
    x_half_ref[...] = x_ref[0, rows_at(place_ref[0], x_half_ref.shape[0])]

    def step(g, carry):
        at = rows_at(g, group * LANES)
        query, key, value = (qkv_ref[c, :, at] for c in range(3))
        outs = attend(query, key, value, bias_ref, group, g * group)
        out_ref[:, at] = jnp.concatenate(outs, axis=1)
        return carry

    lax.fori_loop(0, 2, step, 0)


def project_attend(normed, w_ref, bias_ref, out_ref, part):
    heads = bias_ref.shape[0] // 2
    at = slice(part * heads * LANES, (part + 1) * heads * LANES)
    query, key, value = (dot(normed, w_ref[c, :, at]).astype(BF16) for c in range(3))
    outs = attend(query, key, value, bias_ref, heads, part * heads)
    for h, out in enumerate(outs):
        out_ref[:, h * LANES : (h + 1) * LANES] = out


def forward_a_kernel(
    tick, place_ref, order_ref, mine_ref, other_ref, queue_ref, gain_ref, w_ref, bias_ref,
    out_ref, normed_ref, x_half_ref, x_ref,
):
    core = place_ref[0]
    half = mine_ref.shape[0]
    x_ref[rows_at(core, half)] = mine_ref[...]
    x_ref[rows_at(1 - core, half)] = other_ref[...]

    @pl.when(place_ref[1] == 0)
    def _():
        x_ref[...] = queue_ref[order_ref[tick - 1]]

    x_half_ref[...] = x_ref[rows_at(core, half)]
    normed = rms_normed(x_ref[...], gain_ref[...])
    normed_ref[...] = normed
    project_attend(normed, w_ref, bias_ref, out_ref, 0)


def forward_b_kernel(normed_ref, w_ref, bias_ref, out_ref):
    project_attend(normed_ref[...], w_ref, bias_ref, out_ref, 1)


def forward_c_kernel(place_ref, *refs):
    *attended, wo_ref, send_ref, keep_ref, joined = refs
    core = place_ref[0]
    half = send_ref.shape[0]
    width = 0
    for a in attended:
        joined[:, width : width + a.shape[1]] = a[...]
        width += a.shape[1]
    total = dot(joined[...], wo_ref[...])
    split_halves(core, total, send_ref, keep_ref)


def split_halves(core, total, send_ref, keep_ref):
    half = send_ref.shape[0]

    @pl.when(core == 0)
    def _():
        send_ref[...] = total[half:].astype(BF16)
        keep_ref[...] = total[:half]

    @pl.when(core != 0)
    def _():
        send_ref[...] = total[:half].astype(BF16)
        keep_ref[...] = total[half:]


def stash_kernel(x_ref, gain_ref, w_ref, *refs):
    *outs, normed = refs
    ticks, tokens, _ = x_ref.shape
    for t in range(ticks):
        normed[t * tokens : (t + 1) * tokens] = rms_normed(x_ref[t], gain_ref[...])
    width = min(512, w_ref.shape[2])

    def step(i, carry):
        at = rows_at(i, width)
        for c in range(3):
            out = dot(normed[...], w_ref[c, :, at]).astype(BF16)
            for t in range(ticks):
                outs[t][c, :, at] = out[t * tokens : (t + 1) * tokens]
        return carry

    lax.fori_loop(0, w_ref.shape[2] // width, step, 0)


def probs_kernel(qkv_ref, bias_ref, out_ref):
    heads = bias_ref.shape[0]
    group = heads // 2
    scale = LANES ** (-0.5)

    def step(g, carry):
        at = rows_at(g, group * LANES)
        query, key = (qkv_ref[c, :, at] for c in range(2))
        for h in range(group):
            sl = slice(h * LANES, (h + 1) * LANES)
            out_ref[g * group + h] = probs_of(
                query[:, sl], key[:, sl], bias_ref[g * group + h], scale
            )
        return carry

    lax.fori_loop(0, 2, step, 0)


def grad_attend(g, qkv_ref, probs_ref, wo_ref, acc_in_ref, stacked_ref, acc_ref, part):
    heads = probs_ref.shape[0] // 2
    scale = LANES ** (-0.5)
    at = slice(part * heads * LANES, (part + 1) * heads * LANES)
    grad_attn = dot(g, wo_ref[at], LAST).astype(BF16)
    for h in range(heads):
        here = slice((part * heads + h) * LANES, (part * heads + h + 1) * LANES)
        own = slice(h * LANES, (h + 1) * LANES)
        q, k, v = (qkv_ref[c, :, here] for c in range(3))
        ga = grad_attn[:, own]
        probs = probs_ref[part * heads + h]
        grad_probs = dot(v, ga, LAST)
        total = jnp.sum(probs * grad_probs, axis=0, keepdims=True)
        grad_scores = probs * (grad_probs - total)
        grad16 = grad_scores.astype(BF16)
        if acc_in_ref is None:
            acc_ref[h] = grad_scores
        else:
            acc_ref[h] = acc_in_ref[h] + grad_scores
        stacked_ref[0, :, own] = (dot(grad16, k, FIRST) * scale).astype(BF16)
        stacked_ref[1, :, own] = (dot(grad16, q) * scale).astype(BF16)
        stacked_ref[2, :, own] = dot(probs.astype(BF16), ga).astype(BF16)


def backward_a_kernel(first, place_ref, *refs):
    core = place_ref[0]
    if first:
        full_ref, qkv_ref, probs_ref, wo_ref, stacked_ref, acc_ref, g_ref, g_half_ref = refs
        acc_in_ref = None
        half = g_half_ref.shape[0]
        g_ref[...] = full_ref[...]
    else:
        (mine_ref, other_ref, qkv_ref, probs_ref, wo_ref, acc_in_ref,
         stacked_ref, acc_ref, g_ref, g_half_ref) = refs
        half = g_half_ref.shape[0]
        g_ref[rows_at(core, half)] = mine_ref[...]
        g_ref[rows_at(1 - core, half)] = other_ref[...]
    g_half_ref[...] = g_ref[rows_at(core, half)]
    grad_attend(g_ref[...], qkv_ref, probs_ref, wo_ref, acc_in_ref, stacked_ref, acc_ref, 0)


def backward_b_kernel(first, g_ref, qkv_ref, probs_ref, wo_ref, *refs):
    acc_in_ref = None if first else refs[0]
    stacked_ref, acc_ref = refs[-2:]
    grad_attend(g_ref[...], qkv_ref, probs_ref, wo_ref, acc_in_ref, stacked_ref, acc_ref, 1)


def backward_c_kernel(place_ref, low_ref, high_ref, w_ref, send_ref, keep_ref):
    width = low_ref.shape[2]
    total = None
    for c in range(3):
        for part, ref in enumerate((low_ref, high_ref)):
            term = dot(ref[c], w_ref[c, :, part * width : (part + 1) * width], LAST)
            total = term if total is None else total + term
    split_halves(place_ref[0], total, send_ref, keep_ref)


def pair_kernel(first_ref, second_ref, out_ref):
    out_ref[...] = (first_ref[...].astype(F32) + second_ref[...].astype(F32)).astype(BF16)


def up_term_kernel(place_ref, keep_ref, received_ref, x_ref, out_ref):
    residual = place_ref[3].astype(F32)
    total = keep_ref[...] + received_ref[...].astype(F32)
    out_ref[...] = (total + residual * x_ref[...].astype(F32)).astype(BF16)


def down_term_kernel(tick, place_ref, stash_ref, gain_ref, keep_ref, received_ref, g_ref, out_ref):
    half = out_ref.shape[0]
    residual = place_ref[3].astype(F32)
    x = stash_ref[tick, rows_at(place_ref[0], half)].astype(F32)
    inverse = lax.rsqrt(jnp.mean(x * x, axis=-1, keepdims=True) + EPSILON)
    weighted = gain_ref[...] * (keep_ref[...] + received_ref[...].astype(F32))
    mean = jnp.mean(x * weighted, axis=-1, keepdims=True)
    cubed = inverse * inverse * inverse
    back = inverse * weighted - x * cubed * mean
    out_ref[...] = (residual * g_ref[...].astype(F32) + back).astype(BF16)


def choose_kernel(place_ref, own_ref, own_second_ref, first_ref, second_ref, out_ref):
    @pl.when(place_ref[2] == 1)
    def _():
        pair_kernel(own_ref, own_second_ref, out_ref)

    @pl.when(place_ref[2] == 0)
    def _():
        pair_kernel(first_ref, second_ref, out_ref)


def join_kernel(place_ref, mine_ref, other_ref, out_ref):
    core = place_ref[0]
    half = mine_ref.shape[0]
    out_ref[0, rows_at(core, half)] = mine_ref[...]
    out_ref[0, rows_at(1 - core, half)] = other_ref[...]


def table_kernel(buckets_here, low_ref, high_ref, bucket_ref, out_ref):
    heads, tokens, _ = low_ref.shape
    rows = 8
    cells = 2 * heads * rows
    columns = buckets_here * rows
    total = jnp.zeros((cells, columns), F32)
    turned = bucket_ref[...].T
    for i in range(tokens // rows):
        at = slice(i * rows, (i + 1) * rows)
        ids = turned[at]
        hits = jnp.concatenate(
            [(ids == b).astype(F32) for b in range(buckets_here)], axis=0
        ).astype(BF16)
        part = jnp.concatenate(
            [r[:, at, :].reshape(heads * rows, tokens) for r in (low_ref, high_ref)], axis=0
        )
        high = part.astype(BF16)
        low = (part - high.astype(F32)).astype(BF16)
        total += dot(high, hits, LAST) + dot(low, hits, LAST)
    row = lax.broadcasted_iota(jnp.int32, (cells, columns), 0)
    col = lax.broadcasted_iota(jnp.int32, (cells, columns), 1)
    total = jnp.where((row & (rows - 1)) == (col & (rows - 1)), total, 0.0)
    summed = jnp.sum(total.reshape(2 * heads, rows, columns), axis=1)
    spread = lax.broadcasted_iota(jnp.int32, (columns, buckets_here), 0) >> 3
    bucket = lax.broadcasted_iota(jnp.int32, (columns, buckets_here), 1)
    fold = (spread == bucket).astype(F32)
    out_ref[...] = jnp.dot(
        summed, fold, preferred_element_type=F32, precision=lax.Precision.HIGHEST
    )


def shape(dims, dtype=BF16):
    return jax.ShapeDtypeStruct(dims, dtype)


class Chain:
    def __init__(self):
        self.before = None

    def __call__(self, kernel, out_shape, args, scratch=(), scalars=0, after=(), flops=0, limit=16):
        outs = out_shape if isinstance(out_shape, tuple) else (out_shape,)
        extra = tuple(after) + (() if self.before is None else (self.before,))
        count = len(args)

        def body(*refs):
            kernel(*refs[:count], *refs[count + len(extra) :])

        results = pl.pallas_call(
            body,
            out_shape=outs,
            in_specs=[SCALARS] * scalars + [WHOLE] * (count - scalars) + [UNREAD] * len(extra),
            out_specs=tuple(WHOLE for _ in outs),
            scratch_shapes=list(scratch),
            compiler_params=pltpu.CompilerParams(vmem_limit_bytes=limit * MIB),
            cost_estimate=pl.CostEstimate(flops=flops, bytes_accessed=MIB, transcendentals=0),
        )(*args, *extra)
        self.before = results[0]
        return results if isinstance(out_shape, tuple) else results[0]


def in_hbm(x):
    return pltpu.with_memory_space_constraint(x, pltpu.HBM)


def moved(block, step, bit):
    sections, heads = lax.axis_size("section"), lax.axis_size("head")
    route = [
        (s * heads + h, (s + step) * heads + (h ^ bit))
        for s in range(sections)
        if s + step in range(sections)
        for h in range(heads)
    ]
    return lax.ppermute(block, ("section", "head"), route)


def swapped(block, bit):
    return lax.ppermute(block, "head", [(i, i ^ bit) for i in range(lax.axis_size("head"))])


def swapped_in_last(block, bit):
    sections, heads = lax.axis_size("section"), lax.axis_size("head")
    base = (sections - 1) * heads
    return lax.ppermute(
        block, ("section", "head"), [(base + h, base + (h ^ bit)) for h in range(heads)]
    )


def per_device(rising, falling, stash, queue, order, buckets, bias_table, gain, w_qkv, w_out):
    section_index = lax.axis_index("section")
    section_count = lax.axis_size("section")
    head_index = lax.axis_index("head")
    head_count = lax.axis_size("head")
    _, model_width, heads, _, head_dim = w_qkv.shape
    tokens = buckets.shape[0]
    half = tokens // 2
    inner = heads * head_dim
    core = head_index % 2
    is_last = section_index == section_count - 1
    place = jnp.stack([core, section_index, is_last, head_index < 2]).astype(jnp.int32)
    table = bias_table[0].T
    back = w_out[0].reshape(inner, model_width)
    per_mac = 2 * tokens * model_width * inner
    run = Chain()
    bits = [1 << b for b in range(1, head_count.bit_length() - 1)]
    cross = bits[-1]
    qkv_shape = shape((3, tokens, inner))
    scores_shape = shape((heads, tokens, tokens), F32)

    if heads % ROWS16 == 0:
        rows_first = jnp.transpose(w_qkv[0], (0, 2, 1, 3)).reshape(model_width, 3 * heads, head_dim)
        blocks = 4
        depth = model_width // blocks
        fixed = lambda rank: lambda c, b: (0,) * rank
        weights, qkv, bias, wo = pl.pallas_call(
            relayout_kernel,
            grid=(3, blocks),
            out_shape=(
                pltpu.VMEM((3, model_width, inner), BF16),
                qkv_shape,
                scores_shape,
                pltpu.VMEM((inner, model_width), BF16),
            ),
            in_specs=[
                SCALARS,
                pl.BlockSpec((1, tokens, model_width), fixed(3)),
                pl.BlockSpec((1, model_width), fixed(2)),
                pl.BlockSpec(table.shape, fixed(2)),
                pl.BlockSpec((tokens, tokens), fixed(2)),
                pl.BlockSpec((depth, heads, head_dim), lambda c, b: (b, c, 0)),
                UNREAD,
            ],
            out_specs=(
                WHOLE,
                pl.BlockSpec((3, tokens, inner), fixed(3)),
                pl.BlockSpec((heads, tokens, tokens), fixed(3)),
                WHOLE,
            ),
            scratch_shapes=[pltpu.VMEM((tokens, model_width), BF16), pltpu.SemaphoreType.DMA],
            compiler_params=pltpu.CompilerParams(vmem_limit_bytes=24 * MIB),
            cost_estimate=pl.CostEstimate(
                flops=9 * per_mac, bytes_accessed=2 * w_qkv.size, transcendentals=0
            ),
        )(
            place, in_hbm(rising), in_hbm(gain), in_hbm(table), in_hbm(buckets),
            in_hbm(rows_first), in_hbm(back),
        )
        run.before = qkv
    else:
        wo = back
        weights = jnp.transpose(w_qkv[0], (2, 0, 1, 3)).reshape(3, model_width, inner)
        bias = run(bias_kernel, scores_shape, (table, buckets))
        qkv = run(
            stash_kernel,
            qkv_shape,
            (rising, gain, weights),
            scratch=[pltpu.VMEM((tokens, model_width), BF16)],
            flops=3 * per_mac,
        )
    halves = (shape((half, model_width)), shape((half, model_width), F32))
    half_rows = shape((half, model_width))
    acc_shape = shape((heads // 2, tokens, tokens), F32)
    part_shape = shape((tokens, inner // 2))
    stacked_shape = shape((3, tokens, inner // 2))
    row_scratch = pltpu.VMEM((tokens, model_width), BF16)

    def but_last_bit(term):
        for bit in bits[:-1]:
            term = run(pair_kernel, half_rows, (term, swapped(term, bit)))
        return term

    def down_term(tick, keep, received, g_half):
        term = run(
            functools.partial(down_term_kernel, tick),
            half_rows,
            (place, stash[0], gain, keep, received, g_half),
            scalars=1,
        )
        return but_last_bit(term)

    stashed = arrivals = None
    acc = ()
    for t in range(TICKS):
        final = t + 1 == TICKS
        if t == 0:
            full, x_half = run(
                first_attend_kernel,
                (shape((tokens, inner)), half_rows),
                (place, rising, qkv, bias),
                scalars=1,
            )
            attended = (full,)
        else:
            low, normed, x_half = run(
                functools.partial(forward_a_kernel, t),
                (part_shape, shape((tokens, model_width)), half_rows),
                (place, order, x_mine, x_other, queue, gain, weights, bias),
                scratch=[row_scratch],
                scalars=2,
                flops=3 * per_mac,
            )
            fallen = down_term(t - 1, keep, received, g_half)
            arrivals = (up, in_last, moved(fallen, -1, 0), moved(fallen, -1, cross))
            high = run(forward_b_kernel, part_shape, (normed, weights, bias), flops=3 * per_mac)
            attended = (low, high)
        send, keep = run(
            forward_c_kernel,
            halves,
            (place,) + attended + (wo,),
            scratch=[pltpu.VMEM((tokens, inner), BF16)],
            scalars=1,
            flops=per_mac,
        )
        received = swapped(send, 1)
        if t == 0:
            stashed = run(
                stash_kernel,
                (qkv_shape,) * TICKS,
                (stash[0], gain, weights),
                scratch=[pltpu.VMEM((TICKS * tokens, model_width), BF16)],
                flops=3 * TICKS * per_mac,
            )
        else:
            probs = run(probs_kernel, scores_shape, (stashed[t], bias), flops=per_mac)
        up = but_last_bit(
            run(up_term_kernel, half_rows, (place, keep, received, x_half), scalars=1)
        )
        if final:
            climbed = (up, swapped(up, cross))
        else:
            climbed = (moved(up, 1, 0), moved(up, 1, cross))
            in_last = swapped_in_last(up, cross)
        if t == 0:
            probs = run(probs_kernel, scores_shape, (stashed[t], bias), flops=per_mac)
            g_parts = (falling[0],)
        else:
            g_mine = run(choose_kernel, half_rows, (place,) + arrivals, scalars=1)
            g_parts = (g_mine, swapped(g_mine, 1))

        stacked_low, acc_low, g_full, g_half = run(
            functools.partial(backward_a_kernel, t == 0),
            (stacked_shape, acc_shape, shape((tokens, model_width)), half_rows),
            (place,) + g_parts + (stashed[t], probs, wo) + acc[:1],
            scalars=1,
            flops=2 * per_mac,
        )
        stacked_high, acc_high = run(
            functools.partial(backward_b_kernel, t == 0),
            (stacked_shape, acc_shape),
            (g_full, stashed[t], probs, wo) + acc[1:],
            flops=2 * per_mac,
        )
        acc = (acc_low, acc_high)
        x_mine = run(pair_kernel, half_rows, climbed)
        x_other = swapped(x_mine, 1)
        send, keep = run(
            backward_c_kernel,
            halves,
            (place, stacked_low, stacked_high, weights),
            scalars=1,
            flops=3 * per_mac,
        )
        received = swapped(send, 1)

    rows = shape((1, tokens, model_width))
    rising_out = run(join_kernel, rows, (place, x_mine, x_other), scalars=1)
    fallen = down_term(TICKS - 1, keep, received, g_half)
    fallen_other = swapped(fallen, cross)
    table_grad = run(
        functools.partial(table_kernel, bias_table.shape[1]),
        shape((heads, bias_table.shape[1]), F32),
        acc + (buckets,),
    )
    lowered = run(pair_kernel, half_rows, (fallen, fallen_other))
    falling_out = run(join_kernel, rows, (place, lowered, swapped(lowered, 1)), scalars=1)
    return (rising_out, falling_out, table_grad.T[None])


def solution(mesh):
    return jax.shard_map(
        per_device,
        mesh=mesh,
        in_specs=(
            P(("groups", "section"), None, None),
            P(("groups", "section"), None, None),
            P(("groups", "section"), None, None, None),
            P("groups", None, None),
            P("groups"),
            P(),
            P("section", None, "head"),
            P("section", None),
            P("section", None, "head", None, None),
            P("section", "head", None, None),
        ),
        out_specs=(
            P(("groups", "section"), None, None),
            P(("groups", "section"), None, None),
            P(("groups", "section"), None, "head"),
        ),
        check_vma=False,
    )
```

```python
import functools

import jax
import jax.numpy as jnp
from jax import lax
from jax.experimental import pallas as pl
from jax.experimental.pallas import tpu as pltpu
from jax.sharding import PartitionSpec as P

TICKS = 3
EPSILON = 1e-06
LANES = 128
ROWS16 = 16
LAST = (((1,), (1,)), ((), ()))
FIRST = (((0,), (0,)), ((), ()))
F32 = jnp.float32
BF16 = jnp.bfloat16
WHOLE = pl.BlockSpec(memory_space=pltpu.VMEM)
SCALARS = pl.BlockSpec(memory_space=pltpu.SMEM)
UNREAD = pl.BlockSpec(memory_space=pl.ANY)
MIB = 1 << 20


def dot(a, b, dims=None):
    if dims is None:
        return jnp.dot(a, b, preferred_element_type=F32)
    return lax.dot_general(a, b, dims, preferred_element_type=F32)


def rms_normed(rows, gain_row):
    x = rows.astype(F32)
    inverse = lax.rsqrt(jnp.mean(x * x, axis=-1, keepdims=True) + EPSILON)
    return (x * inverse * gain_row).astype(BF16)


def rows_at(index, size):
    return pl.ds(pl.multiple_of(index * size, size), size)


def fill_bias(table_ref, bucket_ref, bias_ref):
    ids = bucket_ref[...].T
    rows, count = table_ref.shape
    table = jnp.concatenate([table_ref[...], jnp.zeros((rows, LANES - count), F32)], axis=1)
    for h in range(rows):
        row = jnp.broadcast_to(table[h : h + 1], ids.shape)
        bias_ref[h] = jnp.take_along_axis(row, ids, axis=1)


def bias_kernel(table_ref, bucket_ref, bias_ref):
    fill_bias(table_ref, bucket_ref, bias_ref)


def relayout_kernel(
    place_ref, x_ref, gain_ref, table_ref, bucket_ref, w_ref, back_ref,
    w_out_ref, qkv_ref, bias_ref, back_out_ref, normed, arrived,
):
    which = pl.program_id(0)
    block = pl.program_id(1)
    back_copy = pltpu.make_async_copy(back_ref, back_out_ref, arrived)

    @pl.when((which == 0) & (block == 0))
    def _():
        back_copy.start()
        normed[...] = rms_normed(x_ref[0], gain_ref[...])
        fill_bias(table_ref, bucket_ref, bias_ref)

    depth = w_ref.shape[0]
    size = ROWS16 * ROWS16
    row = lax.broadcasted_iota(jnp.int32, (size, size), 0)
    col = lax.broadcasted_iota(jnp.int32, (size, size), 1)
    wanted = (row & (ROWS16 - 1)) * ROWS16 + (row >> 4)
    permute = (col == wanted).astype(F32).astype(BF16)

    def step(i, carry):
        d0 = pl.multiple_of(i * 2 * ROWS16, 2 * ROWS16)
        first = w_ref[pl.ds(d0, ROWS16)].reshape(size, LANES)
        second = w_ref[pl.ds(d0 + ROWS16, ROWS16)].reshape(size, LANES)
        moved = dot(permute, jnp.concatenate([first, second], axis=1)).astype(BF16)
        to = pl.multiple_of(block * depth + d0, 2 * ROWS16)
        for h in range(ROWS16):
            piece = moved[h * ROWS16 : (h + 1) * ROWS16]
            lanes = slice(h * LANES, (h + 1) * LANES)
            w_out_ref[which, pl.ds(to, ROWS16), lanes] = piece[:, :LANES]
            w_out_ref[which, pl.ds(to + ROWS16, ROWS16), lanes] = piece[:, LANES:]
        return carry

    lax.fori_loop(0, depth // (2 * ROWS16), step, 0, unroll=8)

    @pl.when(block == pl.num_programs(1) - 1)
    def _():
        qkv_ref[which] = dot(normed[...], w_out_ref[which]).astype(BF16)

    @pl.when((which == pl.num_programs(0) - 1) & (block == pl.num_programs(1) - 1))
    def _():
        back_copy.wait()


def probs_of(query, key, bias, scale):
    scores = dot(key, query, LAST) * scale + bias
    raised = jnp.exp(scores - jnp.max(scores, axis=0, keepdims=True))
    return raised * (1.0 / jnp.sum(raised, axis=0, keepdims=True))


def attend(query, key, value, bias_ref, heads, first_head):
    scale = LANES ** (-0.5)
    lanes = [slice(h * LANES, (h + 1) * LANES) for h in range(heads)]
    probs = [
        probs_of(query[:, sl], key[:, sl], bias_ref[first_head + h], scale).astype(BF16)
        for h, sl in enumerate(lanes)
    ]
    return [dot(p, value[:, sl], FIRST).astype(BF16) for p, sl in zip(probs, lanes)]


def first_attend_kernel(place_ref, x_ref, qkv_ref, bias_ref, out_ref, x_half_ref):
    heads = bias_ref.shape[0]
    group = heads // 2
    x_half_ref[...] = x_ref[0, rows_at(place_ref[0], x_half_ref.shape[0])]

    def step(g, carry):
        at = rows_at(g, group * LANES)
        query, key, value = (qkv_ref[c, :, at] for c in range(3))
        outs = attend(query, key, value, bias_ref, group, g * group)
        out_ref[:, at] = jnp.concatenate(outs, axis=1)
        return carry

    lax.fori_loop(0, 2, step, 0)


def project_attend(normed, w_ref, bias_ref, out_ref, part):
    heads = bias_ref.shape[0] // 2
    at = slice(part * heads * LANES, (part + 1) * heads * LANES)
    query, key, value = (dot(normed, w_ref[c, :, at]).astype(BF16) for c in range(3))
    outs = attend(query, key, value, bias_ref, heads, part * heads)
    for h, out in enumerate(outs):
        out_ref[:, h * LANES : (h + 1) * LANES] = out


def forward_a_kernel(
    tick, place_ref, order_ref, mine_ref, other_ref, queue_ref, gain_ref, w_ref, bias_ref,
    out_ref, normed_ref, x_half_ref, x_ref,
):
    core = place_ref[0]
    half = mine_ref.shape[0]
    x_ref[rows_at(core, half)] = mine_ref[...]
    x_ref[rows_at(1 - core, half)] = other_ref[...]

    @pl.when(place_ref[1] == 0)
    def _():
        x_ref[...] = queue_ref[order_ref[tick - 1]]

    x_half_ref[...] = x_ref[rows_at(core, half)]
    normed = rms_normed(x_ref[...], gain_ref[...])
    normed_ref[...] = normed
    project_attend(normed, w_ref, bias_ref, out_ref, 0)


def forward_b_kernel(normed_ref, w_ref, bias_ref, out_ref):
    project_attend(normed_ref[...], w_ref, bias_ref, out_ref, 1)


def forward_c_kernel(place_ref, *refs):
    *attended, wo_ref, send_ref, keep_ref, joined = refs
    core = place_ref[0]
    half = send_ref.shape[0]
    width = 0
    for a in attended:
        joined[:, width : width + a.shape[1]] = a[...]
        width += a.shape[1]
    total = dot(joined[...], wo_ref[...])
    split_halves(core, total, send_ref, keep_ref)


def split_halves(core, total, send_ref, keep_ref):
    half = send_ref.shape[0]

    @pl.when(core == 0)
    def _():
        send_ref[...] = total[half:].astype(BF16)
        keep_ref[...] = total[:half]

    @pl.when(core != 0)
    def _():
        send_ref[...] = total[:half].astype(BF16)
        keep_ref[...] = total[half:]


def stash_kernel(x_ref, gain_ref, w_ref, *refs):
    *outs, normed = refs
    ticks, tokens, _ = x_ref.shape
    for t in range(ticks):
        normed[t * tokens : (t + 1) * tokens] = rms_normed(x_ref[t], gain_ref[...])
    width = min(512, w_ref.shape[2])

    def step(i, carry):
        at = rows_at(i, width)
        for c in range(3):
            out = dot(normed[...], w_ref[c, :, at]).astype(BF16)
            for t in range(ticks):
                outs[t][c, :, at] = out[t * tokens : (t + 1) * tokens]
        return carry

    lax.fori_loop(0, w_ref.shape[2] // width, step, 0)


def probs_kernel(qkv_ref, bias_ref, out_ref):
    heads = bias_ref.shape[0]
    group = heads // 2
    scale = LANES ** (-0.5)

    def step(g, carry):
        at = rows_at(g, group * LANES)
        query, key = (qkv_ref[c, :, at] for c in range(2))
        for h in range(group):
            sl = slice(h * LANES, (h + 1) * LANES)
            out_ref[g * group + h] = probs_of(
                query[:, sl], key[:, sl], bias_ref[g * group + h], scale
            )
        return carry

    lax.fori_loop(0, 2, step, 0)


def grad_attend(g, qkv_ref, probs_ref, wo_ref, acc_in_ref, stacked_ref, acc_ref, part):
    heads = probs_ref.shape[0] // 2
    scale = LANES ** (-0.5)
    at = slice(part * heads * LANES, (part + 1) * heads * LANES)
    grad_attn = dot(g, wo_ref[at], LAST).astype(BF16)
    for h in range(heads):
        here = slice((part * heads + h) * LANES, (part * heads + h + 1) * LANES)
        own = slice(h * LANES, (h + 1) * LANES)
        q, k, v = (qkv_ref[c, :, here] for c in range(3))
        ga = grad_attn[:, own]
        probs = probs_ref[part * heads + h]
        grad_probs = dot(v, ga, LAST)
        total = jnp.sum(probs * grad_probs, axis=0, keepdims=True)
        grad_scores = probs * (grad_probs - total)
        grad16 = grad_scores.astype(BF16)
        if acc_in_ref is None:
            acc_ref[h] = grad_scores
        else:
            acc_ref[h] = acc_in_ref[h] + grad_scores
        stacked_ref[0, :, own] = (dot(grad16, k, FIRST) * scale).astype(BF16)
        stacked_ref[1, :, own] = (dot(grad16, q) * scale).astype(BF16)
        stacked_ref[2, :, own] = dot(probs.astype(BF16), ga).astype(BF16)


def backward_a_kernel(first, place_ref, *refs):
    core = place_ref[0]
    if first:
        full_ref, qkv_ref, probs_ref, wo_ref, stacked_ref, acc_ref, g_ref, g_half_ref = refs
        acc_in_ref = None
        half = g_half_ref.shape[0]
        g_ref[...] = full_ref[...]
    else:
        (mine_ref, other_ref, qkv_ref, probs_ref, wo_ref, acc_in_ref,
         stacked_ref, acc_ref, g_ref, g_half_ref) = refs
        half = g_half_ref.shape[0]
        g_ref[rows_at(core, half)] = mine_ref[...]
        g_ref[rows_at(1 - core, half)] = other_ref[...]
    g_half_ref[...] = g_ref[rows_at(core, half)]
    grad_attend(g_ref[...], qkv_ref, probs_ref, wo_ref, acc_in_ref, stacked_ref, acc_ref, 0)


def backward_b_kernel(first, g_ref, qkv_ref, probs_ref, wo_ref, *refs):
    acc_in_ref = None if first else refs[0]
    stacked_ref, acc_ref = refs[-2:]
    grad_attend(g_ref[...], qkv_ref, probs_ref, wo_ref, acc_in_ref, stacked_ref, acc_ref, 1)


def backward_c_kernel(place_ref, low_ref, high_ref, w_ref, send_ref, keep_ref):
    width = low_ref.shape[2]
    total = None
    for c in range(3):
        for part, ref in enumerate((low_ref, high_ref)):
            term = dot(w_ref[c, :, part * width : (part + 1) * width], ref[c], LAST)
            total = term if total is None else total + term
    split_halves(place_ref[0], total.T, send_ref, keep_ref)


def pair_kernel(first_ref, second_ref, out_ref):
    out_ref[...] = (first_ref[...].astype(F32) + second_ref[...].astype(F32)).astype(BF16)


def up_term_kernel(place_ref, keep_ref, received_ref, x_ref, out_ref):
    residual = place_ref[3].astype(F32)
    total = keep_ref[...] + received_ref[...].astype(F32)
    out_ref[...] = (total + residual * x_ref[...].astype(F32)).astype(BF16)


def down_term_kernel(tick, place_ref, stash_ref, gain_ref, keep_ref, received_ref, g_ref, out_ref):
    half = out_ref.shape[0]
    residual = place_ref[3].astype(F32)
    x = stash_ref[tick, rows_at(place_ref[0], half)].astype(F32)
    inverse = lax.rsqrt(jnp.mean(x * x, axis=-1, keepdims=True) + EPSILON)
    weighted = gain_ref[...] * (keep_ref[...] + received_ref[...].astype(F32))
    mean = jnp.mean(x * weighted, axis=-1, keepdims=True)
    cubed = inverse * inverse * inverse
    back = inverse * weighted - x * cubed * mean
    out_ref[...] = (residual * g_ref[...].astype(F32) + back).astype(BF16)


def choose_kernel(place_ref, own_ref, own_second_ref, first_ref, second_ref, out_ref):
    @pl.when(place_ref[2] == 1)
    def _():
        pair_kernel(own_ref, own_second_ref, out_ref)

    @pl.when(place_ref[2] == 0)
    def _():
        pair_kernel(first_ref, second_ref, out_ref)


def join_kernel(place_ref, mine_ref, other_ref, out_ref):
    core = place_ref[0]
    half = mine_ref.shape[0]
    out_ref[0, rows_at(core, half)] = mine_ref[...]
    out_ref[0, rows_at(1 - core, half)] = other_ref[...]


def table_kernel(buckets_here, low_ref, high_ref, bucket_ref, out_ref):
    heads, tokens, _ = low_ref.shape
    rows = 8
    cells = 2 * heads * rows
    columns = buckets_here * rows
    total = jnp.zeros((cells, columns), F32)
    turned = bucket_ref[...].T
    for i in range(tokens // rows):
        at = slice(i * rows, (i + 1) * rows)
        ids = turned[at]
        hits = jnp.concatenate(
            [(ids == b).astype(F32) for b in range(buckets_here)], axis=0
        ).astype(BF16)
        part = jnp.concatenate(
            [r[:, at, :].reshape(heads * rows, tokens) for r in (low_ref, high_ref)], axis=0
        )
        high = part.astype(BF16)
        low = (part - high.astype(F32)).astype(BF16)
        total += dot(high, hits, LAST) + dot(low, hits, LAST)
    row = lax.broadcasted_iota(jnp.int32, (cells, columns), 0)
    col = lax.broadcasted_iota(jnp.int32, (cells, columns), 1)
    total = jnp.where((row & (rows - 1)) == (col & (rows - 1)), total, 0.0)
    summed = jnp.sum(total.reshape(2 * heads, rows, columns), axis=1)
    spread = lax.broadcasted_iota(jnp.int32, (columns, buckets_here), 0) >> 3
    bucket = lax.broadcasted_iota(jnp.int32, (columns, buckets_here), 1)
    fold = (spread == bucket).astype(F32)
    out_ref[...] = jnp.dot(
        summed, fold, preferred_element_type=F32, precision=lax.Precision.HIGHEST
    )


def shape(dims, dtype=BF16):
    return jax.ShapeDtypeStruct(dims, dtype)


class Chain:
    def __init__(self):
        self.before = None

    def __call__(self, kernel, out_shape, args, scratch=(), scalars=0, after=(), limit=16):
        outs = out_shape if isinstance(out_shape, tuple) else (out_shape,)
        extra = tuple(after) + (() if self.before is None else (self.before,))
        count = len(args)

        def body(*refs):
            kernel(*refs[:count], *refs[count + len(extra) :])

        results = pl.pallas_call(
            body,
            out_shape=outs,
            in_specs=[SCALARS] * scalars + [WHOLE] * (count - scalars) + [UNREAD] * len(extra),
            out_specs=tuple(WHOLE for _ in outs),
            scratch_shapes=list(scratch),
            compiler_params=pltpu.CompilerParams(vmem_limit_bytes=limit * MIB),
            cost_estimate=pl.CostEstimate(flops=0, bytes_accessed=LANES, transcendentals=0),
        )(*args, *extra)
        self.before = results[0]
        return results if isinstance(out_shape, tuple) else results[0]


def in_hbm(x):
    return pltpu.with_memory_space_constraint(x, pltpu.HBM)


def moved(block, step, bit):
    sections, heads = lax.axis_size("section"), lax.axis_size("head")
    route = [
        (s * heads + h, (s + step) * heads + (h ^ bit))
        for s in range(sections)
        if s + step in range(sections)
        for h in range(heads)
    ]
    return lax.ppermute(block, ("section", "head"), route)


def swapped(block, bit):
    return lax.ppermute(block, "head", [(i, i ^ bit) for i in range(lax.axis_size("head"))])


def swapped_in_last(block, bit):
    sections, heads = lax.axis_size("section"), lax.axis_size("head")
    base = (sections - 1) * heads
    return lax.ppermute(
        block, ("section", "head"), [(base + h, base + (h ^ bit)) for h in range(heads)]
    )


def per_device(rising, falling, stash, queue, order, buckets, bias_table, gain, w_qkv, w_out):
    section_index = lax.axis_index("section")
    section_count = lax.axis_size("section")
    head_index = lax.axis_index("head")
    head_count = lax.axis_size("head")
    _, model_width, heads, _, head_dim = w_qkv.shape
    tokens = buckets.shape[0]
    half = tokens // 2
    inner = heads * head_dim
    core = head_index % 2
    is_last = section_index == section_count - 1
    place = jnp.stack([core, section_index, is_last, head_index < 2]).astype(jnp.int32)
    table = bias_table[0].T
    back = w_out[0].reshape(inner, model_width)
    per_mac = 2 * tokens * model_width * inner
    run = Chain()
    bits = [1 << b for b in range(1, head_count.bit_length() - 1)]
    cross = bits[-1]
    qkv_shape = shape((3, tokens, inner))
    scores_shape = shape((heads, tokens, tokens), F32)

    if heads % ROWS16 == 0:
        rows_first = jnp.transpose(w_qkv[0], (0, 2, 1, 3)).reshape(model_width, 3 * heads, head_dim)
        blocks = 4
        depth = model_width // blocks
        fixed = lambda rank: lambda c, b: (0,) * rank
        weights, qkv, bias, wo = pl.pallas_call(
            relayout_kernel,
            grid=(3, blocks),
            out_shape=(
                pltpu.VMEM((3, model_width, inner), BF16),
                qkv_shape,
                scores_shape,
                pltpu.VMEM((inner, model_width), BF16),
            ),
            in_specs=[
                SCALARS,
                pl.BlockSpec((1, tokens, model_width), fixed(3)),
                pl.BlockSpec((1, model_width), fixed(2)),
                pl.BlockSpec(table.shape, fixed(2)),
                pl.BlockSpec((tokens, tokens), fixed(2)),
                pl.BlockSpec((depth, heads, head_dim), lambda c, b: (b, c, 0)),
                UNREAD,
            ],
            out_specs=(
                WHOLE,
                pl.BlockSpec((3, tokens, inner), fixed(3)),
                pl.BlockSpec((heads, tokens, tokens), fixed(3)),
                WHOLE,
            ),
            scratch_shapes=[pltpu.VMEM((tokens, model_width), BF16), pltpu.SemaphoreType.DMA],
            compiler_params=pltpu.CompilerParams(vmem_limit_bytes=24 * MIB),
            cost_estimate=pl.CostEstimate(
                flops=9 * per_mac, bytes_accessed=2 * w_qkv.size, transcendentals=0
            ),
        )(
            place, in_hbm(rising), in_hbm(gain), in_hbm(table), in_hbm(buckets),
            in_hbm(rows_first), in_hbm(back),
        )
        run.before = qkv
    else:
        wo = back
        weights = jnp.transpose(w_qkv[0], (2, 0, 1, 3)).reshape(3, model_width, inner)
        bias = run(bias_kernel, scores_shape, (table, buckets))
        qkv = run(
            stash_kernel,
            qkv_shape,
            (rising, gain, weights),
            scratch=[pltpu.VMEM((tokens, model_width), BF16)],
        )
    halves = (shape((half, model_width)), shape((half, model_width), F32))
    half_rows = shape((half, model_width))
    acc_shape = shape((heads // 2, tokens, tokens), F32)
    part_shape = shape((tokens, inner // 2))
    stacked_shape = shape((3, tokens, inner // 2))
    row_scratch = pltpu.VMEM((tokens, model_width), BF16)

    def but_last_bit(term):
        for bit in bits[:-1]:
            term = run(pair_kernel, half_rows, (term, swapped(term, bit)))
        return term

    def down_term(tick, keep, received, g_half):
        term = run(
            functools.partial(down_term_kernel, tick),
            half_rows,
            (place, stash[0], gain, keep, received, g_half),
            scalars=1,
        )
        return but_last_bit(term)

    stashed = arrivals = None
    acc = ()
    for t in range(TICKS):
        final = t + 1 == TICKS
        if t == 0:
            full, x_half = run(
                first_attend_kernel,
                (shape((tokens, inner)), half_rows),
                (place, rising, qkv, bias),
                scalars=1,
            )
            attended = (full,)
        else:
            low, normed, x_half = run(
                functools.partial(forward_a_kernel, t),
                (part_shape, shape((tokens, model_width)), half_rows),
                (place, order, x_mine, x_other, queue, gain, weights, bias),
                scratch=[row_scratch],
                scalars=2,
            )
            fallen = down_term(t - 1, keep, received, g_half)
            arrivals = (up, in_last, moved(fallen, -1, 0), moved(fallen, -1, cross))
            high = run(forward_b_kernel, part_shape, (normed, weights, bias))
            attended = (low, high)
        send, keep = run(
            forward_c_kernel,
            halves,
            (place,) + attended + (wo,),
            scratch=[pltpu.VMEM((tokens, inner), BF16)],
            scalars=1,
        )
        received = swapped(send, 1)
        if t == 0:
            stashed = run(
                stash_kernel,
                (qkv_shape,) * TICKS,
                (stash[0], gain, weights),
                scratch=[pltpu.VMEM((TICKS * tokens, model_width), BF16)],
            )
        else:
            probs = run(probs_kernel, scores_shape, (stashed[t], bias))
        up = but_last_bit(
            run(up_term_kernel, half_rows, (place, keep, received, x_half), scalars=1)
        )
        if final:
            climbed = (up, swapped(up, cross))
        else:
            climbed = (moved(up, 1, 0), moved(up, 1, cross))
            in_last = swapped_in_last(up, cross)
        if t == 0:
            probs = run(probs_kernel, scores_shape, (stashed[t], bias))
            g_parts = (falling[0],)
        else:
            g_mine = run(choose_kernel, half_rows, (place,) + arrivals, scalars=1)
            g_parts = (g_mine, swapped(g_mine, 1))

        stacked_low, acc_low, g_full, g_half = run(
            functools.partial(backward_a_kernel, t == 0),
            (stacked_shape, acc_shape, shape((tokens, model_width)), half_rows),
            (place,) + g_parts + (stashed[t], probs, wo) + acc[:1],
            scalars=1,
        )
        stacked_high, acc_high = run(
            functools.partial(backward_b_kernel, t == 0),
            (stacked_shape, acc_shape),
            (g_full, stashed[t], probs, wo) + acc[1:],
        )
        acc = (acc_low, acc_high)
        x_mine = run(pair_kernel, half_rows, climbed)
        x_other = swapped(x_mine, 1)
        send, keep = run(
            backward_c_kernel,
            halves,
            (place, stacked_low, stacked_high, weights),
            scalars=1,
        )
        received = swapped(send, 1)

    rows = shape((1, tokens, model_width))
    table_grad = run(
        functools.partial(table_kernel, bias_table.shape[1]),
        shape((heads, bias_table.shape[1]), F32),
        acc + (buckets,),
    )
    fallen = down_term(TICKS - 1, keep, received, g_half)
    fallen_other = swapped(fallen, cross)
    rising_out = run(join_kernel, rows, (place, x_mine, x_other), scalars=1)
    lowered = run(pair_kernel, half_rows, (fallen, fallen_other))
    falling_out = run(join_kernel, rows, (place, lowered, swapped(lowered, 1)), scalars=1)
    return (rising_out, falling_out, table_grad.T[None])


def solution(mesh):
    return jax.shard_map(
        per_device,
        mesh=mesh,
        in_specs=(
            P(("groups", "section"), None, None),
            P(("groups", "section"), None, None),
            P(("groups", "section"), None, None, None),
            P("groups", None, None),
            P("groups"),
            P(),
            P("section", None, "head"),
            P("section", None),
            P("section", None, "head", None, None),
            P("section", "head", None, None),
        ),
        out_specs=(
            P(("groups", "section"), None, None),
            P(("groups", "section"), None, None),
            P(("groups", "section"), None, "head"),
        ),
        check_vma=False,
    )
```

```python
import functools

import jax
import jax.numpy as jnp
from jax import lax
from jax.experimental import pallas as pl
from jax.experimental.pallas import tpu as pltpu
from jax.sharding import PartitionSpec as P

TICKS = 3
EPSILON = 1e-06
LANES = 128
ROWS16 = 16
LAST = (((1,), (1,)), ((), ()))
FIRST = (((0,), (0,)), ((), ()))
F32 = jnp.float32
BF16 = jnp.bfloat16
WHOLE = pl.BlockSpec(memory_space=pltpu.VMEM)
SCALARS = pl.BlockSpec(memory_space=pltpu.SMEM)
UNREAD = pl.BlockSpec(memory_space=pl.ANY)
MIB = 1 << 20


def dot(a, b, dims=None):
    if dims is None:
        return jnp.dot(a, b, preferred_element_type=F32)
    return lax.dot_general(a, b, dims, preferred_element_type=F32)


def rms_normed(rows, gain_row):
    x = rows.astype(F32)
    inverse = lax.rsqrt(jnp.mean(x * x, axis=-1, keepdims=True) + EPSILON)
    return (x * inverse * gain_row).astype(BF16)


def rows_at(index, size):
    return pl.ds(pl.multiple_of(index * size, size), size)


def fill_bias(table_ref, bucket_ref, bias_ref):
    ids = bucket_ref[...].T
    rows, count = table_ref.shape
    table = jnp.concatenate([table_ref[...], jnp.zeros((rows, LANES - count), F32)], axis=1)
    for h in range(rows):
        row = jnp.broadcast_to(table[h : h + 1], ids.shape)
        bias_ref[h] = jnp.take_along_axis(row, ids, axis=1)


def bias_kernel(table_ref, bucket_ref, bias_ref):
    fill_bias(table_ref, bucket_ref, bias_ref)


def relayout_kernel(
    place_ref, x_ref, kept_ref, gain_ref, table_ref, bucket_ref, w_ref, back_ref,
    w_out_ref, qkv_ref, kept_qkv_ref, bias_ref, back_out_ref, normed, arrived,
):
    which = pl.program_id(0)
    block = pl.program_id(1)
    back_copy = pltpu.make_async_copy(back_ref, back_out_ref, arrived)

    @pl.when((which == 0) & (block == 0))
    def _():
        back_copy.start()
        tokens = x_ref.shape[1]
        normed[:tokens] = rms_normed(x_ref[0], gain_ref[...])
        normed[tokens:] = rms_normed(kept_ref[0, 0], gain_ref[...])
        fill_bias(table_ref, bucket_ref, bias_ref)

    depth = w_ref.shape[0]
    size = ROWS16 * ROWS16
    row = lax.broadcasted_iota(jnp.int32, (size, size), 0)
    col = lax.broadcasted_iota(jnp.int32, (size, size), 1)
    wanted = (row & (ROWS16 - 1)) * ROWS16 + (row >> 4)
    permute = (col == wanted).astype(F32).astype(BF16)

    def step(i, carry):
        d0 = pl.multiple_of(i * 2 * ROWS16, 2 * ROWS16)
        first = w_ref[pl.ds(d0, ROWS16)].reshape(size, LANES)
        second = w_ref[pl.ds(d0 + ROWS16, ROWS16)].reshape(size, LANES)
        moved = dot(permute, jnp.concatenate([first, second], axis=1)).astype(BF16)
        to = pl.multiple_of(block * depth + d0, 2 * ROWS16)
        for h in range(ROWS16):
            piece = moved[h * ROWS16 : (h + 1) * ROWS16]
            lanes = slice(h * LANES, (h + 1) * LANES)
            w_out_ref[which, pl.ds(to, ROWS16), lanes] = piece[:, :LANES]
            w_out_ref[which, pl.ds(to + ROWS16, ROWS16), lanes] = piece[:, LANES:]
        return carry

    lax.fori_loop(0, depth // (2 * ROWS16), step, 0, unroll=16)

    @pl.when(block == pl.num_programs(1) - 1)
    def _():
        tokens = x_ref.shape[1]
        out = dot(normed[...], w_out_ref[which]).astype(BF16)
        qkv_ref[which] = out[:tokens]
        kept_qkv_ref[which] = out[tokens:]

    @pl.when((which == pl.num_programs(0) - 1) & (block == pl.num_programs(1) - 1))
    def _():
        back_copy.wait()


def probs_of(query, key, bias, scale):
    scores = dot(key, query, LAST) * scale + bias
    raised = jnp.exp(scores - jnp.max(scores, axis=0, keepdims=True))
    return raised * (1.0 / jnp.sum(raised, axis=0, keepdims=True))


def attend(query, key, value, bias_ref, heads, first_head):
    scale = LANES ** (-0.5)
    lanes = [slice(h * LANES, (h + 1) * LANES) for h in range(heads)]
    probs = [
        probs_of(query[:, sl], key[:, sl], bias_ref[first_head + h], scale).astype(BF16)
        for h, sl in enumerate(lanes)
    ]
    return [dot(p, value[:, sl], FIRST).astype(BF16) for p, sl in zip(probs, lanes)]


def forward_kernel(tick, place_ref, *refs):
    if tick == 0:
        x_in_ref, qkv_ref, bias_ref, wo_ref, send_ref, keep_ref, x_half_ref, attended = refs
    else:
        (order_ref, mine_ref, other_ref, queue_ref, gain_ref, w_ref, bias_ref, wo_ref,
         send_ref, keep_ref, x_half_ref, attended, x_ref) = refs
    core = place_ref[0]
    half = send_ref.shape[0]
    heads = bias_ref.shape[0]
    group = heads // 2
    if tick == 0:
        x_half_ref[...] = x_in_ref[0, rows_at(core, half)]
    else:
        x_ref[rows_at(core, half)] = mine_ref[...]
        x_ref[rows_at(1 - core, half)] = other_ref[...]

        @pl.when(place_ref[1] == 0)
        def _():
            x_ref[...] = queue_ref[order_ref[tick - 1]]

        x_half_ref[...] = x_ref[rows_at(core, half)]
        normed = rms_normed(x_ref[...], gain_ref[...])
    for part in range(2):
        at = slice(part * group * LANES, (part + 1) * group * LANES)
        if tick == 0:
            query, key, value = (qkv_ref[c, :, at] for c in range(3))
        else:
            query, key, value = (dot(normed, w_ref[c, :, at]).astype(BF16) for c in range(3))
        outs = attend(query, key, value, bias_ref, group, part * group)
        for h, out in enumerate(outs):
            first = (part * group + h) * LANES
            attended[:, first : first + LANES] = out
    split_halves(core, dot(attended[...], wo_ref[...]), send_ref, keep_ref)


def split_halves(core, total, send_ref, keep_ref):
    half = send_ref.shape[0]

    @pl.when(core == 0)
    def _():
        send_ref[...] = total[half:].astype(BF16)
        keep_ref[...] = total[:half]

    @pl.when(core != 0)
    def _():
        send_ref[...] = total[:half].astype(BF16)
        keep_ref[...] = total[half:]


def stash_kernel(skipped, x_ref, gain_ref, w_ref, *refs):
    *outs, normed = refs
    ticks, tokens = len(outs), x_ref.shape[1]
    for t in range(ticks):
        normed[t * tokens : (t + 1) * tokens] = rms_normed(x_ref[skipped + t], gain_ref[...])
    width = min(512, w_ref.shape[2])

    def step(i, carry):
        at = rows_at(i, width)
        for c in range(3):
            out = dot(normed[...], w_ref[c, :, at]).astype(BF16)
            for t in range(ticks):
                outs[t][c, :, at] = out[t * tokens : (t + 1) * tokens]
        return carry

    lax.fori_loop(0, w_ref.shape[2] // width, step, 0)


def probs_kernel(qkv_ref, bias_ref, out_ref):
    heads = bias_ref.shape[0]
    group = heads // 2
    scale = LANES ** (-0.5)

    def step(g, carry):
        at = rows_at(g, group * LANES)
        query, key = (qkv_ref[c, :, at] for c in range(2))
        for h in range(group):
            sl = slice(h * LANES, (h + 1) * LANES)
            out_ref[g * group + h] = probs_of(
                query[:, sl], key[:, sl], bias_ref[g * group + h], scale
            )
        return carry

    lax.fori_loop(0, 2, step, 0)


def grad_attend(g, qkv_ref, probs_ref, wo_ref, acc_in_ref, stacked, acc_ref, part):
    heads = probs_ref.shape[0] // 2
    scale = LANES ** (-0.5)
    at = slice(part * heads * LANES, (part + 1) * heads * LANES)
    grad_attn = dot(g, wo_ref[at], LAST).astype(BF16)
    for local in range(heads):
        h = part * heads + local
        own = slice(h * LANES, (h + 1) * LANES)
        q, k, v = (qkv_ref[c, :, own] for c in range(3))
        ga = grad_attn[:, local * LANES : (local + 1) * LANES]
        probs = probs_ref[h]
        grad_probs = dot(v, ga, LAST)
        total = jnp.sum(probs * grad_probs, axis=0, keepdims=True)
        grad_scores = probs * (grad_probs - total)
        grad16 = grad_scores.astype(BF16)
        if acc_in_ref is None:
            acc_ref[h] = grad_scores
        else:
            acc_ref[h] = acc_in_ref[h] + grad_scores
        stacked[0, :, own] = (dot(grad16, k, FIRST) * scale).astype(BF16)
        stacked[1, :, own] = (dot(grad16, q) * scale).astype(BF16)
        stacked[2, :, own] = dot(probs.astype(BF16), ga).astype(BF16)


def backward_kernel(first, place_ref, *refs):
    core = place_ref[0]
    if first:
        full_ref, qkv_ref, probs_ref, w_ref, wo_ref, *refs = refs
        send_ref, keep_ref, acc_ref, g_half_ref, stacked, g_ref = refs
        acc_in_ref = None
        g_ref[...] = full_ref[...]
    else:
        mine_ref, other_ref, qkv_ref, probs_ref, w_ref, wo_ref, acc_in_ref, *refs = refs
        send_ref, keep_ref, acc_ref, g_half_ref, stacked, g_ref = refs
        half = g_half_ref.shape[0]
        g_ref[rows_at(core, half)] = mine_ref[...]
        g_ref[rows_at(1 - core, half)] = other_ref[...]
    g_half_ref[...] = g_ref[rows_at(core, g_half_ref.shape[0])]
    for part in range(2):
        grad_attend(g_ref[...], qkv_ref, probs_ref, wo_ref, acc_in_ref, stacked, acc_ref, part)
    total = dot(w_ref[0], stacked[0], LAST)
    total += dot(w_ref[1], stacked[1], LAST)
    total += dot(w_ref[2], stacked[2], LAST)
    split_halves(core, total.T, send_ref, keep_ref)


def pair_kernel(first_ref, second_ref, out_ref):
    out_ref[...] = (first_ref[...].astype(F32) + second_ref[...].astype(F32)).astype(BF16)


def up_term_kernel(place_ref, keep_ref, received_ref, x_ref, out_ref):
    residual = place_ref[3].astype(F32)
    total = keep_ref[...] + received_ref[...].astype(F32)
    out_ref[...] = (total + residual * x_ref[...].astype(F32)).astype(BF16)


def down_term_kernel(tick, place_ref, stash_ref, gain_ref, keep_ref, received_ref, g_ref, out_ref):
    half = out_ref.shape[0]
    residual = place_ref[3].astype(F32)
    x = stash_ref[tick, rows_at(place_ref[0], half)].astype(F32)
    inverse = lax.rsqrt(jnp.mean(x * x, axis=-1, keepdims=True) + EPSILON)
    weighted = gain_ref[...] * (keep_ref[...] + received_ref[...].astype(F32))
    mean = jnp.mean(x * weighted, axis=-1, keepdims=True)
    cubed = inverse * inverse * inverse
    back = inverse * weighted - x * cubed * mean
    out_ref[...] = (residual * g_ref[...].astype(F32) + back).astype(BF16)


def choose_kernel(place_ref, own_ref, own_second_ref, first_ref, second_ref, out_ref):
    @pl.when(place_ref[2] == 1)
    def _():
        pair_kernel(own_ref, own_second_ref, out_ref)

    @pl.when(place_ref[2] == 0)
    def _():
        pair_kernel(first_ref, second_ref, out_ref)


def join_kernel(place_ref, mine_ref, other_ref, out_ref):
    core = place_ref[0]
    half = mine_ref.shape[0]
    out_ref[0, rows_at(core, half)] = mine_ref[...]
    out_ref[0, rows_at(1 - core, half)] = other_ref[...]


def table_kernel(buckets_here, acc_ref, bucket_ref, out_ref):
    heads, tokens, _ = acc_ref.shape
    rows = 8
    cells = heads * rows
    columns = buckets_here * rows
    total = jnp.zeros((cells, columns), F32)
    turned = bucket_ref[...].T
    for i in range(tokens // rows):
        at = slice(i * rows, (i + 1) * rows)
        ids = turned[at]
        hits = jnp.concatenate(
            [(ids == b).astype(F32) for b in range(buckets_here)], axis=0
        ).astype(BF16)
        part = acc_ref[:, at, :].reshape(cells, tokens)
        high = part.astype(BF16)
        low = (part - high.astype(F32)).astype(BF16)
        total += dot(high, hits, LAST) + dot(low, hits, LAST)
    row = lax.broadcasted_iota(jnp.int32, (cells, columns), 0)
    col = lax.broadcasted_iota(jnp.int32, (cells, columns), 1)
    total = jnp.where((row & (rows - 1)) == (col & (rows - 1)), total, 0.0)
    summed = jnp.sum(total.reshape(heads, rows, columns), axis=1)
    spread = lax.broadcasted_iota(jnp.int32, (columns, buckets_here), 0) >> 3
    bucket = lax.broadcasted_iota(jnp.int32, (columns, buckets_here), 1)
    fold = (spread == bucket).astype(F32)
    out_ref[...] = jnp.dot(
        summed, fold, preferred_element_type=F32, precision=lax.Precision.HIGHEST
    )


def shape(dims, dtype=BF16):
    return jax.ShapeDtypeStruct(dims, dtype)


class Chain:
    def __init__(self):
        self.before = None

    def __call__(self, kernel, out_shape, args, scratch=(), scalars=0, after=(), limit=16):
        outs = out_shape if isinstance(out_shape, tuple) else (out_shape,)
        extra = tuple(after) + (() if self.before is None else (self.before,))
        count = len(args)

        def body(*refs):
            kernel(*refs[:count], *refs[count + len(extra) :])

        results = pl.pallas_call(
            body,
            out_shape=outs,
            in_specs=[SCALARS] * scalars + [WHOLE] * (count - scalars) + [UNREAD] * len(extra),
            out_specs=tuple(WHOLE for _ in outs),
            scratch_shapes=list(scratch),
            compiler_params=pltpu.CompilerParams(vmem_limit_bytes=limit * MIB),
            cost_estimate=pl.CostEstimate(flops=0, bytes_accessed=LANES, transcendentals=0),
        )(*args, *extra)
        self.before = results[0]
        return results if isinstance(out_shape, tuple) else results[0]


def in_hbm(x):
    return pltpu.with_memory_space_constraint(x, pltpu.HBM)


def moved(block, step, bit):
    sections, heads = lax.axis_size("section"), lax.axis_size("head")
    route = [
        (s * heads + h, (s + step) * heads + (h ^ bit))
        for s in range(sections)
        if s + step in range(sections)
        for h in range(heads)
    ]
    return lax.ppermute(block, ("section", "head"), route)


def swapped(block, bit):
    return lax.ppermute(block, "head", [(i, i ^ bit) for i in range(lax.axis_size("head"))])


def swapped_in_last(block, bit):
    sections, heads = lax.axis_size("section"), lax.axis_size("head")
    base = (sections - 1) * heads
    return lax.ppermute(
        block, ("section", "head"), [(base + h, base + (h ^ bit)) for h in range(heads)]
    )


def per_device(rising, falling, stash, queue, order, buckets, bias_table, gain, w_qkv, w_out):
    section_index = lax.axis_index("section")
    section_count = lax.axis_size("section")
    head_index = lax.axis_index("head")
    head_count = lax.axis_size("head")
    _, model_width, heads, _, head_dim = w_qkv.shape
    tokens = buckets.shape[0]
    half = tokens // 2
    inner = heads * head_dim
    core = head_index % 2
    is_last = section_index == section_count - 1
    place = jnp.stack([core, section_index, is_last, head_index < 2]).astype(jnp.int32)
    table = bias_table[0].T
    back = w_out[0].reshape(inner, model_width)
    run = Chain()
    bits = [1 << b for b in range(1, head_count.bit_length() - 1)]
    cross = bits[-1]
    qkv_shape = shape((3, tokens, inner))
    scores_shape = shape((heads, tokens, tokens), F32)

    if heads % ROWS16 == 0:
        rows_first = jnp.transpose(w_qkv[0], (0, 2, 1, 3)).reshape(model_width, 3 * heads, head_dim)
        blocks = 2
        depth = model_width // blocks
        fixed = lambda rank: lambda c, b: (0,) * rank
        weights, qkv, kept_qkv, bias, wo = pl.pallas_call(
            relayout_kernel,
            grid=(3, blocks),
            out_shape=(
                pltpu.VMEM((3, model_width, inner), BF16),
                qkv_shape,
                qkv_shape,
                scores_shape,
                pltpu.VMEM((inner, model_width), BF16),
            ),
            in_specs=[
                SCALARS,
                pl.BlockSpec((1, tokens, model_width), fixed(3)),
                pl.BlockSpec((1, 1, tokens, model_width), fixed(4)),
                pl.BlockSpec((1, model_width), fixed(2)),
                pl.BlockSpec(table.shape, fixed(2)),
                pl.BlockSpec((tokens, tokens), fixed(2)),
                pl.BlockSpec((depth, heads, head_dim), lambda c, b: (b, c, 0)),
                UNREAD,
            ],
            out_specs=(
                WHOLE,
                pl.BlockSpec((3, tokens, inner), fixed(3)),
                pl.BlockSpec((3, tokens, inner), fixed(3)),
                pl.BlockSpec((heads, tokens, tokens), fixed(3)),
                WHOLE,
            ),
            scratch_shapes=[pltpu.VMEM((2 * tokens, model_width), BF16), pltpu.SemaphoreType.DMA],
            compiler_params=pltpu.CompilerParams(vmem_limit_bytes=24 * MIB),
            cost_estimate=pl.CostEstimate(
                flops=0, bytes_accessed=2 * w_qkv.size, transcendentals=0
            ),
        )(
            place, in_hbm(rising), in_hbm(stash), in_hbm(gain), in_hbm(table), in_hbm(buckets),
            in_hbm(rows_first), in_hbm(back),
        )
        run.before = qkv
    else:
        wo = back
        weights = jnp.transpose(w_qkv[0], (2, 0, 1, 3)).reshape(3, model_width, inner)
        bias = run(bias_kernel, scores_shape, (table, buckets))
        qkv, kept_qkv = (
            run(
                functools.partial(stash_kernel, 0),
                qkv_shape,
                (rows, gain, weights),
                scratch=[pltpu.VMEM((tokens, model_width), BF16)],
            )
            for rows in (rising, stash[0, :1])
        )
    halves = (shape((half, model_width)), shape((half, model_width), F32))
    half_rows = shape((half, model_width))
    row_scratch = pltpu.VMEM((tokens, model_width), BF16)

    def but_last_bit(term):
        for bit in bits[:-1]:
            term = run(pair_kernel, half_rows, (term, swapped(term, bit)))
        return term

    def down_term(tick, keep, received, g_half):
        term = run(
            functools.partial(down_term_kernel, tick),
            half_rows,
            (place, stash[0], gain, keep, received, g_half),
            scalars=1,
        )
        return but_last_bit(term)

    stashed = [kept_qkv]
    acc = ()
    for t in range(TICKS):
        final = t + 1 == TICKS
        scratch = [pltpu.VMEM((tokens, inner), BF16)]
        if t == 0:
            args = (place, rising, qkv, bias, wo)
        else:
            x_other = swapped(x_mine, 1)
            fallen = down_term(t - 1, keep, received, g_half)
            arrivals = (up, in_last, moved(fallen, -1, 0), moved(fallen, -1, cross))
            args = (place, order, x_mine, x_other, queue, gain, weights, bias, wo)
            scratch += [row_scratch]
        up_send, up_keep, x_half = run(
            functools.partial(forward_kernel, t),
            halves + (half_rows,),
            args,
            scratch=scratch,
            scalars=1 if t == 0 else 2,
        )
        up_received = swapped(up_send, 1)
        if t == 1:
            stashed += run(
                functools.partial(stash_kernel, 1),
                (qkv_shape,) * (TICKS - 1),
                (stash[0], gain, weights),
                scratch=[pltpu.VMEM(((TICKS - 1) * tokens, model_width), BF16)],
            )
        if t == 0:
            g_parts = (falling[0],)
        else:
            g_mine = run(choose_kernel, half_rows, (place,) + arrivals, scalars=1)
            g_parts = (g_mine, swapped(g_mine, 1))
        probs = run(probs_kernel, scores_shape, (stashed[t], bias))
        up = but_last_bit(
            run(up_term_kernel, half_rows, (place, up_keep, up_received, x_half), scalars=1)
        )
        if final:
            climbed = (up, swapped(up, cross))
        else:
            climbed = (moved(up, 1, 0), moved(up, 1, cross))
            in_last = swapped_in_last(up, cross)

        send, keep, acc_next, g_half = run(
            functools.partial(backward_kernel, t == 0),
            halves + (scores_shape, half_rows),
            (place,) + g_parts + (stashed[t], probs, weights, wo) + acc,
            scratch=[pltpu.VMEM((3, tokens, inner), BF16), row_scratch],
            scalars=1,
        )
        acc = (acc_next,)
        received = swapped(send, 1)
        x_mine = run(pair_kernel, half_rows, climbed)

    x_other = swapped(x_mine, 1)
    rows = shape((1, tokens, model_width))
    table_grad = run(
        functools.partial(table_kernel, bias_table.shape[1]),
        shape((heads, bias_table.shape[1]), F32),
        acc + (buckets,),
    )
    fallen = down_term(TICKS - 1, keep, received, g_half)
    fallen_other = swapped(fallen, cross)
    rising_out = run(join_kernel, rows, (place, x_mine, x_other), scalars=1)
    lowered = run(pair_kernel, half_rows, (fallen, fallen_other))
    falling_out = run(join_kernel, rows, (place, lowered, swapped(lowered, 1)), scalars=1)
    return (rising_out, falling_out, table_grad.T[None])


def solution(mesh):
    return jax.shard_map(
        per_device,
        mesh=mesh,
        in_specs=(
            P(("groups", "section"), None, None),
            P(("groups", "section"), None, None),
            P(("groups", "section"), None, None, None),
            P("groups", None, None),
            P("groups"),
            P(),
            P("section", None, "head"),
            P("section", None),
            P("section", None, "head", None, None),
            P("section", "head", None, None),
        ),
        out_specs=(
            P(("groups", "section"), None, None),
            P(("groups", "section"), None, None),
            P(("groups", "section"), None, "head"),
        ),
        check_vma=False,
    )
```

```python
import functools

import jax
import jax.numpy as jnp
from jax import lax
from jax.experimental import pallas as pl
from jax.experimental.pallas import tpu as pltpu
from jax.sharding import PartitionSpec as P

TICKS = 3
EPSILON = 1e-06
LANES = 128
ROWS16 = 16
LAST = (((1,), (1,)), ((), ()))
FIRST = (((0,), (0,)), ((), ()))
F32 = jnp.float32
BF16 = jnp.bfloat16
WHOLE = pl.BlockSpec(memory_space=pltpu.VMEM)
SCALARS = pl.BlockSpec(memory_space=pltpu.SMEM)
UNREAD = pl.BlockSpec(memory_space=pl.ANY)
MIB = 1 << 20


def dot(a, b, dims=None):
    if dims is None:
        return jnp.dot(a, b, preferred_element_type=F32)
    return lax.dot_general(a, b, dims, preferred_element_type=F32)


def rms_normed(rows, gain_row):
    x = rows.astype(F32)
    inverse = lax.rsqrt(jnp.mean(x * x, axis=-1, keepdims=True) + EPSILON)
    return (x * inverse * gain_row).astype(BF16)


def rows_at(index, size):
    return pl.ds(pl.multiple_of(index * size, size), size)


def fill_bias(table_ref, bucket_ref, bias_ref):
    ids = bucket_ref[...].T
    rows, count = table_ref.shape
    table = jnp.concatenate([table_ref[...], jnp.zeros((rows, LANES - count), F32)], axis=1)
    for h in range(rows):
        row = jnp.broadcast_to(table[h : h + 1], ids.shape)
        bias_ref[h] = jnp.take_along_axis(row, ids, axis=1)


def bias_kernel(table_ref, bucket_ref, bias_ref):
    fill_bias(table_ref, bucket_ref, bias_ref)


def relayout_kernel(
    place_ref, x_ref, kept_ref, gain_ref, table_ref, bucket_ref, w_ref, back_ref,
    w_out_ref, qkv_ref, kept_qkv_ref, bias_ref, back_out_ref, normed, arrived,
):
    which = pl.program_id(0)
    block = pl.program_id(1)
    back_copy = pltpu.make_async_copy(back_ref, back_out_ref, arrived)

    @pl.when((which == 0) & (block == 0))
    def _():
        back_copy.start()
        tokens = x_ref.shape[1]
        normed[:tokens] = rms_normed(x_ref[0], gain_ref[...])
        normed[tokens:] = rms_normed(kept_ref[0, 0], gain_ref[...])
        fill_bias(table_ref, bucket_ref, bias_ref)

    depth = w_ref.shape[0]
    size = ROWS16 * ROWS16
    row = lax.broadcasted_iota(jnp.int32, (size, size), 0)
    col = lax.broadcasted_iota(jnp.int32, (size, size), 1)
    wanted = (row & (ROWS16 - 1)) * ROWS16 + (row >> 4)
    permute = (col == wanted).astype(F32).astype(BF16)

    def step(i, carry):
        d0 = pl.multiple_of(i * 2 * ROWS16, 2 * ROWS16)
        first = w_ref[pl.ds(d0, ROWS16)].reshape(size, LANES)
        second = w_ref[pl.ds(d0 + ROWS16, ROWS16)].reshape(size, LANES)
        moved = dot(permute, jnp.concatenate([first, second], axis=1)).astype(BF16)
        to = pl.multiple_of(block * depth + d0, 2 * ROWS16)
        for h in range(ROWS16):
            piece = moved[h * ROWS16 : (h + 1) * ROWS16]
            lanes = slice(h * LANES, (h + 1) * LANES)
            w_out_ref[which, pl.ds(to, ROWS16), lanes] = piece[:, :LANES]
            w_out_ref[which, pl.ds(to + ROWS16, ROWS16), lanes] = piece[:, LANES:]
        return carry

    lax.fori_loop(0, depth // (2 * ROWS16), step, 0, unroll=16)

    @pl.when(block == pl.num_programs(1) - 1)
    def _():
        tokens = x_ref.shape[1]
        out = dot(normed[...], w_out_ref[which]).astype(BF16)
        qkv_ref[which] = out[:tokens]
        kept_qkv_ref[which] = out[tokens:]

    @pl.when((which == pl.num_programs(0) - 1) & (block == pl.num_programs(1) - 1))
    def _():
        back_copy.wait()


def probs_of(query, key, bias, scale):
    scores = dot(key, query, LAST) * scale + bias
    raised = jnp.exp(scores - jnp.max(scores, axis=0, keepdims=True))
    return raised * (1.0 / jnp.sum(raised, axis=0, keepdims=True))


def attend(query, key, value, bias_ref, heads, first_head):
    scale = LANES ** (-0.5)
    lanes = [slice(h * LANES, (h + 1) * LANES) for h in range(heads)]
    probs = [
        probs_of(query[:, sl], key[:, sl], bias_ref[first_head + h], scale).astype(BF16)
        for h, sl in enumerate(lanes)
    ]
    return [dot(p, value[:, sl], FIRST).astype(BF16) for p, sl in zip(probs, lanes)]


def forward_kernel(tick, place_ref, *refs):
    if tick == 0:
        x_in_ref, qkv_ref, bias_ref, wo_ref, send_ref, keep_ref, x_half_ref, attended = refs
    else:
        (order_ref, mine_ref, other_ref, queue_ref, gain_ref, w_ref, bias_ref, wo_ref,
         send_ref, keep_ref, x_half_ref, attended, x_ref) = refs
    core = place_ref[0]
    half = send_ref.shape[0]
    heads = bias_ref.shape[0]
    group = heads // 2
    if tick == 0:
        x_half_ref[...] = x_in_ref[0, rows_at(core, half)]
    else:
        x_ref[rows_at(core, half)] = mine_ref[...]
        x_ref[rows_at(1 - core, half)] = other_ref[...]

        @pl.when(place_ref[1] == 0)
        def _():
            x_ref[...] = queue_ref[order_ref[tick - 1]]

        x_half_ref[...] = x_ref[rows_at(core, half)]
        normed = rms_normed(x_ref[...], gain_ref[...])
    for part in range(2):
        at = slice(part * group * LANES, (part + 1) * group * LANES)
        if tick == 0:
            query, key, value = (qkv_ref[c, :, at] for c in range(3))
        else:
            query, key, value = (dot(normed, w_ref[c, :, at]).astype(BF16) for c in range(3))
        outs = attend(query, key, value, bias_ref, group, part * group)
        for h, out in enumerate(outs):
            first = (part * group + h) * LANES
            attended[:, first : first + LANES] = out
    split_halves(core, dot(attended[...], wo_ref[...]), send_ref, keep_ref)


def split_halves(core, total, send_ref, keep_ref):
    half = send_ref.shape[0]

    @pl.when(core == 0)
    def _():
        send_ref[...] = total[half:].astype(BF16)
        keep_ref[...] = total[:half]

    @pl.when(core != 0)
    def _():
        send_ref[...] = total[:half].astype(BF16)
        keep_ref[...] = total[half:]


def stash_kernel(skipped, x_ref, gain_ref, w_ref, *refs):
    *outs, normed = refs
    ticks, tokens = len(outs), x_ref.shape[1]
    for t in range(ticks):
        normed[t * tokens : (t + 1) * tokens] = rms_normed(x_ref[skipped + t], gain_ref[...])
    width = min(512, w_ref.shape[2])

    def step(i, carry):
        at = rows_at(i, width)
        for c in range(3):
            out = dot(normed[...], w_ref[c, :, at]).astype(BF16)
            for t in range(ticks):
                outs[t][c, :, at] = out[t * tokens : (t + 1) * tokens]
        return carry

    lax.fori_loop(0, w_ref.shape[2] // width, step, 0)


def probs_kernel(qkv_ref, bias_ref, out_ref):
    heads = bias_ref.shape[0]
    group = heads // 2
    scale = LANES ** (-0.5)

    def step(g, carry):
        at = rows_at(g, group * LANES)
        query, key = (qkv_ref[c, :, at] for c in range(2))
        for h in range(group):
            sl = slice(h * LANES, (h + 1) * LANES)
            out_ref[g * group + h] = probs_of(
                query[:, sl], key[:, sl], bias_ref[g * group + h], scale
            )
        return carry

    lax.fori_loop(0, 2, step, 0)


def grad_attend(g, qkv_ref, probs_ref, wo_ref, acc_in_ref, stacked, acc_ref, part):
    heads = probs_ref.shape[0] // 2
    scale = LANES ** (-0.5)
    at = slice(part * heads * LANES, (part + 1) * heads * LANES)
    grad_attn = dot(g, wo_ref[at], LAST).astype(BF16)
    for local in range(heads):
        h = part * heads + local
        own = slice(h * LANES, (h + 1) * LANES)
        q, k, v = (qkv_ref[c, :, own] for c in range(3))
        ga = grad_attn[:, local * LANES : (local + 1) * LANES]
        probs = probs_ref[h]
        grad_probs = dot(v, ga, LAST)
        total = jnp.sum(probs * grad_probs, axis=0, keepdims=True)
        grad_scores = probs * (grad_probs - total)
        grad16 = grad_scores.astype(BF16)
        if acc_in_ref is None:
            acc_ref[h] = grad_scores
        else:
            acc_ref[h] = acc_in_ref[h] + grad_scores
        stacked[0, :, own] = (dot(grad16, k, FIRST) * scale).astype(BF16)
        stacked[1, :, own] = (dot(grad16, q) * scale).astype(BF16)
        stacked[2, :, own] = dot(probs.astype(BF16), ga).astype(BF16)


def backward_kernel(first, place_ref, *refs):
    core = place_ref[0]
    if first:
        full_ref, qkv_ref, probs_ref, w_ref, wo_ref, *refs = refs
        send_ref, keep_ref, acc_ref, g_half_ref, stacked, g_ref = refs
        acc_in_ref = None
        g_ref[...] = full_ref[...]
    else:
        mine_ref, other_ref, qkv_ref, probs_ref, w_ref, wo_ref, acc_in_ref, *refs = refs
        send_ref, keep_ref, acc_ref, g_half_ref, stacked, g_ref = refs
        half = g_half_ref.shape[0]
        g_ref[rows_at(core, half)] = mine_ref[...]
        g_ref[rows_at(1 - core, half)] = other_ref[...]
    g_half_ref[...] = g_ref[rows_at(core, g_half_ref.shape[0])]
    for part in range(2):
        grad_attend(g_ref[...], qkv_ref, probs_ref, wo_ref, acc_in_ref, stacked, acc_ref, part)
    total = dot(w_ref[0], stacked[0], LAST)
    total += dot(w_ref[1], stacked[1], LAST)
    total += dot(w_ref[2], stacked[2], LAST)
    split_halves(core, total.T, send_ref, keep_ref)


def pair_kernel(first_ref, second_ref, out_ref):
    out_ref[...] = (first_ref[...].astype(F32) + second_ref[...].astype(F32)).astype(BF16)


def up_term_kernel(place_ref, keep_ref, received_ref, x_ref, out_ref):
    residual = place_ref[3].astype(F32)
    total = keep_ref[...] + received_ref[...].astype(F32)
    out_ref[...] = (total + residual * x_ref[...].astype(F32)).astype(BF16)


def down_term_kernel(tick, place_ref, stash_ref, gain_ref, keep_ref, received_ref, g_ref, out_ref):
    half = out_ref.shape[0]
    residual = place_ref[3].astype(F32)
    x = stash_ref[tick, rows_at(place_ref[0], half)].astype(F32)
    inverse = lax.rsqrt(jnp.mean(x * x, axis=-1, keepdims=True) + EPSILON)
    weighted = gain_ref[...] * (keep_ref[...] + received_ref[...].astype(F32))
    mean = jnp.mean(x * weighted, axis=-1, keepdims=True)
    cubed = inverse * inverse * inverse
    back = inverse * weighted - x * cubed * mean
    out_ref[...] = (residual * g_ref[...].astype(F32) + back).astype(BF16)


def choose_kernel(place_ref, own_ref, own_second_ref, first_ref, second_ref, out_ref):
    @pl.when(place_ref[2] == 1)
    def _():
        pair_kernel(own_ref, own_second_ref, out_ref)

    @pl.when(place_ref[2] == 0)
    def _():
        pair_kernel(first_ref, second_ref, out_ref)


def join_kernel(place_ref, mine_ref, other_ref, out_ref):
    core = place_ref[0]
    half = mine_ref.shape[0]
    out_ref[0, rows_at(core, half)] = mine_ref[...]
    out_ref[0, rows_at(1 - core, half)] = other_ref[...]


def table_kernel(buckets_here, acc_ref, bucket_ref, out_ref):
    heads, tokens, _ = acc_ref.shape
    rows = 8
    cells = heads * rows
    columns = buckets_here * rows
    total = jnp.zeros((cells, columns), F32)
    turned = bucket_ref[...].T
    for i in range(tokens // rows):
        at = slice(i * rows, (i + 1) * rows)
        ids = turned[at]
        hits = jnp.concatenate(
            [(ids == b).astype(F32) for b in range(buckets_here)], axis=0
        ).astype(BF16)
        part = acc_ref[:, at, :].reshape(cells, tokens)
        high = part.astype(BF16)
        low = (part - high.astype(F32)).astype(BF16)
        total += dot(high, hits, LAST) + dot(low, hits, LAST)
    row = lax.broadcasted_iota(jnp.int32, (cells, columns), 0)
    col = lax.broadcasted_iota(jnp.int32, (cells, columns), 1)
    total = jnp.where((row & (rows - 1)) == (col & (rows - 1)), total, 0.0)
    summed = jnp.sum(total.reshape(heads, rows, columns), axis=1)
    spread = lax.broadcasted_iota(jnp.int32, (columns, buckets_here), 0) >> 3
    bucket = lax.broadcasted_iota(jnp.int32, (columns, buckets_here), 1)
    fold = (spread == bucket).astype(F32)
    out_ref[...] = jnp.dot(
        summed, fold, preferred_element_type=F32, precision=lax.Precision.HIGHEST
    )


def shape(dims, dtype=BF16):
    return jax.ShapeDtypeStruct(dims, dtype)


class Chain:
    def __init__(self):
        self.before = None

    def __call__(self, kernel, out_shape, args, scratch=(), scalars=0, after=(), limit=16):
        outs = out_shape if isinstance(out_shape, tuple) else (out_shape,)
        extra = tuple(after) + (() if self.before is None else (self.before,))
        count = len(args)

        def body(*refs):
            kernel(*refs[:count], *refs[count + len(extra) :])

        results = pl.pallas_call(
            body,
            out_shape=outs,
            in_specs=[SCALARS] * scalars + [WHOLE] * (count - scalars) + [UNREAD] * len(extra),
            out_specs=tuple(WHOLE for _ in outs),
            scratch_shapes=list(scratch),
            compiler_params=pltpu.CompilerParams(vmem_limit_bytes=limit * MIB),
            cost_estimate=pl.CostEstimate(flops=0, bytes_accessed=LANES, transcendentals=0),
        )(*args, *extra)
        self.before = results[0]
        return results if isinstance(out_shape, tuple) else results[0]


def in_hbm(x):
    return pltpu.with_memory_space_constraint(x, pltpu.HBM)


def moved(block, step, bit):
    sections, heads = lax.axis_size("section"), lax.axis_size("head")
    route = [
        (s * heads + h, (s + step) % sections * heads + (h ^ bit))
        for s in range(sections)
        for h in range(heads)
    ]
    return lax.ppermute(block, ("section", "head"), route)


def swapped(block, bit):
    return lax.ppermute(block, "head", [(i, i ^ bit) for i in range(lax.axis_size("head"))])


def per_device(rising, falling, stash, queue, order, buckets, bias_table, gain, w_qkv, w_out):
    section_index = lax.axis_index("section")
    section_count = lax.axis_size("section")
    head_index = lax.axis_index("head")
    head_count = lax.axis_size("head")
    _, model_width, heads, _, head_dim = w_qkv.shape
    tokens = buckets.shape[0]
    half = tokens // 2
    inner = heads * head_dim
    core = head_index % 2
    is_last = section_index == section_count - 1
    place = jnp.stack([core, section_index, is_last, head_index < 2]).astype(jnp.int32)
    table = bias_table[0].T
    back = w_out[0].reshape(inner, model_width)
    run = Chain()
    bits = [1 << b for b in range(1, head_count.bit_length() - 1)]
    cross = bits[-1]
    qkv_shape = shape((3, tokens, inner))
    scores_shape = shape((heads, tokens, tokens), F32)

    if heads % ROWS16 == 0:
        rows_first = jnp.transpose(w_qkv[0], (0, 2, 1, 3)).reshape(model_width, 3 * heads, head_dim)
        blocks = 2
        depth = model_width // blocks
        fixed = lambda rank: lambda c, b: (0,) * rank
        weights, qkv, kept_qkv, bias, wo = pl.pallas_call(
            relayout_kernel,
            grid=(3, blocks),
            out_shape=(
                pltpu.VMEM((3, model_width, inner), BF16),
                qkv_shape,
                qkv_shape,
                scores_shape,
                pltpu.VMEM((inner, model_width), BF16),
            ),
            in_specs=[
                SCALARS,
                pl.BlockSpec((1, tokens, model_width), fixed(3)),
                pl.BlockSpec((1, 1, tokens, model_width), fixed(4)),
                pl.BlockSpec((1, model_width), fixed(2)),
                pl.BlockSpec(table.shape, fixed(2)),
                pl.BlockSpec((tokens, tokens), fixed(2)),
                pl.BlockSpec((depth, heads, head_dim), lambda c, b: (b, c, 0)),
                UNREAD,
            ],
            out_specs=(
                WHOLE,
                pl.BlockSpec((3, tokens, inner), fixed(3)),
                pl.BlockSpec((3, tokens, inner), fixed(3)),
                pl.BlockSpec((heads, tokens, tokens), fixed(3)),
                WHOLE,
            ),
            scratch_shapes=[pltpu.VMEM((2 * tokens, model_width), BF16), pltpu.SemaphoreType.DMA],
            compiler_params=pltpu.CompilerParams(vmem_limit_bytes=24 * MIB),
            cost_estimate=pl.CostEstimate(
                flops=0, bytes_accessed=2 * w_qkv.size, transcendentals=0
            ),
        )(
            place, in_hbm(rising), in_hbm(stash), in_hbm(gain), in_hbm(table), in_hbm(buckets),
            in_hbm(rows_first), in_hbm(back),
        )
        run.before = qkv
    else:
        wo = back
        weights = jnp.transpose(w_qkv[0], (2, 0, 1, 3)).reshape(3, model_width, inner)
        bias = run(bias_kernel, scores_shape, (table, buckets))
        qkv, kept_qkv = (
            run(
                functools.partial(stash_kernel, 0),
                qkv_shape,
                (rows, gain, weights),
                scratch=[pltpu.VMEM((tokens, model_width), BF16)],
            )
            for rows in (rising, stash[0, :1])
        )
    halves = (shape((half, model_width)), shape((half, model_width), F32))
    half_rows = shape((half, model_width))
    row_scratch = pltpu.VMEM((tokens, model_width), BF16)

    def but_last_bit(term):
        for bit in bits[:-1]:
            term = run(pair_kernel, half_rows, (term, swapped(term, bit)))
        return term

    def down_term(tick, keep, received, g_half):
        term = run(
            functools.partial(down_term_kernel, tick),
            half_rows,
            (place, stash[0], gain, keep, received, g_half),
            scalars=1,
        )
        return but_last_bit(term)

    stashed = [kept_qkv]
    acc = ()
    for t in range(TICKS):
        final = t + 1 == TICKS
        scratch = [pltpu.VMEM((tokens, inner), BF16)]
        if t == 0:
            args = (place, rising, qkv, bias, wo)
        else:
            x_other = swapped(x_mine, 1)
            fallen = down_term(t - 1, keep, received, g_half)
            arrivals = (up, in_last, moved(fallen, -1, 0), moved(fallen, -1, cross))
            args = (place, order, x_mine, x_other, queue, gain, weights, bias, wo)
            scratch += [row_scratch]
        up_send, up_keep, x_half = run(
            functools.partial(forward_kernel, t),
            halves + (half_rows,),
            args,
            scratch=scratch,
            scalars=1 if t == 0 else 2,
        )
        up_received = swapped(up_send, 1)
        if t == 1:
            stashed += run(
                functools.partial(stash_kernel, 1),
                (qkv_shape,) * (TICKS - 1),
                (stash[0], gain, weights),
                scratch=[pltpu.VMEM(((TICKS - 1) * tokens, model_width), BF16)],
            )
        if t == 0:
            g_parts = (falling[0],)
        else:
            g_mine = run(choose_kernel, half_rows, (place,) + arrivals, scalars=1)
            g_parts = (g_mine, swapped(g_mine, 1))
        probs = run(probs_kernel, scores_shape, (stashed[t], bias))
        up = but_last_bit(
            run(up_term_kernel, half_rows, (place, up_keep, up_received, x_half), scalars=1)
        )
        if final:
            climbed = (up, swapped(up, cross))
        else:
            climbed = (moved(up, 1, 0), moved(up, 1, cross))
            in_last = swapped(up, cross)

        send, keep, acc_next, g_half = run(
            functools.partial(backward_kernel, t == 0),
            halves + (scores_shape, half_rows),
            (place,) + g_parts + (stashed[t], probs, weights, wo) + acc,
            scratch=[pltpu.VMEM((3, tokens, inner), BF16), row_scratch],
            scalars=1,
        )
        acc = (acc_next,)
        received = swapped(send, 1)
        x_mine = run(pair_kernel, half_rows, climbed)

    x_other = swapped(x_mine, 1)
    rows = shape((1, tokens, model_width))
    fallen = down_term(TICKS - 1, keep, received, g_half)
    fallen_other = swapped(fallen, cross)
    rising_out = run(join_kernel, rows, (place, x_mine, x_other), scalars=1)
    table_grad = run(
        functools.partial(table_kernel, bias_table.shape[1]),
        shape((heads, bias_table.shape[1]), F32),
        acc + (buckets,),
    )
    lowered = run(pair_kernel, half_rows, (fallen, fallen_other))
    falling_out = run(join_kernel, rows, (place, lowered, swapped(lowered, 1)), scalars=1)
    return (rising_out, falling_out, table_grad.T[None])


def solution(mesh):
    return jax.shard_map(
        per_device,
        mesh=mesh,
        in_specs=(
            P(("groups", "section"), None, None),
            P(("groups", "section"), None, None),
            P(("groups", "section"), None, None, None),
            P("groups", None, None),
            P("groups"),
            P(),
            P("section", None, "head"),
            P("section", None),
            P("section", None, "head", None, None),
            P("section", "head", None, None),
        ),
        out_specs=(
            P(("groups", "section"), None, None),
            P(("groups", "section"), None, None),
            P(("groups", "section"), None, "head"),
        ),
        check_vma=False,
    )
```

```python
import functools

import jax
import jax.numpy as jnp
from jax import lax
from jax.experimental import pallas as pl
from jax.experimental.pallas import tpu as pltpu
from jax.sharding import PartitionSpec as P

TICKS = 3
EPSILON = 1e-06
LANES = 128
ROWS16 = 16
LAST = (((1,), (1,)), ((), ()))
FIRST = (((0,), (0,)), ((), ()))
F32 = jnp.float32
BF16 = jnp.bfloat16
WHOLE = pl.BlockSpec(memory_space=pltpu.VMEM)
SCALARS = pl.BlockSpec(memory_space=pltpu.SMEM)
UNREAD = pl.BlockSpec(memory_space=pl.ANY)
MIB = 1 << 20


def dot(a, b, dims=None):
    if dims is None:
        return jnp.dot(a, b, preferred_element_type=F32)
    return lax.dot_general(a, b, dims, preferred_element_type=F32)


def rms_normed(rows, gain_row):
    x = rows.astype(F32)
    inverse = lax.rsqrt(jnp.mean(x * x, axis=-1, keepdims=True) + EPSILON)
    return (x * inverse * gain_row).astype(BF16)


def rows_at(index, size):
    return pl.ds(pl.multiple_of(index * size, size), size)


SECOND_CORE, FIRST_SECTION, LAST_SECTION, ADDS_RESIDUAL = range(4)


def flag(flags_ref, row):
    return flags_ref[row : row + 1, :1]


def pick(chosen, yes, no):
    yes, no = yes.astype(F32), no.astype(F32)
    return jnp.where(jnp.broadcast_to(chosen, yes.shape) > 0.5, yes, no)


def joined(second, mine, other):
    return jnp.concatenate([pick(second, other, mine), pick(second, mine, other)], axis=0)


def own_half(second, rows):
    half = rows.shape[0] // 2
    return pick(second, rows[half:], rows[:half])


def fill_bias(table_ref, bucket_ref, bias_ref):
    ids = bucket_ref[...].T
    rows, count = table_ref.shape
    table = jnp.concatenate([table_ref[...], jnp.zeros((rows, LANES - count), F32)], axis=1)
    for h in range(rows):
        row = jnp.broadcast_to(table[h : h + 1], ids.shape)
        bias_ref[h] = jnp.take_along_axis(row, ids, axis=1)


def bias_kernel(table_ref, bucket_ref, bias_ref):
    fill_bias(table_ref, bucket_ref, bias_ref)


def relayout_kernel(
    order_ref, x_ref, kept_ref, gain_ref, table_ref, bucket_ref, w_ref, back_ref, queue_ref, _,
    w_out_ref, qkv_ref, kept_qkv_ref, bias_ref, back_out_ref, entering_ref, normed, arrived,
):
    which = pl.program_id(0)
    block = pl.program_id(1)
    entering = range(entering_ref.shape[0])
    copies = [pltpu.make_async_copy(back_ref, back_out_ref, arrived.at[len(entering)])] + [
        pltpu.make_async_copy(queue_ref.at[order_ref[t]], entering_ref.at[t], arrived.at[t])
        for t in entering
    ]

    @pl.when((which == 0) & (block == 0))
    def _():
        for copy in copies:
            copy.start()
        tokens = x_ref.shape[1]
        normed[:tokens] = rms_normed(x_ref[0], gain_ref[...])
        normed[tokens:] = rms_normed(kept_ref[0, 0], gain_ref[...])
        fill_bias(table_ref, bucket_ref, bias_ref)

    depth = w_ref.shape[0]
    size = ROWS16 * ROWS16
    row = lax.broadcasted_iota(jnp.int32, (size, size), 0)
    col = lax.broadcasted_iota(jnp.int32, (size, size), 1)
    wanted = (row & (ROWS16 - 1)) * ROWS16 + (row >> 4)
    permute = (col == wanted).astype(F32).astype(BF16)

    def step(i, carry):
        d0 = pl.multiple_of(i * 2 * ROWS16, 2 * ROWS16)
        first = w_ref[pl.ds(d0, ROWS16)].reshape(size, LANES)
        second = w_ref[pl.ds(d0 + ROWS16, ROWS16)].reshape(size, LANES)
        moved = dot(permute, jnp.concatenate([first, second], axis=1)).astype(BF16)
        to = pl.multiple_of(block * depth + d0, 2 * ROWS16)
        for h in range(ROWS16):
            piece = moved[h * ROWS16 : (h + 1) * ROWS16]
            lanes = slice(h * LANES, (h + 1) * LANES)
            w_out_ref[which, pl.ds(to, ROWS16), lanes] = piece[:, :LANES]
            w_out_ref[which, pl.ds(to + ROWS16, ROWS16), lanes] = piece[:, LANES:]
        return carry

    lax.fori_loop(0, depth // (2 * ROWS16), step, 0, unroll=16)

    @pl.when(block == pl.num_programs(1) - 1)
    def _():
        tokens = x_ref.shape[1]
        out = dot(normed[...], w_out_ref[which]).astype(BF16)
        qkv_ref[which] = out[:tokens]
        kept_qkv_ref[which] = out[tokens:]

    @pl.when((which == pl.num_programs(0) - 1) & (block == pl.num_programs(1) - 1))
    def _():
        for copy in copies:
            copy.wait()


def probs_of(query, key, bias, scale):
    scores = dot(key, query, LAST) * scale + bias
    raised = jnp.exp(scores - jnp.max(scores, axis=0, keepdims=True))
    return raised * (1.0 / jnp.sum(raised, axis=0, keepdims=True))


def attend(query, key, value, bias_ref, heads, first_head):
    scale = LANES ** (-0.5)
    lanes = [slice(h * LANES, (h + 1) * LANES) for h in range(heads)]
    probs = [
        probs_of(query[:, sl], key[:, sl], bias_ref[first_head + h], scale).astype(BF16)
        for h, sl in enumerate(lanes)
    ]
    return [dot(p, value[:, sl], FIRST).astype(BF16) for p, sl in zip(probs, lanes)]


def forward_kernel(tick, flags_ref, *refs):
    first = tick == 0
    if first:
        x_ref, qkv_ref, bias_ref, wo_ref, send_ref, keep_ref, x_half_ref, attended = refs
    else:
        (mine_ref, other_ref, entering_ref, gain_ref, w_ref, bias_ref, wo_ref,
         send_ref, keep_ref, x_half_ref, attended) = refs
    second = flag(flags_ref, SECOND_CORE)
    group = bias_ref.shape[0] // 2
    if first:
        x = x_ref[0]
    else:
        x = joined(second, mine_ref[...], other_ref[...])
        x = pick(flag(flags_ref, FIRST_SECTION), entering_ref[tick - 1], x)
        normed = rms_normed(x, gain_ref[...])
    x_half_ref[...] = own_half(second, x).astype(BF16)
    for part in range(2):
        at = slice(part * group * LANES, (part + 1) * group * LANES)
        if first:
            query, key, value = (qkv_ref[c, :, at] for c in range(3))
        else:
            query, key, value = (dot(normed, w_ref[c, :, at]).astype(BF16) for c in range(3))
        outs = attend(query, key, value, bias_ref, group, part * group)
        for h, out in enumerate(outs):
            at = (part * group + h) * LANES
            attended[:, at : at + LANES] = out
    split_halves(second, dot(attended[...], wo_ref[...]), send_ref, keep_ref)


def split_halves(second, total, send_ref, keep_ref):
    send_ref[...] = own_half(1.0 - second, total).astype(BF16)
    keep_ref[...] = own_half(second, total)


def stash_kernel(skipped, x_ref, gain_ref, w_ref, *refs):
    *outs, normed = refs
    ticks, tokens = len(outs), x_ref.shape[1]
    for t in range(ticks):
        normed[t * tokens : (t + 1) * tokens] = rms_normed(x_ref[skipped + t], gain_ref[...])
    width = min(512, w_ref.shape[2])

    def step(i, carry):
        at = rows_at(i, width)
        for c in range(3):
            out = dot(normed[...], w_ref[c, :, at]).astype(BF16)
            for t in range(ticks):
                outs[t][c, :, at] = out[t * tokens : (t + 1) * tokens]
        return carry

    lax.fori_loop(0, w_ref.shape[2] // width, step, 0)


def probs_kernel(qkv_ref, bias_ref, out_ref):
    heads = bias_ref.shape[0]
    group = heads // 2
    scale = LANES ** (-0.5)

    def step(g, carry):
        at = rows_at(g, group * LANES)
        query, key = (qkv_ref[c, :, at] for c in range(2))
        for h in range(group):
            sl = slice(h * LANES, (h + 1) * LANES)
            out_ref[g * group + h] = probs_of(
                query[:, sl], key[:, sl], bias_ref[g * group + h], scale
            )
        return carry

    lax.fori_loop(0, 2, step, 0)


def grad_attend(g, qkv_ref, probs_ref, wo_ref, acc_in_ref, stacked, acc_ref, part):
    heads = probs_ref.shape[0] // 2
    scale = LANES ** (-0.5)
    at = slice(part * heads * LANES, (part + 1) * heads * LANES)
    grad_attn = dot(g, wo_ref[at], LAST).astype(BF16)
    for local in range(heads):
        h = part * heads + local
        own = slice(h * LANES, (h + 1) * LANES)
        q, k, v = (qkv_ref[c, :, own] for c in range(3))
        ga = grad_attn[:, local * LANES : (local + 1) * LANES]
        probs = probs_ref[h]
        grad_probs = dot(v, ga, LAST)
        total = jnp.sum(probs * grad_probs, axis=0, keepdims=True)
        grad_scores = probs * (grad_probs - total)
        grad16 = grad_scores.astype(BF16)
        if acc_in_ref is None:
            acc_ref[h] = grad_scores
        else:
            acc_ref[h] = acc_in_ref[h] + grad_scores
        stacked[0, :, own] = (dot(grad16, k, FIRST) * scale).astype(BF16)
        stacked[1, :, own] = (dot(grad16, q) * scale).astype(BF16)
        stacked[2, :, own] = dot(probs.astype(BF16), ga).astype(BF16)


def backward_kernel(first, flags_ref, *refs):
    second = flag(flags_ref, SECOND_CORE)
    if first:
        full_ref, qkv_ref, probs_ref, w_ref, wo_ref, *refs = refs
        send_ref, keep_ref, acc_ref, g_half_ref, stacked = refs
        acc_in_ref = None
        g = full_ref[...]
    else:
        mine_ref, other_ref, qkv_ref, probs_ref, w_ref, wo_ref, acc_in_ref, *refs = refs
        send_ref, keep_ref, acc_ref, g_half_ref, stacked = refs
        g = joined(second, mine_ref[...], other_ref[...]).astype(BF16)
    g_half_ref[...] = own_half(second, g).astype(BF16)
    for part in range(2):
        grad_attend(g, qkv_ref, probs_ref, wo_ref, acc_in_ref, stacked, acc_ref, part)
    total = dot(w_ref[0], stacked[0], LAST)
    total += dot(w_ref[1], stacked[1], LAST)
    total += dot(w_ref[2], stacked[2], LAST)
    split_halves(second, total.T, send_ref, keep_ref)


def pair_kernel(first_ref, second_ref, out_ref):
    out_ref[...] = (first_ref[...].astype(F32) + second_ref[...].astype(F32)).astype(BF16)


def up_term_kernel(flags_ref, keep_ref, received_ref, x_ref, out_ref):
    residual = flag(flags_ref, ADDS_RESIDUAL)
    total = keep_ref[...] + received_ref[...].astype(F32)
    out_ref[...] = (total + residual * x_ref[...].astype(F32)).astype(BF16)


def down_term_kernel(tick, flags_ref, stash_ref, gain_ref, keep_ref, received_ref, g_ref, out_ref):
    residual = flag(flags_ref, ADDS_RESIDUAL)
    x = own_half(flag(flags_ref, SECOND_CORE), stash_ref[tick])
    inverse = lax.rsqrt(jnp.mean(x * x, axis=-1, keepdims=True) + EPSILON)
    weighted = gain_ref[...] * (keep_ref[...] + received_ref[...].astype(F32))
    mean = jnp.mean(x * weighted, axis=-1, keepdims=True)
    cubed = inverse * inverse * inverse
    back = inverse * weighted - x * cubed * mean
    out_ref[...] = (residual * g_ref[...].astype(F32) + back).astype(BF16)


def choose_kernel(flags_ref, own_ref, own_second_ref, first_ref, second_ref, out_ref):
    own = own_ref[...].astype(F32) + own_second_ref[...].astype(F32)
    arrived = first_ref[...].astype(F32) + second_ref[...].astype(F32)
    out_ref[...] = pick(flag(flags_ref, LAST_SECTION), own, arrived).astype(BF16)


def join_kernel(flags_ref, mine_ref, other_ref, out_ref, token_ref):
    second = flag(flags_ref, SECOND_CORE)
    out_ref[0] = joined(second, mine_ref[...], other_ref[...]).astype(BF16)
    token_ref[...] = jnp.zeros_like(token_ref)


def table_kernel(buckets_here, acc_ref, bucket_ref, out_ref, token_ref):
    heads, tokens, _ = acc_ref.shape
    rows = 8
    cells = heads * rows
    columns = buckets_here * rows
    total = jnp.zeros((cells, columns), F32)
    turned = bucket_ref[...].T
    for i in range(tokens // rows):
        at = slice(i * rows, (i + 1) * rows)
        ids = turned[at]
        hits = jnp.concatenate(
            [(ids == b).astype(F32) for b in range(buckets_here)], axis=0
        ).astype(BF16)
        part = acc_ref[:, at, :].reshape(cells, tokens)
        high = part.astype(BF16)
        low = (part - high.astype(F32)).astype(BF16)
        total += dot(high, hits, LAST) + dot(low, hits, LAST)
    row = lax.broadcasted_iota(jnp.int32, (cells, columns), 0)
    col = lax.broadcasted_iota(jnp.int32, (cells, columns), 1)
    total = jnp.where((row & (rows - 1)) == (col & (rows - 1)), total, 0.0)
    summed = jnp.sum(total.reshape(heads, rows, columns), axis=1)
    spread = lax.broadcasted_iota(jnp.int32, (columns, buckets_here), 0) >> 3
    bucket = lax.broadcasted_iota(jnp.int32, (columns, buckets_here), 1)
    fold = (spread == bucket).astype(F32)
    out_ref[...] = jnp.dot(
        summed, fold, preferred_element_type=F32, precision=lax.Precision.HIGHEST
    )
    token_ref[...] = jnp.zeros_like(token_ref)


def shape(dims, dtype=BF16):
    return jax.ShapeDtypeStruct(dims, dtype)


class Chain:
    def __init__(self):
        self.before = None

    def __call__(self, kernel, out_shape, args, scratch=(), limit=16):
        outs = out_shape if isinstance(out_shape, tuple) else (out_shape,)
        extra = () if self.before is None else (self.before,)
        count = len(args)

        def body(*refs):
            kernel(*refs[:count], *refs[count + len(extra) :])

        results = pl.pallas_call(
            body,
            out_shape=outs,
            in_specs=[WHOLE] * count + [UNREAD] * len(extra),
            out_specs=tuple(WHOLE for _ in outs),
            scratch_shapes=list(scratch),
            compiler_params=pltpu.CompilerParams(vmem_limit_bytes=limit * MIB),
            cost_estimate=pl.CostEstimate(flops=0, bytes_accessed=LANES, transcendentals=0),
        )(*args, *extra)
        self.before = results[-1]
        return results if isinstance(out_shape, tuple) else results[0]


def in_hbm(x):
    return pltpu.with_memory_space_constraint(x, pltpu.HBM)


def moved(block, step, bit):
    sections, heads = lax.axis_size("section"), lax.axis_size("head")
    route = [
        (s * heads + h, (s + step) % sections * heads + (h ^ bit))
        for s in range(sections)
        for h in range(heads)
    ]
    return lax.ppermute(block, ("section", "head"), route)


def swapped(block, bit):
    return lax.ppermute(block, "head", [(i, i ^ bit) for i in range(lax.axis_size("head"))])


def per_device(rising, falling, stash, queue, order, buckets, bias_table, gain, w_qkv, w_out):
    section_index = lax.axis_index("section")
    section_count = lax.axis_size("section")
    head_index = lax.axis_index("head")
    head_count = lax.axis_size("head")
    _, model_width, heads, _, head_dim = w_qkv.shape
    tokens = buckets.shape[0]
    half = tokens // 2
    inner = heads * head_dim
    facts = (
        head_index % 2 == 1,
        section_index == 0,
        section_index == section_count - 1,
        head_index < 2,
    )
    flags = jnp.broadcast_to(jnp.stack(facts).astype(F32)[:, None], (len(facts), LANES))
    table = bias_table[0].T
    back = w_out[0].reshape(inner, model_width)
    run = Chain()
    bits = [1 << b for b in range(1, head_count.bit_length() - 1)]
    cross = bits[-1]
    qkv_shape = shape((3, tokens, inner))
    scores_shape = shape((heads, tokens, tokens), F32)

    if heads % ROWS16 == 0:
        rows_first = jnp.transpose(w_qkv[0], (0, 2, 1, 3)).reshape(model_width, 3 * heads, head_dim)
        blocks = 2
        depth = model_width // blocks
        fixed = lambda rank: lambda c, b: (0,) * rank
        weights, qkv, kept_qkv, bias, wo, entering = pl.pallas_call(
            relayout_kernel,
            grid=(3, blocks),
            out_shape=(
                pltpu.VMEM((3, model_width, inner), BF16),
                qkv_shape,
                qkv_shape,
                scores_shape,
                pltpu.VMEM((inner, model_width), BF16),
                pltpu.VMEM((TICKS - 1, tokens, model_width), BF16),
            ),
            in_specs=[
                SCALARS,
                pl.BlockSpec((1, tokens, model_width), fixed(3)),
                pl.BlockSpec((1, 1, tokens, model_width), fixed(4)),
                pl.BlockSpec((1, model_width), fixed(2)),
                pl.BlockSpec(table.shape, fixed(2)),
                pl.BlockSpec((tokens, tokens), fixed(2)),
                pl.BlockSpec((depth, heads, head_dim), lambda c, b: (b, c, 0)),
                UNREAD,
                UNREAD,
                UNREAD,
            ],
            out_specs=(
                WHOLE,
                pl.BlockSpec((3, tokens, inner), fixed(3)),
                pl.BlockSpec((3, tokens, inner), fixed(3)),
                pl.BlockSpec((heads, tokens, tokens), fixed(3)),
                WHOLE,
                WHOLE,
            ),
            scratch_shapes=[pltpu.VMEM((2 * tokens, model_width), BF16), pltpu.SemaphoreType.DMA((TICKS,))],
            compiler_params=pltpu.CompilerParams(vmem_limit_bytes=24 * MIB),
            cost_estimate=pl.CostEstimate(
                flops=0, bytes_accessed=2 * w_qkv.size, transcendentals=0
            ),
        )(
            order, in_hbm(rising), in_hbm(stash), in_hbm(gain), in_hbm(table), in_hbm(buckets),
            in_hbm(rows_first), in_hbm(back), in_hbm(queue), flags,
        )
        run.before = qkv
    else:
        wo = back
        entering = jnp.stack(
            [lax.dynamic_index_in_dim(queue, order[t], 0, False) for t in range(TICKS - 1)]
        )
        weights = jnp.transpose(w_qkv[0], (2, 0, 1, 3)).reshape(3, model_width, inner)
        bias = run(bias_kernel, scores_shape, (table, buckets))
        qkv, kept_qkv = (
            run(
                functools.partial(stash_kernel, 0),
                qkv_shape,
                (rows, gain, weights),
                scratch=[pltpu.VMEM((tokens, model_width), BF16)],
            )
            for rows in (rising, stash[0, :1])
        )
    halves = (shape((half, model_width)), shape((half, model_width), F32))
    half_rows = shape((half, model_width))

    def but_last_bit(term):
        for bit in bits[:-1]:
            term = run(pair_kernel, half_rows, (term, swapped(term, bit)))
        return term

    def down_term(tick, keep, received, g_half):
        term = run(
            functools.partial(down_term_kernel, tick),
            half_rows,
            (flags, stash[0], gain, keep, received, g_half),
        )
        return but_last_bit(term)

    stashed = [kept_qkv]
    acc = ()
    for t in range(TICKS):
        final = t + 1 == TICKS
        scratch = [pltpu.VMEM((tokens, inner), BF16)]
        if t == 0:
            args = (flags, rising, qkv, bias, wo)
        else:
            x_other = swapped(x_mine, 1)
            fallen = down_term(t - 1, keep, received, g_half)
            arrivals = (up, in_last, moved(fallen, -1, 0), moved(fallen, -1, cross))
            args = (flags, x_mine, x_other, entering, gain, weights, bias, wo)
        up_send, up_keep, x_half = run(
            functools.partial(forward_kernel, t),
            halves + (half_rows,),
            args,
            scratch=scratch,
        )
        up_received = swapped(up_send, 1)
        if t > 0:
            stashed.append(
                run(
                    functools.partial(stash_kernel, t),
                    qkv_shape,
                    (stash[0], gain, weights),
                    scratch=[pltpu.VMEM((tokens, model_width), BF16)],
                )
            )
        probs = run(probs_kernel, scores_shape, (stashed[t], bias))
        if t == 0:
            g_parts = (falling[0],)
        else:
            g_mine = run(choose_kernel, half_rows, (flags,) + arrivals)
            g_parts = (g_mine, swapped(g_mine, 1))
        up = but_last_bit(
            run(up_term_kernel, half_rows, (flags, up_keep, up_received, x_half))
        )
        if final:
            climbed = (up, swapped(up, cross))
        else:
            climbed = (moved(up, 1, 0), moved(up, 1, cross))
            in_last = swapped(up, cross)

        send, keep, acc_next, g_half = run(
            functools.partial(backward_kernel, t == 0),
            halves + (scores_shape, half_rows),
            (flags,) + g_parts + (stashed[t], probs, weights, wo) + acc,
            scratch=[pltpu.VMEM((3, tokens, inner), BF16)],
        )
        acc = (acc_next,)
        received = swapped(send, 1)
        x_mine = run(pair_kernel, half_rows, climbed)

    x_other = swapped(x_mine, 1)
    rows = shape((1, tokens, model_width))
    fallen = down_term(TICKS - 1, keep, received, g_half)
    fallen_other = swapped(fallen, cross)
    token = shape((8, LANES), F32)
    rising_out, _ = run(join_kernel, (rows, token), (flags, x_mine, x_other))
    table_grad, _ = run(
        functools.partial(table_kernel, bias_table.shape[1]),
        (shape((heads, bias_table.shape[1]), F32), token),
        acc + (buckets,),
    )
    lowered = run(pair_kernel, half_rows, (fallen, fallen_other))
    falling_out, _ = run(join_kernel, (rows, token), (flags, lowered, swapped(lowered, 1)))
    return (rising_out, falling_out, table_grad.T[None])


def solution(mesh):
    return jax.shard_map(
        per_device,
        mesh=mesh,
        in_specs=(
            P(("groups", "section"), None, None),
            P(("groups", "section"), None, None),
            P(("groups", "section"), None, None, None),
            P("groups", None, None),
            P("groups"),
            P(),
            P("section", None, "head"),
            P("section", None),
            P("section", None, "head", None, None),
            P("section", "head", None, None),
        ),
        out_specs=(
            P(("groups", "section"), None, None),
            P(("groups", "section"), None, None),
            P(("groups", "section"), None, "head"),
        ),
        check_vma=False,
    )
```

```python
import functools

import jax
import jax.numpy as jnp
from jax import lax
from jax.experimental import pallas as pl
from jax.experimental.pallas import tpu as pltpu
from jax.sharding import PartitionSpec as P

TICKS = 3
EPSILON = 1e-06
LANES = 128
ROWS16 = 16
LAST = (((1,), (1,)), ((), ()))
FIRST = (((0,), (0,)), ((), ()))
F32 = jnp.float32
BF16 = jnp.bfloat16
WHOLE = pl.BlockSpec(memory_space=pltpu.VMEM)
UNREAD = pl.BlockSpec(memory_space=pl.ANY)
MIB = 1 << 20


def dot(a, b, dims=None):
    if dims is None:
        return jnp.dot(a, b, preferred_element_type=F32)
    return lax.dot_general(a, b, dims, preferred_element_type=F32)


def rms_normed(rows, gain_row):
    x = rows.astype(F32)
    inverse = lax.rsqrt(jnp.mean(x * x, axis=-1, keepdims=True) + EPSILON)
    return (x * inverse * gain_row).astype(BF16)


def rows_at(index, size):
    return pl.ds(pl.multiple_of(index * size, size), size)


SECOND_CORE, FIRST_SECTION, LAST_SECTION, ADDS_RESIDUAL = range(4)


def flag(flags_ref, row):
    return flags_ref[row : row + 1, :1]


def pick(chosen, yes, no):
    yes, no = yes.astype(F32), no.astype(F32)
    return jnp.where(jnp.broadcast_to(chosen, yes.shape) > 0.5, yes, no)


def joined(second, mine, other):
    return jnp.concatenate([pick(second, other, mine), pick(second, mine, other)], axis=0)


def own_half(second, rows):
    half = rows.shape[0] // 2
    return pick(second, rows[half:], rows[:half])


def fill_bias(table_ref, bucket_ref, bias_ref):
    ids = bucket_ref[...].T
    rows, count = table_ref.shape
    table = jnp.concatenate([table_ref[...], jnp.zeros((rows, LANES - count), F32)], axis=1)
    for h in range(rows):
        row = jnp.broadcast_to(table[h : h + 1], ids.shape)
        bias_ref[h] = jnp.take_along_axis(row, ids, axis=1)


def bias_kernel(table_ref, bucket_ref, bias_ref):
    fill_bias(table_ref, bucket_ref, bias_ref)


def relayout_kernel(
    order_hbm, x_hbm, kept_hbm, gain_hbm, table_hbm, bucket_hbm, w_hbm, back_hbm, queue_hbm, _,
    w_ref, qkv_ref, kept_qkv_ref, bias_ref, back_ref, entering_ref,
    order_ref, x_ref, kept_ref, gain_ref, table_ref, bucket_ref, raw, normed, small, large, last,
):
    blocks, depth, heads, _ = raw.shape
    blocks //= 3
    small_copies = [
        pltpu.make_async_copy(source, target, small.at[i])
        for i, (source, target) in enumerate(
            (
                (order_hbm, order_ref),
                (x_hbm.at[0], x_ref),
                (kept_hbm.at[0, 0], kept_ref),
                (gain_hbm, gain_ref),
                (table_hbm, table_ref),
                (bucket_hbm, bucket_ref),
            )
        )
    ]
    for copy in small_copies:
        copy.start()
    large_copies = [
        pltpu.make_async_copy(
            w_hbm.at[pl.ds(b * depth, depth), pl.ds(c * heads, heads)],
            raw.at[c * blocks + b],
            large.at[c * blocks + b],
        )
        for c in range(3)
        for b in range(blocks)
    ]
    for copy in large_copies:
        copy.start()
    for copy in small_copies:
        copy.wait()
    last_copies = [pltpu.make_async_copy(back_hbm, back_ref, last.at[0])] + [
        pltpu.make_async_copy(queue_hbm.at[order_ref[t]], entering_ref.at[t], last.at[1 + t])
        for t in range(entering_ref.shape[0])
    ]
    for copy in last_copies:
        copy.start()
    tokens = x_ref.shape[0]
    normed[:tokens] = rms_normed(x_ref[...], gain_ref[...])
    normed[tokens:] = rms_normed(kept_ref[...], gain_ref[...])
    fill_bias(table_ref, bucket_ref, bias_ref)

    size = ROWS16 * ROWS16
    row = lax.broadcasted_iota(jnp.int32, (size, size), 0)
    col = lax.broadcasted_iota(jnp.int32, (size, size), 1)
    wanted = (row & (ROWS16 - 1)) * ROWS16 + (row >> 4)
    permute = (col == wanted).astype(F32).astype(BF16)

    for which in range(3):
        for block in range(blocks):
            large_copies[which * blocks + block].wait()

            def step(i, carry):
                d0 = pl.multiple_of(i * 2 * ROWS16, 2 * ROWS16)
                part = raw.at[which * blocks + block]
                first = part[pl.ds(d0, ROWS16)].reshape(size, LANES)
                second = part[pl.ds(d0 + ROWS16, ROWS16)].reshape(size, LANES)
                moved = dot(permute, jnp.concatenate([first, second], axis=1)).astype(BF16)
                to = pl.multiple_of(block * depth + d0, 2 * ROWS16)
                for h in range(ROWS16):
                    piece = moved[h * ROWS16 : (h + 1) * ROWS16]
                    lanes = slice(h * LANES, (h + 1) * LANES)
                    w_ref[which, pl.ds(to, ROWS16), lanes] = piece[:, :LANES]
                    w_ref[which, pl.ds(to + ROWS16, ROWS16), lanes] = piece[:, LANES:]
                return carry

            lax.fori_loop(0, depth // (2 * ROWS16), step, 0, unroll=8)
        out = dot(normed[...], w_ref[which]).astype(BF16)
        qkv_ref[which] = out[:tokens]
        kept_qkv_ref[which] = out[tokens:]
    for copy in last_copies:
        copy.wait()


def probs_of(query, key, bias, scale):
    scores = dot(key, query, LAST) * scale + bias
    raised = jnp.exp(scores - jnp.max(scores, axis=0, keepdims=True))
    return raised * (1.0 / jnp.sum(raised, axis=0, keepdims=True))


def attend(query, key, value, bias_ref, heads, first_head):
    scale = LANES ** (-0.5)
    lanes = [slice(h * LANES, (h + 1) * LANES) for h in range(heads)]
    probs = [
        probs_of(query[:, sl], key[:, sl], bias_ref[first_head + h], scale).astype(BF16)
        for h, sl in enumerate(lanes)
    ]
    return [dot(p, value[:, sl], FIRST).astype(BF16) for p, sl in zip(probs, lanes)]


def forward_kernel(tick, flags_ref, *refs):
    first = tick == 0
    if first:
        x_ref, qkv_ref, bias_ref, wo_ref, send_ref, keep_ref, x_half_ref, attended = refs
    else:
        (mine_ref, other_ref, entering_ref, gain_ref, w_ref, bias_ref, wo_ref,
         send_ref, keep_ref, x_half_ref, attended) = refs
    second = flag(flags_ref, SECOND_CORE)
    group = bias_ref.shape[0] // 2
    if first:
        x = x_ref[0]
    else:
        x = joined(second, mine_ref[...], other_ref[...])
        x = pick(flag(flags_ref, FIRST_SECTION), entering_ref[tick - 1], x)
        normed = rms_normed(x, gain_ref[...])
    x_half_ref[...] = own_half(second, x).astype(BF16)
    for part in range(2):
        at = slice(part * group * LANES, (part + 1) * group * LANES)
        if first:
            query, key, value = (qkv_ref[c, :, at] for c in range(3))
        else:
            query, key, value = (dot(normed, w_ref[c, :, at]).astype(BF16) for c in range(3))
        outs = attend(query, key, value, bias_ref, group, part * group)
        for h, out in enumerate(outs):
            at = (part * group + h) * LANES
            attended[:, at : at + LANES] = out
    split_halves(second, dot(attended[...], wo_ref[...]), send_ref, keep_ref)


def split_halves(second, total, send_ref, keep_ref):
    send_ref[...] = own_half(1.0 - second, total).astype(BF16)
    keep_ref[...] = own_half(second, total)


def stash_kernel(skipped, x_ref, gain_ref, w_ref, *refs):
    *outs, normed = refs
    ticks, tokens = len(outs), x_ref.shape[1]
    for t in range(ticks):
        normed[t * tokens : (t + 1) * tokens] = rms_normed(x_ref[skipped + t], gain_ref[...])
    width = min(512, w_ref.shape[2])

    def step(i, carry):
        at = rows_at(i, width)
        for c in range(3):
            out = dot(normed[...], w_ref[c, :, at]).astype(BF16)
            for t in range(ticks):
                outs[t][c, :, at] = out[t * tokens : (t + 1) * tokens]
        return carry

    lax.fori_loop(0, w_ref.shape[2] // width, step, 0)


def probs_kernel(qkv_ref, bias_ref, out_ref):
    heads = bias_ref.shape[0]
    group = heads // 2
    scale = LANES ** (-0.5)

    def step(g, carry):
        at = rows_at(g, group * LANES)
        query, key = (qkv_ref[c, :, at] for c in range(2))
        for h in range(group):
            sl = slice(h * LANES, (h + 1) * LANES)
            out_ref[g * group + h] = probs_of(
                query[:, sl], key[:, sl], bias_ref[g * group + h], scale
            )
        return carry

    lax.fori_loop(0, 2, step, 0)


def grad_attend(g, qkv_ref, probs_ref, wo_ref, acc_in_ref, stacked, acc_ref, part):
    heads = probs_ref.shape[0] // 2
    scale = LANES ** (-0.5)
    at = slice(part * heads * LANES, (part + 1) * heads * LANES)
    grad_attn = dot(g, wo_ref[at], LAST).astype(BF16)
    for local in range(heads):
        h = part * heads + local
        own = slice(h * LANES, (h + 1) * LANES)
        q, k, v = (qkv_ref[c, :, own] for c in range(3))
        ga = grad_attn[:, local * LANES : (local + 1) * LANES]
        probs = probs_ref[h]
        grad_probs = dot(v, ga, LAST)
        total = jnp.sum(probs * grad_probs, axis=0, keepdims=True)
        grad_scores = probs * (grad_probs - total)
        grad16 = grad_scores.astype(BF16)
        if acc_in_ref is None:
            acc_ref[h] = grad_scores
        else:
            acc_ref[h] = acc_in_ref[h] + grad_scores
        stacked[0, :, own] = (dot(grad16, k, FIRST) * scale).astype(BF16)
        stacked[1, :, own] = (dot(grad16, q) * scale).astype(BF16)
        stacked[2, :, own] = dot(probs.astype(BF16), ga).astype(BF16)


def backward_kernel(first, flags_ref, *refs):
    second = flag(flags_ref, SECOND_CORE)
    if first:
        full_ref, qkv_ref, probs_ref, w_ref, wo_ref, *refs = refs
        send_ref, keep_ref, acc_ref, g_half_ref, stacked = refs
        acc_in_ref = None
        g = full_ref[...]
    else:
        mine_ref, other_ref, qkv_ref, probs_ref, w_ref, wo_ref, acc_in_ref, *refs = refs
        send_ref, keep_ref, acc_ref, g_half_ref, stacked = refs
        g = joined(second, mine_ref[...], other_ref[...]).astype(BF16)
    g_half_ref[...] = own_half(second, g).astype(BF16)
    for part in range(2):
        grad_attend(g, qkv_ref, probs_ref, wo_ref, acc_in_ref, stacked, acc_ref, part)
    total = dot(w_ref[0], stacked[0], LAST)
    total += dot(w_ref[1], stacked[1], LAST)
    total += dot(w_ref[2], stacked[2], LAST)
    split_halves(second, total.T, send_ref, keep_ref)


def pair_kernel(first_ref, second_ref, out_ref):
    out_ref[...] = (first_ref[...].astype(F32) + second_ref[...].astype(F32)).astype(BF16)


def up_term_kernel(flags_ref, keep_ref, received_ref, x_ref, out_ref):
    residual = flag(flags_ref, ADDS_RESIDUAL)
    total = keep_ref[...] + received_ref[...].astype(F32)
    out_ref[...] = (total + residual * x_ref[...].astype(F32)).astype(BF16)


def down_term_kernel(tick, flags_ref, stash_ref, gain_ref, keep_ref, received_ref, g_ref, out_ref):
    residual = flag(flags_ref, ADDS_RESIDUAL)
    x = own_half(flag(flags_ref, SECOND_CORE), stash_ref[tick])
    inverse = lax.rsqrt(jnp.mean(x * x, axis=-1, keepdims=True) + EPSILON)
    weighted = gain_ref[...] * (keep_ref[...] + received_ref[...].astype(F32))
    mean = jnp.mean(x * weighted, axis=-1, keepdims=True)
    cubed = inverse * inverse * inverse
    back = inverse * weighted - x * cubed * mean
    out_ref[...] = (residual * g_ref[...].astype(F32) + back).astype(BF16)


def choose_kernel(flags_ref, own_ref, own_second_ref, first_ref, second_ref, out_ref):
    own = own_ref[...].astype(F32) + own_second_ref[...].astype(F32)
    arrived = first_ref[...].astype(F32) + second_ref[...].astype(F32)
    out_ref[...] = pick(flag(flags_ref, LAST_SECTION), own, arrived).astype(BF16)


def join_kernel(flags_ref, mine_ref, other_ref, out_ref, token_ref):
    second = flag(flags_ref, SECOND_CORE)
    out_ref[0] = joined(second, mine_ref[...], other_ref[...]).astype(BF16)
    token_ref[...] = jnp.zeros_like(token_ref)


def table_kernel(buckets_here, acc_ref, bucket_ref, out_ref, token_ref):
    heads, tokens, _ = acc_ref.shape
    rows = 8
    cells = heads * rows
    columns = buckets_here * rows
    total = jnp.zeros((cells, columns), F32)
    turned = bucket_ref[...].T
    for i in range(tokens // rows):
        at = slice(i * rows, (i + 1) * rows)
        ids = turned[at]
        hits = jnp.concatenate(
            [(ids == b).astype(F32) for b in range(buckets_here)], axis=0
        ).astype(BF16)
        part = acc_ref[:, at, :].reshape(cells, tokens)
        high = part.astype(BF16)
        low = (part - high.astype(F32)).astype(BF16)
        total += dot(high, hits, LAST) + dot(low, hits, LAST)
    row = lax.broadcasted_iota(jnp.int32, (cells, columns), 0)
    col = lax.broadcasted_iota(jnp.int32, (cells, columns), 1)
    total = jnp.where((row & (rows - 1)) == (col & (rows - 1)), total, 0.0)
    summed = jnp.sum(total.reshape(heads, rows, columns), axis=1)
    spread = lax.broadcasted_iota(jnp.int32, (columns, buckets_here), 0) >> 3
    bucket = lax.broadcasted_iota(jnp.int32, (columns, buckets_here), 1)
    fold = (spread == bucket).astype(F32)
    out_ref[...] = jnp.dot(
        summed, fold, preferred_element_type=F32, precision=lax.Precision.HIGHEST
    )
    token_ref[...] = jnp.zeros_like(token_ref)


def shape(dims, dtype=BF16):
    return jax.ShapeDtypeStruct(dims, dtype)


class Chain:
    def __init__(self):
        self.before = None

    def __call__(self, kernel, out_shape, args, scratch=(), limit=16):
        outs = out_shape if isinstance(out_shape, tuple) else (out_shape,)
        extra = () if self.before is None else (self.before,)
        count = len(args)

        def body(*refs):
            kernel(*refs[:count], *refs[count + len(extra) :])

        results = pl.pallas_call(
            body,
            out_shape=outs,
            in_specs=[WHOLE] * count + [UNREAD] * len(extra),
            out_specs=tuple(WHOLE for _ in outs),
            scratch_shapes=list(scratch),
            compiler_params=pltpu.CompilerParams(vmem_limit_bytes=limit * MIB),
            cost_estimate=pl.CostEstimate(flops=0, bytes_accessed=LANES, transcendentals=0),
        )(*args, *extra)
        self.before = results[-1]
        return results if isinstance(out_shape, tuple) else results[0]


def in_hbm(x):
    return pltpu.with_memory_space_constraint(x, pltpu.HBM)


def moved(block, step, bit):
    sections, heads = lax.axis_size("section"), lax.axis_size("head")
    route = [
        (s * heads + h, (s + step) % sections * heads + (h ^ bit))
        for s in range(sections)
        for h in range(heads)
    ]
    return lax.ppermute(block, ("section", "head"), route)


def swapped(block, bit):
    return lax.ppermute(block, "head", [(i, i ^ bit) for i in range(lax.axis_size("head"))])


def per_device(rising, falling, stash, queue, order, buckets, bias_table, gain, w_qkv, w_out):
    section_index = lax.axis_index("section")
    section_count = lax.axis_size("section")
    head_index = lax.axis_index("head")
    head_count = lax.axis_size("head")
    _, model_width, heads, _, head_dim = w_qkv.shape
    tokens = buckets.shape[0]
    half = tokens // 2
    inner = heads * head_dim
    facts = (
        head_index % 2 == 1,
        section_index == 0,
        section_index == section_count - 1,
        head_index < 2,
    )
    flags = jnp.broadcast_to(jnp.stack(facts).astype(F32)[:, None], (len(facts), LANES))
    table = bias_table[0].T
    back = w_out[0].reshape(inner, model_width)
    run = Chain()
    bits = [1 << b for b in range(1, head_count.bit_length() - 1)]
    cross = bits[-1]
    qkv_shape = shape((3, tokens, inner))
    scores_shape = shape((heads, tokens, tokens), F32)

    if heads % ROWS16 == 0:
        rows_first = jnp.transpose(w_qkv[0], (0, 2, 1, 3)).reshape(model_width, 3 * heads, head_dim)
        blocks = 4
        depth = model_width // blocks
        row_scratch = pltpu.VMEM((tokens, model_width), BF16)
        args = (order, rising, stash, gain, table, buckets, rows_first, back, queue)
        weights, qkv, kept_qkv, bias, wo, entering = pl.pallas_call(
            relayout_kernel,
            out_shape=(
                pltpu.VMEM((3, model_width, inner), BF16),
                qkv_shape,
                qkv_shape,
                scores_shape,
                pltpu.VMEM((inner, model_width), BF16),
                pltpu.VMEM((TICKS - 1, tokens, model_width), BF16),
            ),
            in_specs=[UNREAD] * (len(args) + 1),
            out_specs=(WHOLE,) * 6,
            scratch_shapes=[
                pltpu.SMEM(order.shape, jnp.int32),
                row_scratch,
                row_scratch,
                pltpu.VMEM(gain.shape, F32),
                pltpu.VMEM(table.shape, F32),
                pltpu.VMEM(buckets.shape, jnp.int32),
                pltpu.VMEM((3 * blocks, depth, heads, head_dim), BF16),
                pltpu.VMEM((2 * tokens, model_width), BF16),
                pltpu.SemaphoreType.DMA((6,)),
                pltpu.SemaphoreType.DMA((3 * blocks,)),
                pltpu.SemaphoreType.DMA((TICKS,)),
            ],
            compiler_params=pltpu.CompilerParams(vmem_limit_bytes=28 * MIB),
            cost_estimate=pl.CostEstimate(flops=0, bytes_accessed=w_qkv.size, transcendentals=0),
        )(*(in_hbm(arg) for arg in args), flags)
        run.before = qkv
    else:
        wo = back
        entering = jnp.stack(
            [lax.dynamic_index_in_dim(queue, order[t], 0, False) for t in range(TICKS - 1)]
        )
        weights = jnp.transpose(w_qkv[0], (2, 0, 1, 3)).reshape(3, model_width, inner)
        bias = run(bias_kernel, scores_shape, (table, buckets))
        qkv, kept_qkv = (
            run(
                functools.partial(stash_kernel, 0),
                qkv_shape,
                (rows, gain, weights),
                scratch=[pltpu.VMEM((tokens, model_width), BF16)],
            )
            for rows in (rising, stash[0, :1])
        )
    halves = (shape((half, model_width)), shape((half, model_width), F32))
    half_rows = shape((half, model_width))

    def but_last_bit(term):
        for bit in bits[:-1]:
            term = run(pair_kernel, half_rows, (term, swapped(term, bit)))
        return term

    def down_term(tick, keep, received, g_half):
        term = run(
            functools.partial(down_term_kernel, tick),
            half_rows,
            (flags, stash[0], gain, keep, received, g_half),
        )
        return but_last_bit(term)

    stashed = [kept_qkv]
    acc = ()
    for t in range(TICKS):
        final = t + 1 == TICKS
        scratch = [pltpu.VMEM((tokens, inner), BF16)]
        if t == 0:
            args = (flags, rising, qkv, bias, wo)
        else:
            x_other = swapped(x_mine, 1)
            fallen = down_term(t - 1, keep, received, g_half)
            arrivals = (up, in_last, moved(fallen, -1, 0), moved(fallen, -1, cross))
            args = (flags, x_mine, x_other, entering, gain, weights, bias, wo)
        up_send, up_keep, x_half = run(
            functools.partial(forward_kernel, t),
            halves + (half_rows,),
            args,
            scratch=scratch,
        )
        up_received = swapped(up_send, 1)
        if t > 0:
            stashed.append(
                run(
                    functools.partial(stash_kernel, t),
                    qkv_shape,
                    (stash[0], gain, weights),
                    scratch=[pltpu.VMEM((tokens, model_width), BF16)],
                )
            )
        probs = run(probs_kernel, scores_shape, (stashed[t], bias))
        if t == 0:
            g_parts = (falling[0],)
        else:
            g_mine = run(choose_kernel, half_rows, (flags,) + arrivals)
            g_parts = (g_mine, swapped(g_mine, 1))
        up = but_last_bit(
            run(up_term_kernel, half_rows, (flags, up_keep, up_received, x_half))
        )
        if final:
            climbed = (up, swapped(up, cross))
        else:
            climbed = (moved(up, 1, 0), moved(up, 1, cross))
            in_last = swapped(up, cross)

        send, keep, acc_next, g_half = run(
            functools.partial(backward_kernel, t == 0),
            halves + (scores_shape, half_rows),
            (flags,) + g_parts + (stashed[t], probs, weights, wo) + acc,
            scratch=[pltpu.VMEM((3, tokens, inner), BF16)],
        )
        acc = (acc_next,)
        received = swapped(send, 1)
        x_mine = run(pair_kernel, half_rows, climbed)

    x_other = swapped(x_mine, 1)
    rows = shape((1, tokens, model_width))
    fallen = down_term(TICKS - 1, keep, received, g_half)
    fallen_other = swapped(fallen, cross)
    token = shape((8, LANES), F32)
    rising_out, _ = run(join_kernel, (rows, token), (flags, x_mine, x_other))
    table_grad, _ = run(
        functools.partial(table_kernel, bias_table.shape[1]),
        (shape((heads, bias_table.shape[1]), F32), token),
        acc + (buckets,),
    )
    lowered = run(pair_kernel, half_rows, (fallen, fallen_other))
    falling_out, _ = run(join_kernel, (rows, token), (flags, lowered, swapped(lowered, 1)))
    return (rising_out, falling_out, table_grad.T[None])


def solution(mesh):
    return jax.shard_map(
        per_device,
        mesh=mesh,
        in_specs=(
            P(("groups", "section"), None, None),
            P(("groups", "section"), None, None),
            P(("groups", "section"), None, None, None),
            P("groups", None, None),
            P("groups"),
            P(),
            P("section", None, "head"),
            P("section", None),
            P("section", None, "head", None, None),
            P("section", "head", None, None),
        ),
        out_specs=(
            P(("groups", "section"), None, None),
            P(("groups", "section"), None, None),
            P(("groups", "section"), None, "head"),
        ),
        check_vma=False,
    )
```

```python
import functools

import jax
import jax.numpy as jnp
from jax import lax
from jax.experimental import pallas as pl
from jax.experimental.pallas import tpu as pltpu
from jax.sharding import PartitionSpec as P

TICKS = 3
EPSILON = 1e-06
LANES = 128
ROWS16 = 16
LAST = (((1,), (1,)), ((), ()))
FIRST = (((0,), (0,)), ((), ()))
F32 = jnp.float32
BF16 = jnp.bfloat16
WHOLE = pl.BlockSpec(memory_space=pltpu.VMEM)
SCALARS = pl.BlockSpec(memory_space=pltpu.SMEM)
UNREAD = pl.BlockSpec(memory_space=pl.ANY)
MIB = 1 << 20


def dot(a, b, dims=None):
    if dims is None:
        return jnp.dot(a, b, preferred_element_type=F32)
    return lax.dot_general(a, b, dims, preferred_element_type=F32)


def rms_normed(rows, gain_row):
    x = rows.astype(F32)
    inverse = lax.rsqrt(jnp.mean(x * x, axis=-1, keepdims=True) + EPSILON)
    return (x * inverse * gain_row).astype(BF16)


def rows_at(index, size):
    return pl.ds(pl.multiple_of(index * size, size), size)


SECOND_CORE, FIRST_SECTION, LAST_SECTION, ADDS_RESIDUAL = range(4)


def flag(flags_ref, row):
    return flags_ref[row : row + 1, :1]


def pick(chosen, yes, no):
    yes, no = yes.astype(F32), no.astype(F32)
    return jnp.where(jnp.broadcast_to(chosen, yes.shape) > 0.5, yes, no)


def joined(second, mine, other):
    return jnp.concatenate([pick(second, other, mine), pick(second, mine, other)], axis=0)


def own_half(second, rows):
    half = rows.shape[0] // 2
    return pick(second, rows[half:], rows[:half])


def fill_bias(table_ref, bucket_ref, bias_ref):
    ids = bucket_ref[...].T
    rows, count = table_ref.shape
    table = jnp.concatenate([table_ref[...], jnp.zeros((rows, LANES - count), F32)], axis=1)
    for h in range(rows):
        row = jnp.broadcast_to(table[h : h + 1], ids.shape)
        bias_ref[h] = jnp.take_along_axis(row, ids, axis=1)


def bias_kernel(table_ref, bucket_ref, bias_ref):
    fill_bias(table_ref, bucket_ref, bias_ref)


def relayout_kernel(
    order_ref, x_ref, kept_ref, gain_ref, table_ref, bucket_ref, w_ref, back_ref, queue_ref, _,
    w_out_ref, qkv_ref, kept_qkv_ref, bias_ref, back_out_ref, entering_ref, normed, arrived,
):
    which = pl.program_id(0)
    block = pl.program_id(1)
    entering = range(entering_ref.shape[0])
    copies = [pltpu.make_async_copy(back_ref, back_out_ref, arrived.at[len(entering)])] + [
        pltpu.make_async_copy(queue_ref.at[order_ref[t]], entering_ref.at[t], arrived.at[t])
        for t in entering
    ]

    @pl.when((which == 0) & (block == 0))
    def _():
        for copy in copies:
            copy.start()
        tokens = x_ref.shape[1]
        normed[:tokens] = rms_normed(x_ref[0], gain_ref[...])
        normed[tokens:] = rms_normed(kept_ref[0, 0], gain_ref[...])
        fill_bias(table_ref, bucket_ref, bias_ref)

    depth = w_ref.shape[0]
    size = ROWS16 * ROWS16
    row = lax.broadcasted_iota(jnp.int32, (size, size), 0)
    col = lax.broadcasted_iota(jnp.int32, (size, size), 1)
    wanted = (row & (ROWS16 - 1)) * ROWS16 + (row >> 4)
    permute = (col == wanted).astype(F32).astype(BF16)

    def step(i, carry):
        d0 = pl.multiple_of(i * 2 * ROWS16, 2 * ROWS16)
        first = w_ref[pl.ds(d0, ROWS16)].reshape(size, LANES)
        second = w_ref[pl.ds(d0 + ROWS16, ROWS16)].reshape(size, LANES)
        moved = dot(permute, jnp.concatenate([first, second], axis=1)).astype(BF16)
        to = pl.multiple_of(block * depth + d0, 2 * ROWS16)
        for h in range(ROWS16):
            piece = moved[h * ROWS16 : (h + 1) * ROWS16]
            lanes = slice(h * LANES, (h + 1) * LANES)
            w_out_ref[which, pl.ds(to, ROWS16), lanes] = piece[:, :LANES]
            w_out_ref[which, pl.ds(to + ROWS16, ROWS16), lanes] = piece[:, LANES:]
        return carry

    lax.fori_loop(0, depth // (2 * ROWS16), step, 0, unroll=16)

    @pl.when(block == pl.num_programs(1) - 1)
    def _():
        tokens = x_ref.shape[1]
        out = dot(normed[...], w_out_ref[which]).astype(BF16)
        qkv_ref[which] = out[:tokens]
        kept_qkv_ref[which] = out[tokens:]

    @pl.when((which == pl.num_programs(0) - 1) & (block == pl.num_programs(1) - 1))
    def _():
        for copy in copies:
            copy.wait()


def probs_of(query, key, bias, scale):
    scores = dot(key, query, LAST) * scale + bias
    raised = jnp.exp(scores - jnp.max(scores, axis=0, keepdims=True))
    return raised * (1.0 / jnp.sum(raised, axis=0, keepdims=True))


def attend(query, key, value, bias_ref, heads, first_head):
    scale = LANES ** (-0.5)
    lanes = [slice(h * LANES, (h + 1) * LANES) for h in range(heads)]
    probs = [
        probs_of(query[:, sl], key[:, sl], bias_ref[first_head + h], scale).astype(BF16)
        for h, sl in enumerate(lanes)
    ]
    return [dot(p, value[:, sl], FIRST).astype(BF16) for p, sl in zip(probs, lanes)]


def forward_kernel(tick, flags_ref, *refs):
    first = tick == 0
    if first:
        x_ref, qkv_ref, bias_ref, wo_ref, send_ref, keep_ref, x_half_ref, attended = refs
    else:
        (mine_ref, other_ref, entering_ref, gain_ref, w_ref, bias_ref, wo_ref,
         send_ref, keep_ref, x_half_ref, attended) = refs
    second = flag(flags_ref, SECOND_CORE)
    group = bias_ref.shape[0] // 2
    if first:
        x = x_ref[0]
    else:
        x = joined(second, mine_ref[...], other_ref[...])
        x = pick(flag(flags_ref, FIRST_SECTION), entering_ref[tick - 1], x)
        normed = rms_normed(x, gain_ref[...])
    x_half_ref[...] = own_half(second, x).astype(BF16)
    for part in range(2):
        at = slice(part * group * LANES, (part + 1) * group * LANES)
        if first:
            query, key, value = (qkv_ref[c, :, at] for c in range(3))
        else:
            query, key, value = (dot(normed, w_ref[c, :, at]).astype(BF16) for c in range(3))
        outs = attend(query, key, value, bias_ref, group, part * group)
        for h, out in enumerate(outs):
            at = (part * group + h) * LANES
            attended[:, at : at + LANES] = out
    split_halves(second, dot(attended[...], wo_ref[...]), send_ref, keep_ref)


def split_halves(second, total, send_ref, keep_ref):
    send_ref[...] = own_half(1.0 - second, total).astype(BF16)
    keep_ref[...] = own_half(second, total)


def stash_kernel(skipped, x_ref, gain_ref, w_ref, *refs):
    *outs, normed = refs
    ticks, tokens = len(outs), x_ref.shape[1]
    for t in range(ticks):
        normed[t * tokens : (t + 1) * tokens] = rms_normed(x_ref[skipped + t], gain_ref[...])
    width = min(512, w_ref.shape[2])

    def step(i, carry):
        at = rows_at(i, width)
        for c in range(3):
            out = dot(normed[...], w_ref[c, :, at]).astype(BF16)
            for t in range(ticks):
                outs[t][c, :, at] = out[t * tokens : (t + 1) * tokens]
        return carry

    lax.fori_loop(0, w_ref.shape[2] // width, step, 0)


def probs_kernel(qkv_ref, bias_ref, out_ref):
    heads = bias_ref.shape[0]
    group = heads // 2
    scale = LANES ** (-0.5)

    def step(g, carry):
        at = rows_at(g, group * LANES)
        query, key = (qkv_ref[c, :, at] for c in range(2))
        for h in range(group):
            sl = slice(h * LANES, (h + 1) * LANES)
            out_ref[g * group + h] = probs_of(
                query[:, sl], key[:, sl], bias_ref[g * group + h], scale
            )
        return carry

    lax.fori_loop(0, 2, step, 0)


def grad_attend(g, qkv_ref, probs_ref, wo_ref, acc_in_ref, stacked, acc_ref, part):
    heads = probs_ref.shape[0] // 2
    scale = LANES ** (-0.5)
    at = slice(part * heads * LANES, (part + 1) * heads * LANES)
    grad_attn = dot(g, wo_ref[at], LAST).astype(BF16)
    for local in range(heads):
        h = part * heads + local
        own = slice(h * LANES, (h + 1) * LANES)
        q, k, v = (qkv_ref[c, :, own] for c in range(3))
        ga = grad_attn[:, local * LANES : (local + 1) * LANES]
        probs = probs_ref[h]
        grad_probs = dot(v, ga, LAST)
        total = jnp.sum(probs * grad_probs, axis=0, keepdims=True)
        grad_scores = probs * (grad_probs - total)
        grad16 = grad_scores.astype(BF16)
        if acc_in_ref is None:
            acc_ref[h] = grad_scores
        else:
            acc_ref[h] = acc_in_ref[h] + grad_scores
        stacked[0, :, own] = (dot(grad16, k, FIRST) * scale).astype(BF16)
        stacked[1, :, own] = (dot(grad16, q) * scale).astype(BF16)
        stacked[2, :, own] = dot(probs.astype(BF16), ga).astype(BF16)


def backward_kernel(first, flags_ref, *refs):
    second = flag(flags_ref, SECOND_CORE)
    if first:
        full_ref, qkv_ref, probs_ref, wo_ref, stacked, acc_ref, g_half_ref = refs
        acc_in_ref = None
        g = full_ref[...]
    else:
        mine_ref, other_ref, qkv_ref, probs_ref, wo_ref, acc_in_ref, *refs = refs
        stacked, acc_ref, g_half_ref = refs
        g = joined(second, mine_ref[...], other_ref[...]).astype(BF16)
    g_half_ref[...] = own_half(second, g).astype(BF16)
    for part in range(2):
        grad_attend(g, qkv_ref, probs_ref, wo_ref, acc_in_ref, stacked, acc_ref, part)


def input_gradient_kernel(flags_ref, stacked, w_ref, send_ref, keep_ref):
    total = dot(w_ref[0], stacked[0], LAST)
    total += dot(w_ref[1], stacked[1], LAST)
    total += dot(w_ref[2], stacked[2], LAST)
    split_halves(flag(flags_ref, SECOND_CORE), total.T, send_ref, keep_ref)


def pair_kernel(first_ref, second_ref, out_ref):
    out_ref[...] = (first_ref[...].astype(F32) + second_ref[...].astype(F32)).astype(BF16)


def up_term_kernel(flags_ref, keep_ref, received_ref, x_ref, out_ref):
    residual = flag(flags_ref, ADDS_RESIDUAL)
    total = keep_ref[...] + received_ref[...].astype(F32)
    out_ref[...] = (total + residual * x_ref[...].astype(F32)).astype(BF16)


def down_term_kernel(tick, flags_ref, stash_ref, gain_ref, keep_ref, received_ref, g_ref, out_ref):
    residual = flag(flags_ref, ADDS_RESIDUAL)
    x = own_half(flag(flags_ref, SECOND_CORE), stash_ref[tick])
    inverse = lax.rsqrt(jnp.mean(x * x, axis=-1, keepdims=True) + EPSILON)
    weighted = gain_ref[...] * (keep_ref[...] + received_ref[...].astype(F32))
    mean = jnp.mean(x * weighted, axis=-1, keepdims=True)
    cubed = inverse * inverse * inverse
    back = inverse * weighted - x * cubed * mean
    out_ref[...] = (residual * g_ref[...].astype(F32) + back).astype(BF16)


def choose_kernel(flags_ref, own_ref, first_ref, second_ref, out_ref):
    arrived = first_ref[...].astype(F32) + second_ref[...].astype(F32)
    own = flag(flags_ref, LAST_SECTION)
    out_ref[...] = pick(own, own_ref[...], arrived).astype(BF16)


def join_kernel(flags_ref, mine_ref, other_ref, out_ref, token_ref):
    second = flag(flags_ref, SECOND_CORE)
    out_ref[0] = joined(second, mine_ref[...], other_ref[...]).astype(BF16)
    token_ref[...] = jnp.zeros_like(token_ref)


def table_kernel(buckets_here, acc_ref, bucket_ref, out_ref, token_ref):
    heads, tokens, _ = acc_ref.shape
    rows = 8
    cells = heads * rows
    columns = buckets_here * rows
    total = jnp.zeros((cells, columns), F32)
    turned = bucket_ref[...].T
    for i in range(tokens // rows):
        at = slice(i * rows, (i + 1) * rows)
        ids = turned[at]
        hits = jnp.concatenate(
            [(ids == b).astype(F32) for b in range(buckets_here)], axis=0
        ).astype(BF16)
        part = acc_ref[:, at, :].reshape(cells, tokens)
        high = part.astype(BF16)
        low = (part - high.astype(F32)).astype(BF16)
        total += dot(high, hits, LAST) + dot(low, hits, LAST)
    row = lax.broadcasted_iota(jnp.int32, (cells, columns), 0)
    col = lax.broadcasted_iota(jnp.int32, (cells, columns), 1)
    total = jnp.where((row & (rows - 1)) == (col & (rows - 1)), total, 0.0)
    summed = jnp.sum(total.reshape(heads, rows, columns), axis=1)
    spread = lax.broadcasted_iota(jnp.int32, (columns, buckets_here), 0) >> 3
    bucket = lax.broadcasted_iota(jnp.int32, (columns, buckets_here), 1)
    fold = (spread == bucket).astype(F32)
    out_ref[...] = jnp.dot(
        summed, fold, preferred_element_type=F32, precision=lax.Precision.HIGHEST
    )
    token_ref[...] = jnp.zeros_like(token_ref)


def shape(dims, dtype=BF16):
    return jax.ShapeDtypeStruct(dims, dtype)


class Chain:
    def __init__(self):
        self.before = None

    def __call__(self, kernel, out_shape, args, scratch=(), limit=16):
        outs = out_shape if isinstance(out_shape, tuple) else (out_shape,)
        extra = () if self.before is None else (self.before,)
        count = len(args)

        def body(*refs):
            kernel(*refs[:count], *refs[count + len(extra) :])

        results = pl.pallas_call(
            body,
            out_shape=outs,
            in_specs=[WHOLE] * count + [UNREAD] * len(extra),
            out_specs=tuple(WHOLE for _ in outs),
            scratch_shapes=list(scratch),
            compiler_params=pltpu.CompilerParams(vmem_limit_bytes=limit * MIB),
            cost_estimate=pl.CostEstimate(flops=0, bytes_accessed=LANES, transcendentals=0),
        )(*args, *extra)
        self.before = results[-1]
        return results if isinstance(out_shape, tuple) else results[0]


def in_hbm(x):
    return pltpu.with_memory_space_constraint(x, pltpu.HBM)


def moved(block, step, bit):
    sections, heads = lax.axis_size("section"), lax.axis_size("head")
    route = [
        (s * heads + h, (s + step) % sections * heads + (h ^ bit))
        for s in range(sections)
        for h in range(heads)
    ]
    return lax.ppermute(block, ("section", "head"), route)


def swapped(block, bit):
    return lax.ppermute(block, "head", [(i, i ^ bit) for i in range(lax.axis_size("head"))])


def per_device(rising, falling, stash, queue, order, buckets, bias_table, gain, w_qkv, w_out):
    section_index = lax.axis_index("section")
    section_count = lax.axis_size("section")
    head_index = lax.axis_index("head")
    head_count = lax.axis_size("head")
    _, model_width, heads, _, head_dim = w_qkv.shape
    tokens = buckets.shape[0]
    half = tokens // 2
    inner = heads * head_dim
    facts = (
        head_index % 2 == 1,
        section_index == 0,
        section_index == section_count - 1,
        head_index < 2,
    )
    flags = jnp.broadcast_to(jnp.stack(facts).astype(F32)[:, None], (len(facts), LANES))
    table = bias_table[0].T
    back = w_out[0].reshape(inner, model_width)
    run = Chain()
    bits = [1 << b for b in range(1, head_count.bit_length() - 1)]
    cross = bits[-1]
    qkv_shape = shape((3, tokens, inner))
    scores_shape = shape((heads, tokens, tokens), F32)

    if heads % ROWS16 == 0:
        rows_first = jnp.transpose(w_qkv[0], (0, 2, 1, 3)).reshape(model_width, 3 * heads, head_dim)
        blocks = 2
        depth = model_width // blocks
        fixed = lambda rank: lambda c, b: (0,) * rank
        weights, qkv, kept_qkv, bias, wo, entering = pl.pallas_call(
            relayout_kernel,
            grid=(3, blocks),
            out_shape=(
                pltpu.VMEM((3, model_width, inner), BF16),
                qkv_shape,
                qkv_shape,
                scores_shape,
                pltpu.VMEM((inner, model_width), BF16),
                pltpu.VMEM((TICKS - 1, tokens, model_width), BF16),
            ),
            in_specs=[
                SCALARS,
                pl.BlockSpec((1, tokens, model_width), fixed(3)),
                pl.BlockSpec((1, 1, tokens, model_width), fixed(4)),
                pl.BlockSpec((1, model_width), fixed(2)),
                pl.BlockSpec(table.shape, fixed(2)),
                pl.BlockSpec((tokens, tokens), fixed(2)),
                pl.BlockSpec((depth, heads, head_dim), lambda c, b: (b, c, 0)),
                UNREAD,
                UNREAD,
                UNREAD,
            ],
            out_specs=(
                WHOLE,
                pl.BlockSpec((3, tokens, inner), fixed(3)),
                pl.BlockSpec((3, tokens, inner), fixed(3)),
                pl.BlockSpec((heads, tokens, tokens), fixed(3)),
                WHOLE,
                WHOLE,
            ),
            scratch_shapes=[pltpu.VMEM((2 * tokens, model_width), BF16), pltpu.SemaphoreType.DMA((TICKS,))],
            compiler_params=pltpu.CompilerParams(vmem_limit_bytes=24 * MIB),
            cost_estimate=pl.CostEstimate(
                flops=0, bytes_accessed=2 * w_qkv.size, transcendentals=0
            ),
        )(
            order, in_hbm(rising), in_hbm(stash), in_hbm(gain), in_hbm(table), in_hbm(buckets),
            in_hbm(rows_first), in_hbm(back), in_hbm(queue), flags,
        )
        run.before = qkv
    else:
        wo = back
        entering = jnp.stack(
            [lax.dynamic_index_in_dim(queue, order[t], 0, False) for t in range(TICKS - 1)]
        )
        weights = jnp.transpose(w_qkv[0], (2, 0, 1, 3)).reshape(3, model_width, inner)
        bias = run(bias_kernel, scores_shape, (table, buckets))
        qkv, kept_qkv = (
            run(
                functools.partial(stash_kernel, 0),
                qkv_shape,
                (rows, gain, weights),
                scratch=[pltpu.VMEM((tokens, model_width), BF16)],
            )
            for rows in (rising, stash[0, :1])
        )
    halves = (shape((half, model_width)), shape((half, model_width), F32))
    half_rows = shape((half, model_width))

    def but_last_bit(term):
        for bit in bits[:-1]:
            term = run(pair_kernel, half_rows, (term, swapped(term, bit)))
        return term

    def down_term(tick, keep, received, g_half):
        term = run(
            functools.partial(down_term_kernel, tick),
            half_rows,
            (flags, stash[0], gain, keep, received, g_half),
        )
        return but_last_bit(term)

    stashed = [kept_qkv]
    acc = ()
    for t in range(TICKS):
        final = t + 1 == TICKS
        scratch = [pltpu.VMEM((tokens, inner), BF16)]
        if t == 0:
            args = (flags, rising, qkv, bias, wo)
        else:
            x_other = swapped(x_mine, 1)
            fallen = down_term(t - 1, keep, received, g_half)
            arrivals = (lifted, moved(fallen, -1, 0), moved(fallen, -1, cross))
            args = (flags, x_mine, x_other, entering, gain, weights, bias, wo)
        up_send, up_keep, x_half = run(
            functools.partial(forward_kernel, t),
            halves + (half_rows,),
            args,
            scratch=scratch,
        )
        up_received = swapped(up_send, 1)
        if t > 0:
            stashed.append(
                run(
                    functools.partial(stash_kernel, t),
                    qkv_shape,
                    (stash[0], gain, weights),
                    scratch=[pltpu.VMEM((tokens, model_width), BF16)],
                )
            )
        probs = run(probs_kernel, scores_shape, (stashed[t], bias))
        if t == 0:
            g_parts = (falling[0],)
        else:
            g_mine = run(choose_kernel, half_rows, (flags,) + arrivals)
            g_parts = (g_mine, swapped(g_mine, 1))
        up = but_last_bit(
            run(up_term_kernel, half_rows, (flags, up_keep, up_received, x_half))
        )
        up_other = swapped(up, cross)

        stacked, acc_next, g_half = run(
            functools.partial(backward_kernel, t == 0),
            (shape((3, tokens, inner)), scores_shape, half_rows),
            (flags,) + g_parts + (stashed[t], probs, wo) + acc,
        )
        acc = (acc_next,)
        lifted = run(pair_kernel, half_rows, (up, up_other))
        x_mine = lifted if final else moved(lifted, 1, 0)
        send, keep = run(input_gradient_kernel, halves, (flags, stacked, weights))
        received = swapped(send, 1)

    x_other = swapped(x_mine, 1)
    rows = shape((1, tokens, model_width))
    fallen = down_term(TICKS - 1, keep, received, g_half)
    fallen_other = swapped(fallen, cross)
    token = shape((8, LANES), F32)
    rising_out, _ = run(join_kernel, (rows, token), (flags, x_mine, x_other))
    table_grad, _ = run(
        functools.partial(table_kernel, bias_table.shape[1]),
        (shape((heads, bias_table.shape[1]), F32), token),
        acc + (buckets,),
    )
    lowered = run(pair_kernel, half_rows, (fallen, fallen_other))
    falling_out, _ = run(join_kernel, (rows, token), (flags, lowered, swapped(lowered, 1)))
    return (rising_out, falling_out, table_grad.T[None])


def solution(mesh):
    return jax.shard_map(
        per_device,
        mesh=mesh,
        in_specs=(
            P(("groups", "section"), None, None),
            P(("groups", "section"), None, None),
            P(("groups", "section"), None, None, None),
            P("groups", None, None),
            P("groups"),
            P(),
            P("section", None, "head"),
            P("section", None),
            P("section", None, "head", None, None),
            P("section", "head", None, None),
        ),
        out_specs=(
            P(("groups", "section"), None, None),
            P(("groups", "section"), None, None),
            P(("groups", "section"), None, "head"),
        ),
        check_vma=False,
    )
```

```python
import functools

import jax
import jax.numpy as jnp
from jax import lax
from jax.experimental import pallas as pl
from jax.experimental.pallas import tpu as pltpu
from jax.sharding import PartitionSpec as P

TICKS = 3
EPSILON = 1e-06
LANES = 128
ROWS16 = 16
LAST = (((1,), (1,)), ((), ()))
FIRST = (((0,), (0,)), ((), ()))
F32 = jnp.float32
BF16 = jnp.bfloat16
WHOLE = pl.BlockSpec(memory_space=pltpu.VMEM)
SCALARS = pl.BlockSpec(memory_space=pltpu.SMEM)
UNREAD = pl.BlockSpec(memory_space=pl.ANY)
MIB = 1 << 20


def dot(a, b, dims=None):
    if dims is None:
        return jnp.dot(a, b, preferred_element_type=F32)
    return lax.dot_general(a, b, dims, preferred_element_type=F32)


def rms_normed(rows, gain_row):
    x = rows.astype(F32)
    inverse = lax.rsqrt(jnp.mean(x * x, axis=-1, keepdims=True) + EPSILON)
    return (x * inverse * gain_row).astype(BF16)


def rows_at(index, size):
    return pl.ds(pl.multiple_of(index * size, size), size)


SECOND_CORE, FIRST_SECTION, LAST_SECTION, ADDS_RESIDUAL = range(4)


def flag(flags_ref, row):
    return flags_ref[row : row + 1, :1]


def pick(chosen, yes, no):
    yes, no = yes.astype(F32), no.astype(F32)
    return jnp.where(jnp.broadcast_to(chosen, yes.shape) > 0.5, yes, no)


def joined(second, mine, other):
    return jnp.concatenate([pick(second, other, mine), pick(second, mine, other)], axis=0)


def own_half(second, rows):
    half = rows.shape[0] // 2
    return pick(second, rows[half:], rows[:half])


def fill_bias(table_ref, bucket_ref, bias_ref):
    ids = bucket_ref[...].T
    rows, count = table_ref.shape
    table = jnp.concatenate([table_ref[...], jnp.zeros((rows, LANES - count), F32)], axis=1)
    for h in range(rows):
        row = jnp.broadcast_to(table[h : h + 1], ids.shape)
        bias_ref[h] = jnp.take_along_axis(row, ids, axis=1)


def bias_kernel(table_ref, bucket_ref, bias_ref):
    fill_bias(table_ref, bucket_ref, bias_ref)


def relayout_kernel(
    order_ref, x_ref, kept_ref, gain_ref, table_ref, bucket_ref, w_ref, back_ref, queue_ref, _,
    w_out_ref, qkv_ref, kept_qkv_ref, bias_ref, back_out_ref, entering_ref, normed, arrived,
):
    which = pl.program_id(0)
    block = pl.program_id(1)
    entering = range(entering_ref.shape[0])
    copies = [pltpu.make_async_copy(back_ref, back_out_ref, arrived.at[len(entering)])] + [
        pltpu.make_async_copy(queue_ref.at[order_ref[t]], entering_ref.at[t], arrived.at[t])
        for t in entering
    ]

    @pl.when((which == 0) & (block == 0))
    def _():
        for copy in copies:
            copy.start()
        tokens = x_ref.shape[1]
        normed[:tokens] = rms_normed(x_ref[0], gain_ref[...])
        normed[tokens:] = rms_normed(kept_ref[0, 0], gain_ref[...])
        fill_bias(table_ref, bucket_ref, bias_ref)

    depth = w_ref.shape[0]
    size = ROWS16 * ROWS16
    row = lax.broadcasted_iota(jnp.int32, (size, size), 0)
    col = lax.broadcasted_iota(jnp.int32, (size, size), 1)
    wanted = (row & (ROWS16 - 1)) * ROWS16 + (row >> 4)
    permute = (col == wanted).astype(F32).astype(BF16)

    def step(i, carry):
        d0 = pl.multiple_of(i * 2 * ROWS16, 2 * ROWS16)
        first = w_ref[pl.ds(d0, ROWS16)].reshape(size, LANES)
        second = w_ref[pl.ds(d0 + ROWS16, ROWS16)].reshape(size, LANES)
        moved = dot(permute, jnp.concatenate([first, second], axis=1)).astype(BF16)
        to = pl.multiple_of(block * depth + d0, 2 * ROWS16)
        for h in range(ROWS16):
            piece = moved[h * ROWS16 : (h + 1) * ROWS16]
            lanes = slice(h * LANES, (h + 1) * LANES)
            w_out_ref[which, pl.ds(to, ROWS16), lanes] = piece[:, :LANES]
            w_out_ref[which, pl.ds(to + ROWS16, ROWS16), lanes] = piece[:, LANES:]
        return carry

    lax.fori_loop(0, depth // (2 * ROWS16), step, 0, unroll=32)

    @pl.when(block == pl.num_programs(1) - 1)
    def _():
        tokens = x_ref.shape[1]
        out = dot(normed[...], w_out_ref[which]).astype(BF16)
        qkv_ref[which] = out[:tokens]
        kept_qkv_ref[which] = out[tokens:]

    @pl.when((which == pl.num_programs(0) - 1) & (block == pl.num_programs(1) - 1))
    def _():
        for copy in copies:
            copy.wait()


def probs_of(query, key, bias, scale):
    scores = dot(key, query, LAST) * scale + bias
    raised = jnp.exp(scores - jnp.max(scores, axis=0, keepdims=True))
    return raised * (1.0 / jnp.sum(raised, axis=0, keepdims=True))


def attend(query, key, value, bias_ref, heads, first_head):
    scale = LANES ** (-0.5)
    lanes = [slice(h * LANES, (h + 1) * LANES) for h in range(heads)]
    probs = [
        probs_of(query[:, sl], key[:, sl], bias_ref[first_head + h], scale).astype(BF16)
        for h, sl in enumerate(lanes)
    ]
    return [dot(p, value[:, sl], FIRST).astype(BF16) for p, sl in zip(probs, lanes)]


def forward_kernel(tick, flags_ref, *refs):
    first = tick == 0
    if first:
        x_ref, qkv_ref, bias_ref, wo_ref, send_ref, keep_ref, x_half_ref, attended = refs
    else:
        (mine_ref, other_ref, entering_ref, gain_ref, w_ref, bias_ref, wo_ref,
         send_ref, keep_ref, x_half_ref, attended) = refs
    second = flag(flags_ref, SECOND_CORE)
    group = bias_ref.shape[0] // 2
    if first:
        x = x_ref[0]
    else:
        x = joined(second, mine_ref[...], other_ref[...])
        x = pick(flag(flags_ref, FIRST_SECTION), entering_ref[tick - 1], x)
        normed = rms_normed(x, gain_ref[...])
    x_half_ref[...] = own_half(second, x).astype(BF16)
    for part in range(2):
        at = slice(part * group * LANES, (part + 1) * group * LANES)
        if first:
            query, key, value = (qkv_ref[c, :, at] for c in range(3))
        else:
            query, key, value = (dot(normed, w_ref[c, :, at]).astype(BF16) for c in range(3))
        outs = attend(query, key, value, bias_ref, group, part * group)
        for h, out in enumerate(outs):
            at = (part * group + h) * LANES
            attended[:, at : at + LANES] = out
    split_halves(second, dot(attended[...], wo_ref[...]), send_ref, keep_ref)


def split_halves(second, total, send_ref, keep_ref):
    send_ref[...] = own_half(1.0 - second, total).astype(BF16)
    keep_ref[...] = own_half(second, total)


def stash_kernel(skipped, x_ref, gain_ref, w_ref, *refs):
    *outs, normed = refs
    ticks, tokens = len(outs), x_ref.shape[1]
    for t in range(ticks):
        normed[t * tokens : (t + 1) * tokens] = rms_normed(x_ref[skipped + t], gain_ref[...])
    width = min(512, w_ref.shape[2])

    def step(i, carry):
        at = rows_at(i, width)
        for c in range(3):
            out = dot(normed[...], w_ref[c, :, at]).astype(BF16)
            for t in range(ticks):
                outs[t][c, :, at] = out[t * tokens : (t + 1) * tokens]
        return carry

    lax.fori_loop(0, w_ref.shape[2] // width, step, 0)


def probs_kernel(qkv_ref, bias_ref, out_ref):
    heads = bias_ref.shape[0]
    group = heads // 2
    scale = LANES ** (-0.5)

    def step(g, carry):
        at = rows_at(g, group * LANES)
        query, key = (qkv_ref[c, :, at] for c in range(2))
        for h in range(group):
            sl = slice(h * LANES, (h + 1) * LANES)
            out_ref[g * group + h] = probs_of(
                query[:, sl], key[:, sl], bias_ref[g * group + h], scale
            )
        return carry

    lax.fori_loop(0, 2, step, 0)


def grad_attend(g, qkv_ref, probs_ref, wo_ref, acc_in_ref, stacked, acc_ref, part):
    heads = probs_ref.shape[0] // 2
    scale = LANES ** (-0.5)
    at = slice(part * heads * LANES, (part + 1) * heads * LANES)
    grad_attn = dot(g, wo_ref[at], LAST).astype(BF16)
    lanes = [slice(h * LANES, (h + 1) * LANES) for h in range(part * heads, (part + 1) * heads)]
    attn = [grad_attn[:, h * LANES : (h + 1) * LANES] for h in range(heads)]
    grad_probs = [dot(qkv_ref[2, :, own], ga, LAST) for own, ga in zip(lanes, attn)]
    halved = []
    for h, of_probs in enumerate(grad_probs, part * heads):
        probs = probs_ref[h]
        total = jnp.sum(probs * of_probs, axis=0, keepdims=True)
        grad_scores = probs * (of_probs - total)
        halved.append(grad_scores.astype(BF16))
        if acc_in_ref is None:
            acc_ref[h] = grad_scores
        else:
            acc_ref[h] = acc_in_ref[h] + grad_scores
    for h, (own, ga, grad16) in enumerate(zip(lanes, attn, halved), part * heads):
        stacked[0, :, own] = (dot(grad16, qkv_ref[1, :, own], FIRST) * scale).astype(BF16)
        stacked[1, :, own] = (dot(grad16, qkv_ref[0, :, own]) * scale).astype(BF16)
        stacked[2, :, own] = dot(probs_ref[h].astype(BF16), ga).astype(BF16)


def backward_kernel(first, flags_ref, *refs):
    second = flag(flags_ref, SECOND_CORE)
    if first:
        full_ref, qkv_ref, probs_ref, wo_ref, stacked, acc_ref, g_half_ref = refs
        acc_in_ref = None
        g = full_ref[...]
    else:
        mine_ref, other_ref, qkv_ref, probs_ref, wo_ref, acc_in_ref, *refs = refs
        stacked, acc_ref, g_half_ref = refs
        g = joined(second, mine_ref[...], other_ref[...]).astype(BF16)
    g_half_ref[...] = own_half(second, g).astype(BF16)
    for part in range(2):
        grad_attend(g, qkv_ref, probs_ref, wo_ref, acc_in_ref, stacked, acc_ref, part)


def input_gradient_kernel(flags_ref, stacked, w_ref, send_ref, keep_ref):
    total = dot(w_ref[0], stacked[0], LAST)
    total += dot(w_ref[1], stacked[1], LAST)
    total += dot(w_ref[2], stacked[2], LAST)
    split_halves(flag(flags_ref, SECOND_CORE), total.T, send_ref, keep_ref)


def pair_kernel(first_ref, second_ref, out_ref):
    out_ref[...] = (first_ref[...].astype(F32) + second_ref[...].astype(F32)).astype(BF16)


def up_term_kernel(flags_ref, keep_ref, received_ref, x_ref, out_ref):
    residual = flag(flags_ref, ADDS_RESIDUAL)
    total = keep_ref[...] + received_ref[...].astype(F32)
    out_ref[...] = (total + residual * x_ref[...].astype(F32)).astype(BF16)


def down_term_kernel(tick, flags_ref, stash_ref, gain_ref, keep_ref, received_ref, g_ref, out_ref):
    residual = flag(flags_ref, ADDS_RESIDUAL)
    x = own_half(flag(flags_ref, SECOND_CORE), stash_ref[tick])
    inverse = lax.rsqrt(jnp.mean(x * x, axis=-1, keepdims=True) + EPSILON)
    weighted = gain_ref[...] * (keep_ref[...] + received_ref[...].astype(F32))
    mean = jnp.mean(x * weighted, axis=-1, keepdims=True)
    cubed = inverse * inverse * inverse
    back = inverse * weighted - x * cubed * mean
    out_ref[...] = (residual * g_ref[...].astype(F32) + back).astype(BF16)


def choose_kernel(flags_ref, own_ref, first_ref, second_ref, out_ref):
    arrived = first_ref[...].astype(F32) + second_ref[...].astype(F32)
    own = flag(flags_ref, LAST_SECTION)
    out_ref[...] = pick(own, own_ref[...], arrived).astype(BF16)


def join_kernel(flags_ref, mine_ref, other_ref, out_ref, token_ref):
    second = flag(flags_ref, SECOND_CORE)
    out_ref[0] = joined(second, mine_ref[...], other_ref[...]).astype(BF16)
    token_ref[...] = jnp.zeros_like(token_ref)


def table_kernel(buckets_here, acc_ref, bucket_ref, out_ref, token_ref):
    heads, tokens, _ = acc_ref.shape
    rows = 8
    cells = heads * rows
    columns = buckets_here * rows
    total = jnp.zeros((cells, columns), F32)
    turned = bucket_ref[...].T
    for i in range(tokens // rows):
        at = slice(i * rows, (i + 1) * rows)
        ids = turned[at]
        hits = jnp.concatenate(
            [(ids == b).astype(F32) for b in range(buckets_here)], axis=0
        ).astype(BF16)
        part = acc_ref[:, at, :].reshape(cells, tokens)
        high = part.astype(BF16)
        low = (part - high.astype(F32)).astype(BF16)
        total += dot(high, hits, LAST) + dot(low, hits, LAST)
    row = lax.broadcasted_iota(jnp.int32, (cells, columns), 0)
    col = lax.broadcasted_iota(jnp.int32, (cells, columns), 1)
    total = jnp.where((row & (rows - 1)) == (col & (rows - 1)), total, 0.0)
    summed = jnp.sum(total.reshape(heads, rows, columns), axis=1)
    spread = lax.broadcasted_iota(jnp.int32, (columns, buckets_here), 0) >> 3
    bucket = lax.broadcasted_iota(jnp.int32, (columns, buckets_here), 1)
    fold = (spread == bucket).astype(F32)
    out_ref[...] = jnp.dot(
        summed, fold, preferred_element_type=F32, precision=lax.Precision.HIGHEST
    )
    token_ref[...] = jnp.zeros_like(token_ref)


def shape(dims, dtype=BF16):
    return jax.ShapeDtypeStruct(dims, dtype)


class Chain:
    def __init__(self):
        self.before = None

    def __call__(self, kernel, out_shape, args, scratch=(), limit=16):
        outs = out_shape if isinstance(out_shape, tuple) else (out_shape,)
        extra = () if self.before is None else (self.before,)
        count = len(args)

        def body(*refs):
            kernel(*refs[:count], *refs[count + len(extra) :])

        results = pl.pallas_call(
            body,
            out_shape=outs,
            in_specs=[WHOLE] * count + [UNREAD] * len(extra),
            out_specs=tuple(WHOLE for _ in outs),
            scratch_shapes=list(scratch),
            compiler_params=pltpu.CompilerParams(vmem_limit_bytes=limit * MIB),
            cost_estimate=pl.CostEstimate(flops=0, bytes_accessed=LANES, transcendentals=0),
        )(*args, *extra)
        self.before = results[-1]
        return results if isinstance(out_shape, tuple) else results[0]


def in_hbm(x):
    return pltpu.with_memory_space_constraint(x, pltpu.HBM)


def moved(block, step, bit):
    sections, heads = lax.axis_size("section"), lax.axis_size("head")
    route = [
        (s * heads + h, (s + step) % sections * heads + (h ^ bit))
        for s in range(sections)
        for h in range(heads)
    ]
    return lax.ppermute(block, ("section", "head"), route)


def swapped(block, bit):
    return lax.ppermute(block, "head", [(i, i ^ bit) for i in range(lax.axis_size("head"))])


def per_device(rising, falling, stash, queue, order, buckets, bias_table, gain, w_qkv, w_out):
    section_index = lax.axis_index("section")
    section_count = lax.axis_size("section")
    head_index = lax.axis_index("head")
    head_count = lax.axis_size("head")
    _, model_width, heads, _, head_dim = w_qkv.shape
    tokens = buckets.shape[0]
    half = tokens // 2
    inner = heads * head_dim
    facts = (
        head_index % 2 == 1,
        section_index == 0,
        section_index == section_count - 1,
        head_index < 2,
    )
    flags = jnp.broadcast_to(jnp.stack(facts).astype(F32)[:, None], (len(facts), LANES))
    table = bias_table[0].T
    back = w_out[0].reshape(inner, model_width)
    run = Chain()
    bits = [1 << b for b in range(1, head_count.bit_length() - 1)]
    cross = bits[-1]
    qkv_shape = shape((3, tokens, inner))
    scores_shape = shape((heads, tokens, tokens), F32)

    if heads % ROWS16 == 0:
        rows_first = jnp.transpose(w_qkv[0], (0, 2, 1, 3)).reshape(model_width, 3 * heads, head_dim)
        blocks = 1
        depth = model_width // blocks
        fixed = lambda rank: lambda c, b: (0,) * rank
        weights, qkv, kept_qkv, bias, wo, entering = pl.pallas_call(
            relayout_kernel,
            grid=(3, blocks),
            out_shape=(
                pltpu.VMEM((3, model_width, inner), BF16),
                qkv_shape,
                qkv_shape,
                scores_shape,
                pltpu.VMEM((inner, model_width), BF16),
                pltpu.VMEM((TICKS - 1, tokens, model_width), BF16),
            ),
            in_specs=[
                SCALARS,
                pl.BlockSpec((1, tokens, model_width), fixed(3)),
                pl.BlockSpec((1, 1, tokens, model_width), fixed(4)),
                pl.BlockSpec((1, model_width), fixed(2)),
                pl.BlockSpec(table.shape, fixed(2)),
                pl.BlockSpec((tokens, tokens), fixed(2)),
                pl.BlockSpec((depth, heads, head_dim), lambda c, b: (b, c, 0)),
                UNREAD,
                UNREAD,
                UNREAD,
            ],
            out_specs=(
                WHOLE,
                pl.BlockSpec((3, tokens, inner), fixed(3)),
                pl.BlockSpec((3, tokens, inner), fixed(3)),
                pl.BlockSpec((heads, tokens, tokens), fixed(3)),
                WHOLE,
                WHOLE,
            ),
            scratch_shapes=[pltpu.VMEM((2 * tokens, model_width), BF16), pltpu.SemaphoreType.DMA((TICKS,))],
            compiler_params=pltpu.CompilerParams(vmem_limit_bytes=24 * MIB),
            cost_estimate=pl.CostEstimate(
                flops=0, bytes_accessed=2 * w_qkv.size, transcendentals=0
            ),
        )(
            in_hbm(order), in_hbm(rising), in_hbm(stash), in_hbm(gain), in_hbm(table), in_hbm(buckets),
            in_hbm(rows_first), in_hbm(back), in_hbm(queue), flags,
        )
        run.before = qkv
    else:
        wo = back
        entering = jnp.stack(
            [lax.dynamic_index_in_dim(queue, order[t], 0, False) for t in range(TICKS - 1)]
        )
        weights = jnp.transpose(w_qkv[0], (2, 0, 1, 3)).reshape(3, model_width, inner)
        bias = run(bias_kernel, scores_shape, (table, buckets))
        qkv, kept_qkv = (
            run(
                functools.partial(stash_kernel, 0),
                qkv_shape,
                (rows, gain, weights),
                scratch=[pltpu.VMEM((tokens, model_width), BF16)],
            )
            for rows in (rising, stash[0, :1])
        )
    halves = (shape((half, model_width)), shape((half, model_width), F32))
    half_rows = shape((half, model_width))

    def but_last_bit(term):
        for bit in bits[:-1]:
            term = run(pair_kernel, half_rows, (term, swapped(term, bit)))
        return term

    def down_term(tick, keep, received, g_half):
        term = run(
            functools.partial(down_term_kernel, tick),
            half_rows,
            (flags, stash[0], gain, keep, received, g_half),
        )
        return but_last_bit(term)

    stashed = [kept_qkv]
    acc = ()
    for t in range(TICKS):
        final = t + 1 == TICKS
        scratch = [pltpu.VMEM((tokens, inner), BF16)]
        if t == 0:
            args = (flags, rising, qkv, bias, wo)
        else:
            x_other = swapped(x_mine, 1)
            fallen = down_term(t - 1, keep, received, g_half)
            arrivals = (lifted, moved(fallen, -1, 0), moved(fallen, -1, cross))
            args = (flags, x_mine, x_other, entering, gain, weights, bias, wo)
        up_send, up_keep, x_half = run(
            functools.partial(forward_kernel, t),
            halves + (half_rows,),
            args,
            scratch=scratch,
        )
        up_received = swapped(up_send, 1)
        if t > 0:
            stashed.append(
                run(
                    functools.partial(stash_kernel, t),
                    qkv_shape,
                    (stash[0], gain, weights),
                    scratch=[pltpu.VMEM((tokens, model_width), BF16)],
                )
            )
        probs = run(probs_kernel, scores_shape, (stashed[t], bias))
        if t == 0:
            g_parts = (falling[0],)
        else:
            g_mine = run(choose_kernel, half_rows, (flags,) + arrivals)
            g_parts = (g_mine, swapped(g_mine, 1))
        up = but_last_bit(
            run(up_term_kernel, half_rows, (flags, up_keep, up_received, x_half))
        )
        up_other = swapped(up, cross)

        stacked, acc_next, g_half = run(
            functools.partial(backward_kernel, t == 0),
            (shape((3, tokens, inner)), scores_shape, half_rows),
            (flags,) + g_parts + (stashed[t], probs, wo) + acc,
        )
        acc = (acc_next,)
        lifted = run(pair_kernel, half_rows, (up, up_other))
        x_mine = lifted if final else moved(lifted, 1, 0)
        send, keep = run(input_gradient_kernel, halves, (flags, stacked, weights))
        received = swapped(send, 1)

    x_other = swapped(x_mine, 1)
    rows = shape((1, tokens, model_width))
    fallen = down_term(TICKS - 1, keep, received, g_half)
    fallen_other = swapped(fallen, cross)
    token = shape((8, LANES), F32)
    rising_out, _ = run(join_kernel, (rows, token), (flags, x_mine, x_other))
    table_grad, _ = run(
        functools.partial(table_kernel, bias_table.shape[1]),
        (shape((heads, bias_table.shape[1]), F32), token),
        acc + (buckets,),
    )
    lowered = run(pair_kernel, half_rows, (fallen, fallen_other))
    falling_out, _ = run(join_kernel, (rows, token), (flags, lowered, swapped(lowered, 1)))
    return (rising_out, falling_out, table_grad.T[None])


def solution(mesh):
    return jax.shard_map(
        per_device,
        mesh=mesh,
        in_specs=(
            P(("groups", "section"), None, None),
            P(("groups", "section"), None, None),
            P(("groups", "section"), None, None, None),
            P("groups", None, None),
            P("groups"),
            P(),
            P("section", None, "head"),
            P("section", None),
            P("section", None, "head", None, None),
            P("section", "head", None, None),
        ),
        out_specs=(
            P(("groups", "section"), None, None),
            P(("groups", "section"), None, None),
            P(("groups", "section"), None, "head"),
        ),
        check_vma=False,
    )
```

```python
import functools

import jax
import jax.numpy as jnp
from jax import lax
from jax.experimental import pallas as pl
from jax.experimental.pallas import tpu as pltpu
from jax.sharding import PartitionSpec as P

TICKS = 3
EPSILON = 1e-06
LANES = 128
ROWS16 = 16
LAST = (((1,), (1,)), ((), ()))
FIRST = (((0,), (0,)), ((), ()))
F32 = jnp.float32
BF16 = jnp.bfloat16
WHOLE = pl.BlockSpec(memory_space=pltpu.VMEM)
SCALARS = pl.BlockSpec(memory_space=pltpu.SMEM)
UNREAD = pl.BlockSpec(memory_space=pl.ANY)
MIB = 1 << 20


def dot(a, b, dims=None):
    if dims is None:
        return jnp.dot(a, b, preferred_element_type=F32)
    return lax.dot_general(a, b, dims, preferred_element_type=F32)


def rms_normed(rows, gain_row):
    x = rows.astype(F32)
    inverse = lax.rsqrt(jnp.mean(x * x, axis=-1, keepdims=True) + EPSILON)
    return (x * inverse * gain_row).astype(BF16)


def rows_at(index, size):
    return pl.ds(pl.multiple_of(index * size, size), size)


SECOND_CORE, FIRST_SECTION, LAST_SECTION, ADDS_RESIDUAL = range(4)


def flag(flags_ref, row):
    return flags_ref[row : row + 1, :1]


def pick(chosen, yes, no):
    yes, no = yes.astype(F32), no.astype(F32)
    return jnp.where(jnp.broadcast_to(chosen, yes.shape) > 0.5, yes, no)


def joined(second, mine, other):
    return jnp.concatenate([pick(second, other, mine), pick(second, mine, other)], axis=0)


def own_half(second, rows):
    half = rows.shape[0] // 2
    return pick(second, rows[half:], rows[:half])


def fill_bias(table_ref, bucket_ref, bias_ref):
    ids = bucket_ref[...].T
    rows, count = table_ref.shape
    table = jnp.concatenate([table_ref[...], jnp.zeros((rows, LANES - count), F32)], axis=1)
    for h in range(rows):
        row = jnp.broadcast_to(table[h : h + 1], ids.shape)
        bias_ref[h] = jnp.take_along_axis(row, ids, axis=1)


def bias_kernel(table_ref, bucket_ref, bias_ref):
    fill_bias(table_ref, bucket_ref, bias_ref)


def relayout_kernel(
    order_ref, x_ref, kept_ref, gain_ref, table_ref, bucket_ref, w_ref, back_ref, queue_ref, _,
    w_out_ref, qkv_ref, kept_qkv_ref, bias_ref, back_out_ref, entering_ref, normed, arrived,
):
    which = pl.program_id(0)
    block = pl.program_id(1)
    entering = range(entering_ref.shape[0])
    copies = [pltpu.make_async_copy(back_ref, back_out_ref, arrived.at[len(entering)])] + [
        pltpu.make_async_copy(queue_ref.at[order_ref[t]], entering_ref.at[t], arrived.at[t])
        for t in entering
    ]

    @pl.when((which == 0) & (block == 0))
    def _():
        for copy in copies:
            copy.start()
        tokens = x_ref.shape[1]
        normed[:tokens] = rms_normed(x_ref[0], gain_ref[...])
        normed[tokens:] = rms_normed(kept_ref[0, 0], gain_ref[...])
        fill_bias(table_ref, bucket_ref, bias_ref)

    depth = w_ref.shape[0]
    size = ROWS16 * ROWS16
    row = lax.broadcasted_iota(jnp.int32, (size, size), 0)
    col = lax.broadcasted_iota(jnp.int32, (size, size), 1)
    wanted = (row & (ROWS16 - 1)) * ROWS16 + (row >> 4)
    permute = (col == wanted).astype(F32).astype(BF16)

    def step(i, carry):
        d0 = pl.multiple_of(i * 2 * ROWS16, 2 * ROWS16)
        first = w_ref[pl.ds(d0, ROWS16)].reshape(size, LANES)
        second = w_ref[pl.ds(d0 + ROWS16, ROWS16)].reshape(size, LANES)
        moved = dot(permute, jnp.concatenate([first, second], axis=1)).astype(BF16)
        to = pl.multiple_of(block * depth + d0, 2 * ROWS16)
        for h in range(ROWS16):
            piece = moved[h * ROWS16 : (h + 1) * ROWS16]
            lanes = slice(h * LANES, (h + 1) * LANES)
            w_out_ref[which, pl.ds(to, ROWS16), lanes] = piece[:, :LANES]
            w_out_ref[which, pl.ds(to + ROWS16, ROWS16), lanes] = piece[:, LANES:]
        return carry

    lax.fori_loop(0, depth // (2 * ROWS16), step, 0, unroll=32)

    @pl.when(block == pl.num_programs(1) - 1)
    def _():
        tokens = x_ref.shape[1]
        out = dot(normed[...], w_out_ref[which]).astype(BF16)
        qkv_ref[which] = out[:tokens]
        kept_qkv_ref[which] = out[tokens:]

    @pl.when((which == pl.num_programs(0) - 1) & (block == pl.num_programs(1) - 1))
    def _():
        for copy in copies:
            copy.wait()


def probs_of(query, key, bias, scale):
    scores = dot(key, query, LAST) * scale + bias
    raised = jnp.exp(scores - jnp.max(scores, axis=0, keepdims=True))
    return raised * (1.0 / jnp.sum(raised, axis=0, keepdims=True))


def attend(query, key, value, bias_ref, heads, first_head):
    scale = LANES ** (-0.5)
    lanes = [slice(h * LANES, (h + 1) * LANES) for h in range(heads)]
    probs = [
        probs_of(query[:, sl], key[:, sl], bias_ref[first_head + h], scale).astype(BF16)
        for h, sl in enumerate(lanes)
    ]
    return [dot(p, value[:, sl], FIRST).astype(BF16) for p, sl in zip(probs, lanes)]


def forward_kernel(tick, flags_ref, *refs):
    first = tick == 0
    if first:
        x_ref, qkv_ref, bias_ref, wo_ref, send_ref, keep_ref, x_half_ref, attended = refs
    else:
        (mine_ref, other_ref, entering_ref, gain_ref, w_ref, bias_ref, wo_ref,
         send_ref, keep_ref, x_half_ref, attended) = refs
    second = flag(flags_ref, SECOND_CORE)
    group = bias_ref.shape[0] // 2
    if first:
        x = x_ref[0]
    else:
        x = joined(second, mine_ref[...], other_ref[...])
        x = pick(flag(flags_ref, FIRST_SECTION), entering_ref[tick - 1], x)
        normed = rms_normed(x, gain_ref[...])
    x_half_ref[...] = own_half(second, x).astype(BF16)
    for part in range(2):
        at = slice(part * group * LANES, (part + 1) * group * LANES)
        if first:
            query, key, value = (qkv_ref[c, :, at] for c in range(3))
        else:
            query, key, value = (dot(normed, w_ref[c, :, at]).astype(BF16) for c in range(3))
        outs = attend(query, key, value, bias_ref, group, part * group)
        for h, out in enumerate(outs):
            at = (part * group + h) * LANES
            attended[:, at : at + LANES] = out
    split_halves(second, dot(attended[...], wo_ref[...]), send_ref, keep_ref)


def split_halves(second, total, send_ref, keep_ref):
    send_ref[...] = own_half(1.0 - second, total).astype(BF16)
    keep_ref[...] = own_half(second, total)


def stash_kernel(skipped, x_ref, gain_ref, w_ref, *refs):
    *outs, normed = refs
    ticks, tokens = len(outs), x_ref.shape[1]
    for t in range(ticks):
        normed[t * tokens : (t + 1) * tokens] = rms_normed(x_ref[skipped + t], gain_ref[...])
    width = min(512, w_ref.shape[2])

    def step(i, carry):
        at = rows_at(i, width)
        for c in range(3):
            out = dot(normed[...], w_ref[c, :, at]).astype(BF16)
            for t in range(ticks):
                outs[t][c, :, at] = out[t * tokens : (t + 1) * tokens]
        return carry

    lax.fori_loop(0, w_ref.shape[2] // width, step, 0)


def probs_kernel(qkv_ref, bias_ref, out_ref):
    heads = bias_ref.shape[0]
    group = heads // 2
    scale = LANES ** (-0.5)

    def step(g, carry):
        at = rows_at(g, group * LANES)
        query, key = (qkv_ref[c, :, at] for c in range(2))
        for h in range(group):
            sl = slice(h * LANES, (h + 1) * LANES)
            out_ref[g * group + h] = probs_of(
                query[:, sl], key[:, sl], bias_ref[g * group + h], scale
            )
        return carry

    lax.fori_loop(0, 2, step, 0)


def grad_attend(g, qkv_ref, probs_ref, wo_ref, acc_in_ref, stacked, acc_ref, part):
    heads = probs_ref.shape[0] // 2
    scale = LANES ** (-0.5)
    at = slice(part * heads * LANES, (part + 1) * heads * LANES)
    grad_attn = dot(g, wo_ref[at], LAST).astype(BF16)
    lanes = [slice(h * LANES, (h + 1) * LANES) for h in range(part * heads, (part + 1) * heads)]
    attn = [grad_attn[:, h * LANES : (h + 1) * LANES] for h in range(heads)]
    grad_probs = [dot(qkv_ref[2, :, own], ga, LAST) for own, ga in zip(lanes, attn)]
    halved = []
    for h, of_probs in enumerate(grad_probs, part * heads):
        probs = probs_ref[h]
        total = jnp.sum(probs * of_probs, axis=0, keepdims=True)
        grad_scores = probs * (of_probs - total)
        halved.append(grad_scores.astype(BF16))
        if acc_in_ref is None:
            acc_ref[h] = grad_scores
        else:
            acc_ref[h] = acc_in_ref[h] + grad_scores
    for h, (own, ga, grad16) in enumerate(zip(lanes, attn, halved), part * heads):
        stacked[0, :, own] = (dot(grad16, qkv_ref[1, :, own], FIRST) * scale).astype(BF16)
        stacked[1, :, own] = (dot(grad16, qkv_ref[0, :, own]) * scale).astype(BF16)
        stacked[2, :, own] = dot(probs_ref[h].astype(BF16), ga).astype(BF16)


def backward_kernel(first, flags_ref, *refs):
    second = flag(flags_ref, SECOND_CORE)
    if first:
        full_ref, qkv_ref, probs_ref, wo_ref, stacked, acc_ref, g_half_ref = refs
        acc_in_ref = None
        g = full_ref[...]
    else:
        mine_ref, other_ref, qkv_ref, probs_ref, wo_ref, acc_in_ref, *refs = refs
        stacked, acc_ref, g_half_ref = refs
        g = joined(second, mine_ref[...], other_ref[...]).astype(BF16)
    g_half_ref[...] = own_half(second, g).astype(BF16)
    for part in range(2):
        grad_attend(g, qkv_ref, probs_ref, wo_ref, acc_in_ref, stacked, acc_ref, part)


def input_gradient_kernel(flags_ref, stacked, w_ref, send_ref, keep_ref):
    total = dot(w_ref[0], stacked[0], LAST)
    total += dot(w_ref[1], stacked[1], LAST)
    total += dot(w_ref[2], stacked[2], LAST)
    split_halves(flag(flags_ref, SECOND_CORE), total.T, send_ref, keep_ref)


def pair_kernel(first_ref, second_ref, out_ref):
    out_ref[...] = (first_ref[...].astype(F32) + second_ref[...].astype(F32)).astype(BF16)


def up_term_kernel(flags_ref, keep_ref, received_ref, x_ref, out_ref):
    residual = flag(flags_ref, ADDS_RESIDUAL)
    total = keep_ref[...] + received_ref[...].astype(F32)
    out_ref[...] = (total + residual * x_ref[...].astype(F32)).astype(BF16)


def down_term_kernel(tick, flags_ref, stash_ref, gain_ref, keep_ref, received_ref, g_ref, out_ref):
    residual = flag(flags_ref, ADDS_RESIDUAL)
    x = own_half(flag(flags_ref, SECOND_CORE), stash_ref[tick])
    inverse = lax.rsqrt(jnp.mean(x * x, axis=-1, keepdims=True) + EPSILON)
    weighted = gain_ref[...] * (keep_ref[...] + received_ref[...].astype(F32))
    mean = jnp.mean(x * weighted, axis=-1, keepdims=True)
    cubed = inverse * inverse * inverse
    back = inverse * weighted - x * cubed * mean
    out_ref[...] = (residual * g_ref[...].astype(F32) + back).astype(BF16)


def choose_kernel(flags_ref, own_ref, first_ref, second_ref, out_ref):
    arrived = first_ref[...].astype(F32) + second_ref[...].astype(F32)
    own = flag(flags_ref, LAST_SECTION)
    out_ref[...] = pick(own, own_ref[...], arrived).astype(BF16)


def join_kernel(flags_ref, mine_ref, other_ref, out_ref, token_ref):
    second = flag(flags_ref, SECOND_CORE)
    out_ref[0] = joined(second, mine_ref[...], other_ref[...]).astype(BF16)
    token_ref[...] = jnp.zeros_like(token_ref)


def table_kernel(buckets_here, acc_ref, bucket_ref, out_ref, token_ref):
    heads, tokens, _ = acc_ref.shape
    rows = 8
    cells = heads * rows
    columns = buckets_here * rows
    total = jnp.zeros((cells, columns), F32)
    turned = bucket_ref[...].T
    for i in range(tokens // rows):
        at = slice(i * rows, (i + 1) * rows)
        ids = turned[at]
        hits = jnp.concatenate(
            [(ids == b).astype(F32) for b in range(buckets_here)], axis=0
        ).astype(BF16)
        part = acc_ref[:, at, :].reshape(cells, tokens)
        high = part.astype(BF16)
        low = (part - high.astype(F32)).astype(BF16)
        total += dot(high, hits, LAST) + dot(low, hits, LAST)
    row = lax.broadcasted_iota(jnp.int32, (cells, columns), 0)
    col = lax.broadcasted_iota(jnp.int32, (cells, columns), 1)
    total = jnp.where((row & (rows - 1)) == (col & (rows - 1)), total, 0.0)
    summed = jnp.sum(total.reshape(heads, rows, columns), axis=1)
    spread = lax.broadcasted_iota(jnp.int32, (columns, buckets_here), 0) >> 3
    bucket = lax.broadcasted_iota(jnp.int32, (columns, buckets_here), 1)
    fold = (spread == bucket).astype(F32)
    out_ref[...] = jnp.dot(
        summed, fold, preferred_element_type=F32, precision=lax.Precision.HIGHEST
    )
    token_ref[...] = jnp.zeros_like(token_ref)


def shape(dims, dtype=BF16):
    return jax.ShapeDtypeStruct(dims, dtype)


class Chain:
    def __init__(self):
        self.before = None

    def __call__(self, kernel, out_shape, args, scratch=(), limit=16):
        outs = out_shape if isinstance(out_shape, tuple) else (out_shape,)
        extra = () if self.before is None else (self.before,)
        count = len(args)

        def body(*refs):
            kernel(*refs[:count], *refs[count + len(extra) :])

        results = pl.pallas_call(
            body,
            out_shape=outs,
            in_specs=[WHOLE] * count + [UNREAD] * len(extra),
            out_specs=tuple(WHOLE for _ in outs),
            scratch_shapes=list(scratch),
            compiler_params=pltpu.CompilerParams(vmem_limit_bytes=limit * MIB),
            cost_estimate=pl.CostEstimate(flops=0, bytes_accessed=LANES, transcendentals=0),
        )(*args, *extra)
        self.before = results[-1]
        return results if isinstance(out_shape, tuple) else results[0]


def in_hbm(x):
    return pltpu.with_memory_space_constraint(x, pltpu.HBM)


def moved(block, step, bit):
    sections, heads = lax.axis_size("section"), lax.axis_size("head")
    route = [
        (s * heads + h, (s + step) % sections * heads + (h ^ bit))
        for s in range(sections)
        for h in range(heads)
    ]
    return lax.ppermute(block, ("section", "head"), route)


def swapped(block, bit):
    return lax.ppermute(block, "head", [(i, i ^ bit) for i in range(lax.axis_size("head"))])


def per_device(rising, falling, stash, queue, order, buckets, bias_table, gain, w_qkv, w_out):
    section_index = lax.axis_index("section")
    section_count = lax.axis_size("section")
    head_index = lax.axis_index("head")
    head_count = lax.axis_size("head")
    _, model_width, heads, _, head_dim = w_qkv.shape
    tokens = buckets.shape[0]
    half = tokens // 2
    inner = heads * head_dim
    facts = (
        head_index % 2 == 1,
        section_index == 0,
        section_index == section_count - 1,
        head_index < 2,
    )
    flags = jnp.broadcast_to(jnp.stack(facts).astype(F32)[:, None], (len(facts), LANES))
    table = bias_table[0].T
    back = w_out[0].reshape(inner, model_width)
    run = Chain()
    bits = [1 << b for b in range(1, head_count.bit_length() - 1)]
    cross = bits[-1]
    qkv_shape = shape((3, tokens, inner))
    scores_shape = shape((heads, tokens, tokens), F32)

    if heads % ROWS16 == 0:
        rows_first = jnp.transpose(w_qkv[0], (0, 2, 1, 3)).reshape(model_width, 3 * heads, head_dim)
        blocks = 1
        depth = model_width // blocks
        fixed = lambda rank: lambda c, b: (0,) * rank
        weights, qkv, kept_qkv, bias, wo, entering = pl.pallas_call(
            relayout_kernel,
            grid=(3, blocks),
            out_shape=(
                pltpu.VMEM((3, model_width, inner), BF16),
                qkv_shape,
                qkv_shape,
                scores_shape,
                pltpu.VMEM((inner, model_width), BF16),
                pltpu.VMEM((TICKS - 1, tokens, model_width), BF16),
            ),
            in_specs=[
                SCALARS,
                pl.BlockSpec((1, tokens, model_width), fixed(3)),
                pl.BlockSpec((1, 1, tokens, model_width), fixed(4)),
                pl.BlockSpec((1, model_width), fixed(2)),
                pl.BlockSpec(table.shape, fixed(2)),
                pl.BlockSpec((tokens, tokens), fixed(2)),
                pl.BlockSpec((depth, heads, head_dim), lambda c, b: (b, c, 0)),
                UNREAD,
                UNREAD,
                UNREAD,
            ],
            out_specs=(
                WHOLE,
                pl.BlockSpec((3, tokens, inner), fixed(3)),
                pl.BlockSpec((3, tokens, inner), fixed(3)),
                pl.BlockSpec((heads, tokens, tokens), fixed(3)),
                WHOLE,
                WHOLE,
            ),
            scratch_shapes=[pltpu.VMEM((2 * tokens, model_width), BF16), pltpu.SemaphoreType.DMA((TICKS,))],
            compiler_params=pltpu.CompilerParams(vmem_limit_bytes=24 * MIB),
            cost_estimate=pl.CostEstimate(
                flops=0, bytes_accessed=2 * w_qkv.size, transcendentals=0
            ),
        )(
            in_hbm(order), in_hbm(rising), in_hbm(stash), in_hbm(gain), in_hbm(table), in_hbm(buckets),
            in_hbm(rows_first), in_hbm(back), in_hbm(queue), flags,
        )
        run.before = qkv
    else:
        wo = back
        entering = jnp.stack(
            [lax.dynamic_index_in_dim(queue, order[t], 0, False) for t in range(TICKS - 1)]
        )
        weights = jnp.transpose(w_qkv[0], (2, 0, 1, 3)).reshape(3, model_width, inner)
        bias = run(bias_kernel, scores_shape, (table, buckets))
        qkv, kept_qkv = (
            run(
                functools.partial(stash_kernel, 0),
                qkv_shape,
                (rows, gain, weights),
                scratch=[pltpu.VMEM((tokens, model_width), BF16)],
            )
            for rows in (rising, stash[0, :1])
        )
    halves = (shape((half, model_width)), shape((half, model_width), F32))
    half_rows = shape((half, model_width))

    def but_last_bit(term):
        for bit in bits[:-1]:
            term = run(pair_kernel, half_rows, (term, swapped(term, bit)))
        return term

    def down_term(tick, keep, received, g_half):
        term = run(
            functools.partial(down_term_kernel, tick),
            half_rows,
            (flags, stash[0], gain, keep, received, g_half),
        )
        return but_last_bit(term)

    stashed = [kept_qkv]
    acc = ()
    for t in range(TICKS):
        final = t + 1 == TICKS
        scratch = [pltpu.VMEM((tokens, inner), BF16)]
        if t == 0:
            args = (flags, rising, qkv, bias, wo)
        else:
            x_other = swapped(x_mine, 1)
            fallen = down_term(t - 1, keep, received, g_half)
            arrivals = (lifted, moved(fallen, -1, 0), moved(fallen, -1, cross))
            args = (flags, x_mine, x_other, entering, gain, weights, bias, wo)
        up_send, up_keep, x_half = run(
            functools.partial(forward_kernel, t),
            halves + (half_rows,),
            args,
            scratch=scratch,
        )
        up_received = swapped(up_send, 1)
        if t > 0:
            stashed.append(
                run(
                    functools.partial(stash_kernel, t),
                    qkv_shape,
                    (stash[0], gain, weights),
                    scratch=[pltpu.VMEM((tokens, model_width), BF16)],
                )
            )
        probs = run(probs_kernel, scores_shape, (stashed[t], bias))
        if t == 0:
            g_parts = (falling[0],)
        else:
            g_mine = run(choose_kernel, half_rows, (flags,) + arrivals)
            g_parts = (g_mine, swapped(g_mine, 1))
        up = but_last_bit(
            run(up_term_kernel, half_rows, (flags, up_keep, up_received, x_half))
        )
        up_other = swapped(up, cross)

        stacked, acc_next, g_half = run(
            functools.partial(backward_kernel, t == 0),
            (shape((3, tokens, inner)), scores_shape, half_rows),
            (flags,) + g_parts + (stashed[t], probs, wo) + acc,
        )
        acc = (acc_next,)
        if not final:
            lifted = run(pair_kernel, half_rows, (up, up_other))
            x_mine = moved(lifted, 1, 0)
        send, keep = run(input_gradient_kernel, halves, (flags, stacked, weights))
        received = swapped(send, 1)
        if final:
            x_mine = run(pair_kernel, half_rows, (up, up_other))

    x_other = swapped(x_mine, 1)
    rows = shape((1, tokens, model_width))
    fallen = down_term(TICKS - 1, keep, received, g_half)
    fallen_other = swapped(fallen, cross)
    token = shape((8, LANES), F32)
    rising_out, _ = run(join_kernel, (rows, token), (flags, x_mine, x_other))
    table_grad, _ = run(
        functools.partial(table_kernel, bias_table.shape[1]),
        (shape((heads, bias_table.shape[1]), F32), token),
        acc + (buckets,),
    )
    lowered = run(pair_kernel, half_rows, (fallen, fallen_other))
    falling_out, _ = run(join_kernel, (rows, token), (flags, lowered, swapped(lowered, 1)))
    return (rising_out, falling_out, table_grad.T[None])


def solution(mesh):
    return jax.shard_map(
        per_device,
        mesh=mesh,
        in_specs=(
            P(("groups", "section"), None, None),
            P(("groups", "section"), None, None),
            P(("groups", "section"), None, None, None),
            P("groups", None, None),
            P("groups"),
            P(),
            P("section", None, "head"),
            P("section", None),
            P("section", None, "head", None, None),
            P("section", "head", None, None),
        ),
        out_specs=(
            P(("groups", "section"), None, None),
            P(("groups", "section"), None, None),
            P(("groups", "section"), None, "head"),
        ),
        check_vma=False,
    )
```

```python
import functools

import jax
import jax.numpy as jnp
from jax import lax
from jax.experimental import pallas as pl
from jax.experimental.pallas import tpu as pltpu
from jax.sharding import PartitionSpec as P

TICKS = 3
EPSILON = 1e-06
LANES = 128
ROWS16 = 16
LAST = (((1,), (1,)), ((), ()))
FIRST = (((0,), (0,)), ((), ()))
F32 = jnp.float32
BF16 = jnp.bfloat16
WHOLE = pl.BlockSpec(memory_space=pltpu.VMEM)
SCALARS = pl.BlockSpec(memory_space=pltpu.SMEM)
UNREAD = pl.BlockSpec(memory_space=pl.ANY)
MIB = 1 << 20


def dot(a, b, dims=None):
    if dims is None:
        return jnp.dot(a, b, preferred_element_type=F32)
    return lax.dot_general(a, b, dims, preferred_element_type=F32)


def rms_normed(rows, gain_row):
    x = rows.astype(F32)
    inverse = lax.rsqrt(jnp.mean(x * x, axis=-1, keepdims=True) + EPSILON)
    return (x * inverse * gain_row).astype(BF16)


def rows_at(index, size):
    return pl.ds(pl.multiple_of(index * size, size), size)


SECOND_CORE, FIRST_SECTION, LAST_SECTION, ADDS_RESIDUAL = range(4)


def flag(flags_ref, row):
    return flags_ref[row : row + 1, :1]


def pick(chosen, yes, no):
    yes, no = yes.astype(F32), no.astype(F32)
    return jnp.where(jnp.broadcast_to(chosen, yes.shape) > 0.5, yes, no)


def joined(second, mine, other):
    return jnp.concatenate([pick(second, other, mine), pick(second, mine, other)], axis=0)


def own_half(second, rows):
    half = rows.shape[0] // 2
    return pick(second, rows[half:], rows[:half])


def fill_bias(table_ref, bucket_ref, bias_ref):
    ids = bucket_ref[...].T
    rows, count = table_ref.shape
    table = jnp.concatenate([table_ref[...], jnp.zeros((rows, LANES - count), F32)], axis=1)
    for h in range(rows):
        row = jnp.broadcast_to(table[h : h + 1], ids.shape)
        bias_ref[h] = jnp.take_along_axis(row, ids, axis=1)


def bias_kernel(table_ref, bucket_ref, bias_ref):
    fill_bias(table_ref, bucket_ref, bias_ref)


def relayout_kernel(
    order_ref, x_ref, kept_ref, gain_ref, table_ref, bucket_ref, w_ref, back_ref, queue_ref, _,
    w_out_ref, qkv_ref, kept_qkv_ref, bias_ref, back_out_ref, entering_ref, normed, arrived,
):
    which = pl.program_id(0)
    block = pl.program_id(1)
    entering = range(entering_ref.shape[0])
    copies = [pltpu.make_async_copy(back_ref, back_out_ref, arrived.at[len(entering)])] + [
        pltpu.make_async_copy(queue_ref.at[order_ref[t]], entering_ref.at[t], arrived.at[t])
        for t in entering
    ]

    @pl.when((which == 0) & (block == 0))
    def _():
        for copy in copies:
            copy.start()
        tokens = x_ref.shape[1]
        normed[:tokens] = rms_normed(x_ref[0], gain_ref[...])
        normed[tokens:] = rms_normed(kept_ref[0, 0], gain_ref[...])
        fill_bias(table_ref, bucket_ref, bias_ref)

    depth = w_ref.shape[0]
    size = ROWS16 * ROWS16
    row = lax.broadcasted_iota(jnp.int32, (size, size), 0)
    col = lax.broadcasted_iota(jnp.int32, (size, size), 1)
    wanted = (row & (ROWS16 - 1)) * ROWS16 + (row >> 4)
    permute = (col == wanted).astype(F32).astype(BF16)

    def step(i, carry):
        d0 = pl.multiple_of(i * 2 * ROWS16, 2 * ROWS16)
        first = w_ref[pl.ds(d0, ROWS16)].reshape(size, LANES)
        second = w_ref[pl.ds(d0 + ROWS16, ROWS16)].reshape(size, LANES)
        moved = dot(permute, jnp.concatenate([first, second], axis=1)).astype(BF16)
        to = pl.multiple_of(block * depth + d0, 2 * ROWS16)
        for h in range(ROWS16):
            piece = moved[h * ROWS16 : (h + 1) * ROWS16]
            lanes = slice(h * LANES, (h + 1) * LANES)
            w_out_ref[which, pl.ds(to, ROWS16), lanes] = piece[:, :LANES]
            w_out_ref[which, pl.ds(to + ROWS16, ROWS16), lanes] = piece[:, LANES:]
        return carry

    lax.fori_loop(0, depth // (2 * ROWS16), step, 0, unroll=32)

    @pl.when(block == pl.num_programs(1) - 1)
    def _():
        tokens = x_ref.shape[1]
        out = dot(normed[...], w_out_ref[which]).astype(BF16)
        qkv_ref[which] = out[:tokens]
        kept_qkv_ref[which] = out[tokens:]

    @pl.when((which == pl.num_programs(0) - 1) & (block == pl.num_programs(1) - 1))
    def _():
        for copy in copies:
            copy.wait()


def probs_of(query, key, bias, scale):
    scores = dot(key, query, LAST) * scale + bias
    raised = jnp.exp(scores - jnp.max(scores, axis=0, keepdims=True))
    return raised * (1.0 / jnp.sum(raised, axis=0, keepdims=True))


def attend(query, key, value, bias_ref, heads, first_head):
    scale = LANES ** (-0.5)
    lanes = [slice(h * LANES, (h + 1) * LANES) for h in range(heads)]
    probs = [
        probs_of(query[:, sl], key[:, sl], bias_ref[first_head + h], scale).astype(BF16)
        for h, sl in enumerate(lanes)
    ]
    return [dot(p, value[:, sl], FIRST).astype(BF16) for p, sl in zip(probs, lanes)]


def forward_kernel(tick, flags_ref, *refs):
    first = tick == 0
    if first:
        x_ref, qkv_ref, bias_ref, wo_ref, send_ref, keep_ref, x_half_ref, attended = refs
    else:
        (mine_ref, other_ref, entering_ref, gain_ref, w_ref, bias_ref, wo_ref,
         send_ref, keep_ref, x_half_ref, attended) = refs
    second = flag(flags_ref, SECOND_CORE)
    group = bias_ref.shape[0] // 2
    if first:
        x = x_ref[0]
    else:
        x = joined(second, mine_ref[...], other_ref[...])
        x = pick(flag(flags_ref, FIRST_SECTION), entering_ref[tick - 1], x)
        normed = rms_normed(x, gain_ref[...])
    x_half_ref[...] = own_half(second, x).astype(BF16)
    for part in range(2):
        at = slice(part * group * LANES, (part + 1) * group * LANES)
        if first:
            query, key, value = (qkv_ref[c, :, at] for c in range(3))
        else:
            query, key, value = (dot(normed, w_ref[c, :, at]).astype(BF16) for c in range(3))
        outs = attend(query, key, value, bias_ref, group, part * group)
        for h, out in enumerate(outs):
            at = (part * group + h) * LANES
            attended[:, at : at + LANES] = out
    split_halves(second, dot(attended[...], wo_ref[...]), send_ref, keep_ref)


def split_halves(second, total, send_ref, keep_ref):
    send_ref[...] = own_half(1.0 - second, total).astype(BF16)
    keep_ref[...] = own_half(second, total)


def stash_kernel(skipped, x_ref, gain_ref, w_ref, *refs):
    *outs, normed = refs
    ticks, tokens = len(outs), x_ref.shape[1]
    for t in range(ticks):
        normed[t * tokens : (t + 1) * tokens] = rms_normed(x_ref[skipped + t], gain_ref[...])
    width = min(512, w_ref.shape[2])

    def step(i, carry):
        at = rows_at(i, width)
        for c in range(3):
            out = dot(normed[...], w_ref[c, :, at]).astype(BF16)
            for t in range(ticks):
                outs[t][c, :, at] = out[t * tokens : (t + 1) * tokens]
        return carry

    lax.fori_loop(0, w_ref.shape[2] // width, step, 0)


def probs_kernel(qkv_ref, bias_ref, out_ref):
    heads = bias_ref.shape[0]
    group = heads // 2
    scale = LANES ** (-0.5)

    def step(g, carry):
        at = rows_at(g, group * LANES)
        query, key = (qkv_ref[c, :, at] for c in range(2))
        for h in range(group):
            sl = slice(h * LANES, (h + 1) * LANES)
            out_ref[g * group + h] = probs_of(
                query[:, sl], key[:, sl], bias_ref[g * group + h], scale
            )
        return carry

    lax.fori_loop(0, 2, step, 0)


def grad_attend(g, qkv_ref, probs_ref, wo_ref, acc_in_ref, stacked, acc_ref, parts, part):
    heads = probs_ref.shape[0] // parts
    scale = LANES ** (-0.5)
    at = slice(part * heads * LANES, (part + 1) * heads * LANES)
    grad_attn = dot(g, wo_ref[at], LAST).astype(BF16)
    lanes = [slice(h * LANES, (h + 1) * LANES) for h in range(part * heads, (part + 1) * heads)]
    attn = [grad_attn[:, h * LANES : (h + 1) * LANES] for h in range(heads)]
    grad_probs = [dot(qkv_ref[2, :, own], ga, LAST) for own, ga in zip(lanes, attn)]
    halved = []
    for h, of_probs in enumerate(grad_probs, part * heads):
        probs = probs_ref[h]
        total = jnp.sum(probs * of_probs, axis=0, keepdims=True)
        grad_scores = probs * (of_probs - total)
        halved.append(grad_scores.astype(BF16))
        if acc_in_ref is None:
            acc_ref[h] = grad_scores
        else:
            acc_ref[h] = acc_in_ref[h] + grad_scores
    for h, (own, ga, grad16) in enumerate(zip(lanes, attn, halved), part * heads):
        stacked[0, :, own] = (dot(grad16, qkv_ref[1, :, own], FIRST) * scale).astype(BF16)
        stacked[1, :, own] = (dot(grad16, qkv_ref[0, :, own]) * scale).astype(BF16)
        stacked[2, :, own] = dot(probs_ref[h].astype(BF16), ga).astype(BF16)


def backward_kernel(first, flags_ref, *refs):
    second = flag(flags_ref, SECOND_CORE)
    if first:
        full_ref, qkv_ref, probs_ref, wo_ref, stacked, acc_ref, g_half_ref = refs
        acc_in_ref = None
        g = full_ref[...]
    else:
        mine_ref, other_ref, qkv_ref, probs_ref, wo_ref, acc_in_ref, *refs = refs
        stacked, acc_ref, g_half_ref = refs
        g = joined(second, mine_ref[...], other_ref[...]).astype(BF16)
    g_half_ref[...] = own_half(second, g).astype(BF16)
    grad_attend(g, qkv_ref, probs_ref, wo_ref, acc_in_ref, stacked, acc_ref, 1, 0)


def input_gradient_kernel(flags_ref, stacked, w_ref, send_ref, keep_ref):
    total = dot(w_ref[0], stacked[0], LAST)
    total += dot(w_ref[1], stacked[1], LAST)
    total += dot(w_ref[2], stacked[2], LAST)
    split_halves(flag(flags_ref, SECOND_CORE), total.T, send_ref, keep_ref)


def pair_kernel(first_ref, second_ref, out_ref):
    out_ref[...] = (first_ref[...].astype(F32) + second_ref[...].astype(F32)).astype(BF16)


def up_term_kernel(flags_ref, keep_ref, received_ref, x_ref, out_ref):
    residual = flag(flags_ref, ADDS_RESIDUAL)
    total = keep_ref[...] + received_ref[...].astype(F32)
    out_ref[...] = (total + residual * x_ref[...].astype(F32)).astype(BF16)


def down_term_kernel(tick, flags_ref, stash_ref, gain_ref, keep_ref, received_ref, g_ref, out_ref):
    residual = flag(flags_ref, ADDS_RESIDUAL)
    x = own_half(flag(flags_ref, SECOND_CORE), stash_ref[tick])
    inverse = lax.rsqrt(jnp.mean(x * x, axis=-1, keepdims=True) + EPSILON)
    weighted = gain_ref[...] * (keep_ref[...] + received_ref[...].astype(F32))
    mean = jnp.mean(x * weighted, axis=-1, keepdims=True)
    cubed = inverse * inverse * inverse
    back = inverse * weighted - x * cubed * mean
    out_ref[...] = (residual * g_ref[...].astype(F32) + back).astype(BF16)


def choose_kernel(flags_ref, own_ref, first_ref, second_ref, out_ref):
    arrived = first_ref[...].astype(F32) + second_ref[...].astype(F32)
    own = flag(flags_ref, LAST_SECTION)
    out_ref[...] = pick(own, own_ref[...], arrived).astype(BF16)


def join_kernel(flags_ref, mine_ref, other_ref, out_ref, token_ref):
    second = flag(flags_ref, SECOND_CORE)
    out_ref[0] = joined(second, mine_ref[...], other_ref[...]).astype(BF16)
    token_ref[...] = jnp.zeros_like(token_ref)


def table_kernel(buckets_here, acc_ref, bucket_ref, out_ref, token_ref):
    heads, tokens, _ = acc_ref.shape
    rows = 8
    cells = heads * rows
    columns = buckets_here * rows
    total = jnp.zeros((cells, columns), F32)
    turned = bucket_ref[...].T
    for i in range(tokens // rows):
        at = slice(i * rows, (i + 1) * rows)
        ids = turned[at]
        hits = jnp.concatenate(
            [(ids == b).astype(F32) for b in range(buckets_here)], axis=0
        ).astype(BF16)
        part = acc_ref[:, at, :].reshape(cells, tokens)
        high = part.astype(BF16)
        low = (part - high.astype(F32)).astype(BF16)
        total += dot(high, hits, LAST) + dot(low, hits, LAST)
    row = lax.broadcasted_iota(jnp.int32, (cells, columns), 0)
    col = lax.broadcasted_iota(jnp.int32, (cells, columns), 1)
    total = jnp.where((row & (rows - 1)) == (col & (rows - 1)), total, 0.0)
    summed = jnp.sum(total.reshape(heads, rows, columns), axis=1)
    spread = lax.broadcasted_iota(jnp.int32, (columns, buckets_here), 0) >> 3
    bucket = lax.broadcasted_iota(jnp.int32, (columns, buckets_here), 1)
    fold = (spread == bucket).astype(F32)
    out_ref[...] = jnp.dot(
        summed, fold, preferred_element_type=F32, precision=lax.Precision.HIGHEST
    )
    token_ref[...] = jnp.zeros_like(token_ref)


def shape(dims, dtype=BF16):
    return jax.ShapeDtypeStruct(dims, dtype)


class Chain:
    def __init__(self):
        self.before = None

    def __call__(self, kernel, out_shape, args, scratch=(), limit=16):
        outs = out_shape if isinstance(out_shape, tuple) else (out_shape,)
        extra = () if self.before is None else (self.before,)
        count = len(args)

        def body(*refs):
            kernel(*refs[:count], *refs[count + len(extra) :])

        results = pl.pallas_call(
            body,
            out_shape=outs,
            in_specs=[WHOLE] * count + [UNREAD] * len(extra),
            out_specs=tuple(WHOLE for _ in outs),
            scratch_shapes=list(scratch),
            compiler_params=pltpu.CompilerParams(vmem_limit_bytes=limit * MIB),
            cost_estimate=pl.CostEstimate(flops=0, bytes_accessed=LANES, transcendentals=0),
        )(*args, *extra)
        self.before = results[-1]
        return results if isinstance(out_shape, tuple) else results[0]


def in_hbm(x):
    return pltpu.with_memory_space_constraint(x, pltpu.HBM)


def moved(block, step, bit):
    sections, heads = lax.axis_size("section"), lax.axis_size("head")
    route = [
        (s * heads + h, (s + step) % sections * heads + (h ^ bit))
        for s in range(sections)
        for h in range(heads)
    ]
    return lax.ppermute(block, ("section", "head"), route)


def swapped(block, bit):
    return lax.ppermute(block, "head", [(i, i ^ bit) for i in range(lax.axis_size("head"))])


def per_device(rising, falling, stash, queue, order, buckets, bias_table, gain, w_qkv, w_out):
    section_index = lax.axis_index("section")
    section_count = lax.axis_size("section")
    head_index = lax.axis_index("head")
    head_count = lax.axis_size("head")
    _, model_width, heads, _, head_dim = w_qkv.shape
    tokens = buckets.shape[0]
    half = tokens // 2
    inner = heads * head_dim
    facts = (
        head_index % 2 == 1,
        section_index == 0,
        section_index == section_count - 1,
        head_index < 2,
    )
    flags = jnp.broadcast_to(jnp.stack(facts).astype(F32)[:, None], (len(facts), LANES))
    table = bias_table[0].T
    back = w_out[0].reshape(inner, model_width)
    run = Chain()
    bits = [1 << b for b in range(1, head_count.bit_length() - 1)]
    cross = bits[-1]
    qkv_shape = shape((3, tokens, inner))
    scores_shape = shape((heads, tokens, tokens), F32)

    if heads % ROWS16 == 0:
        rows_first = jnp.transpose(w_qkv[0], (0, 2, 1, 3)).reshape(model_width, 3 * heads, head_dim)
        blocks = 1
        depth = model_width // blocks
        fixed = lambda rank: lambda c, b: (0,) * rank
        weights, qkv, kept_qkv, bias, wo, entering = pl.pallas_call(
            relayout_kernel,
            grid=(3, blocks),
            out_shape=(
                pltpu.VMEM((3, model_width, inner), BF16),
                qkv_shape,
                qkv_shape,
                scores_shape,
                pltpu.VMEM((inner, model_width), BF16),
                pltpu.VMEM((TICKS - 1, tokens, model_width), BF16),
            ),
            in_specs=[
                SCALARS,
                pl.BlockSpec((1, tokens, model_width), fixed(3)),
                pl.BlockSpec((1, 1, tokens, model_width), fixed(4)),
                pl.BlockSpec((1, model_width), fixed(2)),
                pl.BlockSpec(table.shape, fixed(2)),
                pl.BlockSpec((tokens, tokens), fixed(2)),
                pl.BlockSpec((depth, heads, head_dim), lambda c, b: (b, c, 0)),
                UNREAD,
                UNREAD,
                UNREAD,
            ],
            out_specs=(
                WHOLE,
                pl.BlockSpec((3, tokens, inner), fixed(3)),
                pl.BlockSpec((3, tokens, inner), fixed(3)),
                pl.BlockSpec((heads, tokens, tokens), fixed(3)),
                WHOLE,
                WHOLE,
            ),
            scratch_shapes=[pltpu.VMEM((2 * tokens, model_width), BF16), pltpu.SemaphoreType.DMA((TICKS,))],
            compiler_params=pltpu.CompilerParams(vmem_limit_bytes=24 * MIB),
            cost_estimate=pl.CostEstimate(
                flops=0, bytes_accessed=2 * w_qkv.size, transcendentals=0
            ),
        )(
            in_hbm(order), in_hbm(rising), in_hbm(stash), in_hbm(gain), in_hbm(table), in_hbm(buckets),
            in_hbm(rows_first), in_hbm(back), in_hbm(queue), flags,
        )
        run.before = qkv
    else:
        wo = back
        entering = jnp.stack(
            [lax.dynamic_index_in_dim(queue, order[t], 0, False) for t in range(TICKS - 1)]
        )
        weights = jnp.transpose(w_qkv[0], (2, 0, 1, 3)).reshape(3, model_width, inner)
        bias = run(bias_kernel, scores_shape, (table, buckets))
        qkv, kept_qkv = (
            run(
                functools.partial(stash_kernel, 0),
                qkv_shape,
                (rows, gain, weights),
                scratch=[pltpu.VMEM((tokens, model_width), BF16)],
            )
            for rows in (rising, stash[0, :1])
        )
    halves = (shape((half, model_width)), shape((half, model_width), F32))
    half_rows = shape((half, model_width))

    def but_last_bit(term):
        for bit in bits[:-1]:
            term = run(pair_kernel, half_rows, (term, swapped(term, bit)))
        return term

    def down_term(tick, keep, received, g_half):
        term = run(
            functools.partial(down_term_kernel, tick),
            half_rows,
            (flags, stash[0], gain, keep, received, g_half),
        )
        return but_last_bit(term)

    stashed = [kept_qkv]
    acc = ()
    for t in range(TICKS):
        final = t + 1 == TICKS
        scratch = [pltpu.VMEM((tokens, inner), BF16)]
        if t == 0:
            args = (flags, rising, qkv, bias, wo)
        else:
            x_other = swapped(x_mine, 1)
            fallen = down_term(t - 1, keep, received, g_half)
            arrivals = (lifted, moved(fallen, -1, 0), moved(fallen, -1, cross))
            args = (flags, x_mine, x_other, entering, gain, weights, bias, wo)
        up_send, up_keep, x_half = run(
            functools.partial(forward_kernel, t),
            halves + (half_rows,),
            args,
            scratch=scratch,
        )
        up_received = swapped(up_send, 1)
        if t > 0:
            stashed.append(
                run(
                    functools.partial(stash_kernel, t),
                    qkv_shape,
                    (stash[0], gain, weights),
                    scratch=[pltpu.VMEM((tokens, model_width), BF16)],
                )
            )
        probs = run(probs_kernel, scores_shape, (stashed[t], bias))
        if t == 0:
            g_parts = (falling[0],)
        else:
            g_mine = run(choose_kernel, half_rows, (flags,) + arrivals)
            g_parts = (g_mine, swapped(g_mine, 1))
        up = but_last_bit(
            run(up_term_kernel, half_rows, (flags, up_keep, up_received, x_half))
        )
        up_other = swapped(up, cross)

        stacked, acc_next, g_half = run(
            functools.partial(backward_kernel, t == 0),
            (shape((3, tokens, inner)), scores_shape, half_rows),
            (flags,) + g_parts + (stashed[t], probs, wo) + acc,
        )
        acc = (acc_next,)
        if not final:
            lifted = run(pair_kernel, half_rows, (up, up_other))
            x_mine = moved(lifted, 1, 0)
        send, keep = run(input_gradient_kernel, halves, (flags, stacked, weights))
        received = swapped(send, 1)
        if final:
            x_mine = run(pair_kernel, half_rows, (up, up_other))

    x_other = swapped(x_mine, 1)
    rows = shape((1, tokens, model_width))
    fallen = down_term(TICKS - 1, keep, received, g_half)
    fallen_other = swapped(fallen, cross)
    token = shape((8, LANES), F32)
    rising_out, _ = run(join_kernel, (rows, token), (flags, x_mine, x_other))
    table_grad, _ = run(
        functools.partial(table_kernel, bias_table.shape[1]),
        (shape((heads, bias_table.shape[1]), F32), token),
        acc + (buckets,),
    )
    lowered = run(pair_kernel, half_rows, (fallen, fallen_other))
    falling_out, _ = run(join_kernel, (rows, token), (flags, lowered, swapped(lowered, 1)))
    return (rising_out, falling_out, table_grad.T[None])


def solution(mesh):
    return jax.shard_map(
        per_device,
        mesh=mesh,
        in_specs=(
            P(("groups", "section"), None, None),
            P(("groups", "section"), None, None),
            P(("groups", "section"), None, None, None),
            P("groups", None, None),
            P("groups"),
            P(),
            P("section", None, "head"),
            P("section", None),
            P("section", None, "head", None, None),
            P("section", "head", None, None),
        ),
        out_specs=(
            P(("groups", "section"), None, None),
            P(("groups", "section"), None, None),
            P(("groups", "section"), None, "head"),
        ),
        check_vma=False,
    )
```
